32 devices in a mesh: group: 2 (over y), attn: 4 (over z), sect: 2 (over x), pair: 2 (over core).
Axes of the slice: x: 2, y: 2, z: 4, core: 2. Of those that a mesh axis runs over, the one named last changes fastest.
Arguments:
- queries: bfloat16 [512, 4096], P(('group', 'attn'), ('sect', 'pair')), parts along dimension 0, may hold values from -200 to 200
- kv_pool: bfloat16 [4, 8, 128, 256], P('sect', ('group', 'attn')), parts along dimension 1, may hold values from -8 to 8
- block_list: int32 [8, 2], P(('group', 'attn')), parts along dimension 0, may hold values from 0 to 3, as said below
- cache_len: int32 [8], P(('group', 'attn')), parts along dimension 0, may hold values from 128 to 256, as said below
- out_weight: bfloat16 [4096, 2048], P(('sect', 'pair'), 'attn'), may hold values from -0.09375 to 0.09375
- residual: bfloat16 [512, 2048], P(('group', 'attn', 'sect', 'pair')), parts along dimension 0, may hold values from -4 to 4
- norm_gain: float32 [2048], replicated, may hold values from 0.1 to 1.9
- router: bfloat16 [2048, 8], replicated, may hold values from -50 to 50
- expert_ids: int32 [512, 4], P(('group', 'attn', 'sect', 'pair')), parts along dimension 0, may hold values from 0 to 7, all different within a row; in each aligned block of 16 rows (0 to 15, 16 to 31, ...) at most 16 rows name the same one
- w_gate: bfloat16 [8, 2048, 768], P(('attn', 'pair'), None, 'sect'), may hold values from -0.125 to 0.125
- w_up: bfloat16 [8, 2048, 768], P(('attn', 'pair'), None, 'sect'), may hold values from -0.125 to 0.125
- w_down: bfloat16 [8, 768, 2048], P(('attn', 'pair'), None, 'sect'), may hold values from -0.21875 to 0.21875
Outputs:
- layer_out: bfloat16 [512, 2048], P(('group', 'attn', 'sect', 'pair')), parts along dimension 0
The draws below stay inside these ranges and needn't reach their ends.
There are 2 independent parts, one for each index of `group`. The reference program is written for one: setup_inputs(seed, part) draws one part's arguments, and reference() takes and returns one part's arrays. A program takes and returns all parts, laid end to end along the dimension named above; an argument that names none is the same for every part. Nothing has to cross between parts.
Inputs may be any that keep to these rules, and one draw needn't show every extreme that they name: `block_list`: A group's 2 blocks are distinct, and every block of the pool is listed by some group. `cache_len`: some group has 256 live positions and some group 128. `expert_ids`: each row names 4 different experts; among the rows of one device no expert is named by more than 16 rows, a bound that some block reaches.
All inputs are finite; a program needn't handle non-finite values.
Results may differ from the reference program's by a relative error of at most 0.013.
Values may be sent and summed in bfloat16 or wider, within the bound.
A program may use at most 64 MiB of HBM per device.

```python
import math
import jax
import jax.numpy as jnp
import numpy as np
from jax import lax

D = 2048
HEADS = 32
KV_HEADS = 4
HEAD_DIM = 128
FF = 768
BLOCK_KEYS = 128
ROW_DEV = 16
EXPERTS = 8
TOPK = 4
CAP = 16
NPOOL = 4
LIST = 2
GROUPS = 4
ROWS_GROUP = 64
TOKENS = 256


def block_lists(base_key):
    pool_order = jax.random.permutation(jax.random.fold_in(base_key, 101), NPOOL)
    base_index = (jnp.arange(GROUPS)[:, None] * LIST + jnp.arange(LIST)[None, :]) % NPOOL
    chosen = pool_order[base_index]
    shuffle_scores = jax.random.randint(jax.random.fold_in(base_key, 102), (GROUPS, LIST), 0, 1 << 20) * LIST + jnp.arange(LIST)[None, :]
    places = jnp.argsort(shuffle_scores, axis=1)
    return jnp.take_along_axis(chosen, places, axis=1).astype(jnp.int32)


def pool_values(base_key):
    pool_shape = (KV_HEADS, NPOOL, BLOCK_KEYS, 2 * HEAD_DIM)
    pool_data = jax.random.truncated_normal(jax.random.fold_in(base_key, 106), -6.0, 6.0, pool_shape, jnp.float32)
    return pool_data


def draw_block_list(key, part):
    return block_lists(key)


def draw_cache_len(key, part):
    lengths = jax.random.randint(jax.random.fold_in(key, 103), (GROUPS,), BLOCK_KEYS, LIST * BLOCK_KEYS + 1)
    longest = jax.random.randint(jax.random.fold_in(key, 104), (), 0, GROUPS)
    shortest = (longest + 1 + jax.random.randint(jax.random.fold_in(key, 105), (), 0, GROUPS - 1)) % GROUPS
    lengths = lengths.at[longest].set(LIST * BLOCK_KEYS).at[shortest].set(BLOCK_KEYS)
    return lengths.astype(jnp.int32)


def draw_kv_pool(key, part):
    return pool_values(key).astype(jnp.bfloat16)


def draw_queries(key, part):
    query_shape = (TOKENS, HEADS * HEAD_DIM)
    query_data = 2.0 * jax.random.truncated_normal(jax.random.fold_in(key, 107), -4.0, 4.0, query_shape, jnp.float32)
    return query_data.astype(jnp.bfloat16)


def draw_router(key, part):
    router_data = jax.random.truncated_normal(jax.random.fold_in(key, 110), -4.0, 4.0, (D, EXPERTS), jnp.float32) / D ** 0.5
    return router_data.astype(jnp.bfloat16)


def levels(own_key, shape, pieces, smallest, top_value):
    loudness = 1.0
    for position, parts in pieces:
        steps = jax.random.uniform(jax.random.fold_in(jax.random.fold_in(own_key, 6), position), (parts,), jnp.float32, smallest / len(pieces), top_value / len(pieces))
        loudness = loudness * jnp.repeat(jnp.exp(steps), shape[position] // parts).reshape((-1,) + (1,) * (len(shape) - 1 - position))
    return loudness


def assign_block(stream_key, own, number, rows, number_of, top, bound, lean):
    ranking = jax.random.permutation(stream_key, number_of)
    packed, ordinary = portions_of(number_of, rows * top, bound, lean, True), portions_of(number_of, rows * top, bound, lean, False)
    places = jnp.arange(number_of)

    def named(sizes, turn):
        used = int((sizes > 0).sum())
        fixed = max(1, used // 4)
        shifted = fixed + (places - fixed + turn * (used - fixed)) % max(1, number_of - fixed)
        return jnp.zeros((number_of,), jnp.int32).at[ranking[jnp.where(places < fixed, places, shifted)]].set(jnp.asarray(sizes, jnp.int32))

    sizes = jnp.where(number % 4 == 0, named(packed, number // 4), named(ordinary, number - number // 4 - 1))
    mixed = jax.random.permutation(jax.random.fold_in(own, 3), number_of)
    source_of, receiver = mixed[0:number_of // 2 * 2:2], mixed[1:number_of // 2 * 2:2]
    slack = jnp.minimum(sizes[source_of] - 1, bound - sizes[receiver]) // 2
    slack = jnp.where((source_of == ranking[0]) | (receiver == ranking[0]) | (sizes[receiver] == 0), 0, jnp.maximum(slack, 0))
    shifted = jax.random.randint(jax.random.fold_in(own, 4), (number_of // 2,), 0, 1 << 20) % (slack + 1)
    sizes = sizes.at[source_of].add(-shifted).at[receiver].add(shifted)
    labels = jnp.searchsorted(jnp.cumsum(sizes), jnp.arange(rows * top), side="right").astype(jnp.int32)
    table = labels.reshape(top, rows).T
    table = table[jax.random.permutation(jax.random.fold_in(own, 1), rows)]
    turn = jax.random.randint(jax.random.fold_in(own, 2), (rows, 1), 0, top)
    return jnp.take_along_axis(table, (jnp.arange(top)[None, :] + turn) % top, axis=1)


def portions_of(count, total, limit, skew, full):
    loads = [(1 << 20) // math.isqrt(standing ** skew) + 1 for standing in range(1, count + 1)]
    largest = limit if full else min(limit, max(-(-total // count), total * loads[0] // sum(loads)))
    least = 1 if total - largest >= count - 1 else 0
    counts, spare = [largest] + [least] * (count - 1), total - largest - least * (count - 1)
    while spare > 0:
        movable = [i for i in range(1, count) if counts[i] < largest] or [i for i in range(1, count) if counts[i] < limit]
        whole, remaining = sum([loads[i] for i in movable]), spare
        for i in movable:
            more = min(limit - counts[i], max(1, remaining * loads[i] // whole), spare)
            counts[i] = counts[i] + more
            spare = spare - more
    return np.array(counts)


def centred(rng, dims, width, bound, cuts=(), held_as=jnp.bfloat16):
    array = jax.random.normal(rng, dims, jnp.float32) * width
    if len(cuts) > 0:
        array = levels(rng, dims, cuts, -0.22, 0.18) * array
    return jnp.clip(array, min=-bound, max=bound).astype(held_as)


def setup_inputs(seed: int = 0, part: int = 0) -> dict:
    key_list = jax.random.split(jax.random.key(seed), 13)
    part_keys = jax.random.split(jax.random.fold_in(key_list[12], part), 13)
    queries = draw_queries(jax.random.fold_in(jax.random.fold_in(key_list[12], part), 71), part)
    kv_pool = draw_kv_pool(jax.random.fold_in(jax.random.fold_in(key_list[12], part), 71), part)
    block_list = draw_block_list(jax.random.fold_in(jax.random.fold_in(key_list[12], part), 71), part)
    cache_len = draw_cache_len(jax.random.fold_in(jax.random.fold_in(key_list[12], part), 71), part)
    out_weight = centred(key_list[4], (HEADS * HEAD_DIM, D), (HEADS * HEAD_DIM) ** -0.5, 0.09375, ((0, 4), (1, 4)))
    residual = centred(part_keys[5], (TOKENS, D), 0.3, 4.0, ((0, 16),))
    norm_gain = jnp.clip(1.0 + 0.18 * jax.random.normal(key_list[6], (D,), jnp.float32), 0.1, 1.9)
    router = draw_router(jax.random.fold_in(key_list[12], 71), part)
    expert_ids_keys = jax.random.split(jax.random.fold_in(part_keys[8], 1), TOKENS // ROW_DEV)
    expert_ids_turns = jax.random.permutation(jax.random.fold_in(part_keys[8], 3), TOKENS // ROW_DEV)
    expert_ids = jax.vmap(lambda own, number: assign_block(jax.random.fold_in(part_keys[8], 2), own, number, ROW_DEV, EXPERTS, TOPK, CAP, 2))(expert_ids_keys, expert_ids_turns).reshape((TOKENS, TOPK))
    w_gate = centred(key_list[9], (EXPERTS, D, FF), D ** -0.5, 0.125, ((0, 8), (2, 2)))
    w_up = centred(key_list[10], (EXPERTS, D, FF), D ** -0.5, 0.125, ((0, 8), (2, 2)))
    w_down = centred(key_list[11], (EXPERTS, FF, D), FF ** -0.5, 0.21875, ((0, 8), (2, 2)))
    return {"queries": queries, "kv_pool": kv_pool, "block_list": block_list, "cache_len": cache_len, "out_weight": out_weight, "residual": residual, "norm_gain": norm_gain, "router": router, "expert_ids": expert_ids, "w_gate": w_gate, "w_up": w_up, "w_down": w_down}


def attend_group(group, queries, kv_pool, block_list, cache_len):
    head_dim = HEAD_DIM
    per_kv = HEADS // KV_HEADS
    row_block = lax.dynamic_slice_in_dim(queries, (group * ROWS_GROUP).astype(jnp.int32), ROWS_GROUP, 0)
    row_block = row_block.astype(jnp.float32).reshape(ROWS_GROUP, KV_HEADS, per_kv, head_dim)
    listed = jnp.take(kv_pool, block_list[group], axis=1)
    listed = listed.reshape(KV_HEADS, LIST * BLOCK_KEYS, 2 * head_dim).astype(jnp.float32)
    key_rows = listed[:, :, :head_dim]
    values = listed[:, :, head_dim:]
    scores = jnp.einsum('rkgd,ktd->rkgt', row_block, key_rows) / math.sqrt(head_dim)
    live_mask = jnp.arange(LIST * BLOCK_KEYS) < cache_len[group]
    scores = jnp.where(live_mask, scores, -jnp.inf)
    row_top = lax.optimization_barrier(jnp.max(scores, axis=-1, keepdims=True))
    lifted = jnp.exp(scores - row_top)
    row_total = lax.optimization_barrier(jnp.sum(lifted, axis=-1))
    soft_weights = lax.optimization_barrier(lifted.astype(jnp.bfloat16)).astype(jnp.float32)
    mixed_heads = jnp.einsum('rkgt,ktd->rkgd', soft_weights, values) / row_total[..., None]
    return mixed_heads.reshape(ROWS_GROUP, HEADS * head_dim).astype(jnp.bfloat16)

def expert_step(operands):
    buffer, gate_part, up_part, down_part = operands
    gate_val = jnp.dot(buffer, gate_part, preferred_element_type=jnp.float32)
    up_val = jnp.dot(buffer, up_part, preferred_element_type=jnp.float32)
    hidden = (jax.nn.silu(gate_val) * up_val).astype(jnp.bfloat16)
    return jnp.dot(hidden, down_part, preferred_element_type=jnp.float32).astype(jnp.bfloat16)

def reference(queries, kv_pool, block_list, cache_len, out_weight, residual, norm_gain, router, expert_ids, w_gate, w_up, w_down):
    attended = lax.map(lambda group: attend_group(group, queries, kv_pool, block_list, cache_len), jnp.arange(GROUPS, dtype=jnp.int32))
    attended = attended.reshape(TOKENS, HEADS * HEAD_DIM)
    mixed_rows = (residual.astype(jnp.float32) + jnp.dot(attended, out_weight, preferred_element_type=jnp.float32)).astype(jnp.bfloat16)
    mixed_f32 = mixed_rows.astype(jnp.float32)
    normed = (mixed_f32 * lax.rsqrt(lax.optimization_barrier(jnp.mean(mixed_f32 * mixed_f32, axis=-1, keepdims=True)) + 1e-06) * norm_gain).astype(jnp.bfloat16)
    logits = jnp.dot(normed, router, preferred_element_type=jnp.float32)
    chosen_logits = jnp.take_along_axis(logits, expert_ids, axis=1)
    route_weights = jax.nn.softmax(chosen_logits, axis=-1)
    flat_ids = expert_ids.reshape(-1)
    onehot = (flat_ids[:, None] == jnp.arange(EXPERTS, dtype=jnp.int32)[None, :]).astype(jnp.int32)
    earlier = jnp.cumsum(onehot, axis=0) - onehot
    slot_index = lax.optimization_barrier(jnp.sum(earlier * onehot, axis=1)).astype(jnp.int32)
    source = jnp.repeat(jnp.arange(TOKENS, dtype=jnp.int32), TOPK)
    most_slots = TOKENS // ROW_DEV * CAP
    buffer = jnp.zeros((EXPERTS, most_slots, D), jnp.bfloat16).at[flat_ids, slot_index].set(normed[source])
    expert_outs = lax.map(expert_step, (buffer, w_gate, w_up, w_down))
    gathered = expert_outs[flat_ids, slot_index].reshape(TOKENS, TOPK, D).astype(jnp.float32)
    joined = lax.optimization_barrier(jnp.sum(route_weights[:, :, None] * gathered, axis=1))
    return (mixed_f32 + joined).astype(jnp.bfloat16)
```

```python
import functools
import math

import jax
import jax.numpy as jnp
from jax import lax
from jax.experimental import pallas as pl
from jax.experimental.pallas import tpu as pltpu
from jax.sharding import PartitionSpec as P

HEADS = 32
KV_HEADS = 4
HEAD_DIM = 128


def by_collectives(
    queries,
    kv_pool,
    block_list,
    cache_len,
    out_weight,
    residual,
    norm_gain,
    router,
    expert_ids,
    w_gate,
    w_up,
    w_down,
):
    head_dim = HEAD_DIM
    per_kv = HEADS // KV_HEADS
    group_rows, head_cols = queries.shape
    local_heads = head_cols // head_dim
    pool_all = lax.all_gather(kv_pool, "attn", axis=1, tiled=True)
    picked = jnp.take(pool_all, block_list[0], axis=1)
    kv_local = lax.axis_index("pair") * local_heads // per_kv
    chosen = lax.dynamic_index_in_dim(picked, kv_local, 0, keepdims=False)
    chosen = chosen.reshape(-1, 2 * head_dim)
    key_rows = chosen[:, :head_dim]
    values = chosen[:, head_dim:]
    query_heads = queries.reshape(group_rows, local_heads, head_dim)
    scores = jnp.einsum(
        "rhd,td->rht", query_heads, key_rows, preferred_element_type=jnp.float32
    ) / math.sqrt(head_dim)
    live_mask = jnp.arange(key_rows.shape[0]) < cache_len[0]
    scores = jnp.where(live_mask, scores, -jnp.inf)
    row_top = jnp.max(scores, axis=-1, keepdims=True)
    lifted = jnp.exp(scores - row_top)
    row_total = jnp.sum(lifted, axis=-1)
    soft_weights = lifted.astype(jnp.bfloat16)
    mixed_heads = (
        jnp.einsum("rht,td->rhd", soft_weights, values, preferred_element_type=jnp.float32)
        / row_total[..., None]
    )
    attended = mixed_heads.reshape(group_rows, head_cols).astype(jnp.bfloat16)
    partial_value = jnp.dot(
        attended,
        lax.all_gather(out_weight, "attn", axis=1, tiled=True),
        preferred_element_type=jnp.float32,
    )
    summed = lax.psum_scatter(partial_value, ("sect", "pair"), scatter_dimension=0, tiled=True)
    mixed_f32 = residual.astype(jnp.float32) + summed
    mixed_rows = mixed_f32.astype(jnp.bfloat16)
    mixed_f32 = mixed_rows.astype(jnp.float32)
    normed = (
        mixed_f32
        * lax.rsqrt(jnp.mean(mixed_f32 * mixed_f32, axis=-1, keepdims=True) + 1e-06)
        * norm_gain
    ).astype(jnp.bfloat16)
    logits = jnp.dot(normed, router, preferred_element_type=jnp.float32)
    chosen_logits = jnp.take_along_axis(logits, expert_ids, axis=1)
    route_weights = jax.nn.softmax(chosen_logits, axis=-1)
    row_count, top_count = expert_ids.shape
    expert_count = router.shape[1]
    model_width = residual.shape[1]
    capacity = max(2, row_count * top_count // expert_count * 2)
    flat_ids = expert_ids.reshape(-1)
    onehot = (flat_ids[:, None] == jnp.arange(expert_count, dtype=jnp.int32)[None, :]).astype(
        jnp.int32
    )
    earlier = jnp.cumsum(onehot, axis=0) - onehot
    slot_index = jnp.sum(earlier * onehot, axis=1)
    source = jnp.repeat(jnp.arange(row_count, dtype=jnp.int32), top_count)
    outgoing = (
        jnp.zeros((expert_count, capacity, model_width), jnp.bfloat16)
        .at[flat_ids, slot_index]
        .set(normed[source])
    )
    received = lax.all_to_all(outgoing, ("attn", "pair"), split_axis=0, concat_axis=0, tiled=True)
    sections = lax.axis_size("sect")
    every_section = lax.all_gather(received, "sect", axis=0, tiled=True)
    tokens_in = every_section.reshape(-1, model_width)
    gate_val = jnp.dot(tokens_in, w_gate[0], preferred_element_type=jnp.float32)
    up_val = jnp.dot(tokens_in, w_up[0], preferred_element_type=jnp.float32)
    part_hidden = (jax.nn.silu(gate_val) * up_val).astype(jnp.bfloat16)
    hidden = lax.all_gather(part_hidden, "sect", axis=1, tiled=True)
    out_slice = jnp.dot(hidden, w_down[0], preferred_element_type=jnp.float32).astype(jnp.bfloat16)
    out_slice = out_slice.reshape(sections, expert_count, capacity, model_width // sections)
    segmented = lax.all_to_all(out_slice, "sect", split_axis=0, concat_axis=3, tiled=True)
    returned = lax.all_to_all(
        segmented[0], ("attn", "pair"), split_axis=0, concat_axis=0, tiled=True
    )
    gathered = (
        returned[flat_ids, slot_index]
        .reshape(row_count, top_count, model_width)
        .astype(jnp.float32)
    )
    joined = jnp.sum(route_weights[:, :, None] * gathered, axis=1)
    return (mixed_f32 + joined).astype(jnp.bfloat16)


MESH = pl.DeviceIdType.MESH
LANES = 128
VMEM_BYTES = 48 * 1024 * 1024
BF16 = jnp.bfloat16
F32 = jnp.float32


def layer_kernel(
    sizes,
    q_ref,
    kv_ref,
    list_ref,
    len_ref,
    res_ref,
    gain_ref,
    router_ref,
    ids_ref,
    wo_hbm,
    wg_hbm,
    wu_hbm,
    wd_hbm,
    out_ref,
    wo,
    wg,
    wu,
    wd,
    kvbuf,
    att,
    part_f32,
    part,
    rs_in,
    sum_out,
    mix_in,
    mix_f32,
    router_pad,
    rows,
    hid,
    prod_f32,
    prod,
    pair_in,
    ret_out,
    ret_in,
    tot_f32,
    tot,
    fin_in,
    fin_f32,
    w_sem,
    kv_s,
    kv_r,
    att_s,
    att_r,
    rs_s,
    rs_r,
    mix_s,
    mix_r,
    nz_s,
    nz_r,
    nx_s,
    nx_r,
    nc_s,
    nc_r,
    hid_s,
    hid_r,
    pair_s,
    pair_r,
    ret_s,
    ret_r,
    fin_s,
    fin_r,
):
    n_attn, n_sect, n_pair = sizes
    quarters = n_sect * n_pair
    z = lax.axis_index("attn")
    x = lax.axis_index("sect")
    c = lax.axis_index("pair")
    quarter = x * n_pair + c
    own = res_ref.shape[0]
    width = res_ref.shape[1]
    group_rows, head_cols = q_ref.shape
    local_heads = head_cols // HEAD_DIM
    kv_local = c * local_heads // (HEADS // KV_HEADS)
    blocks = kv_ref.shape[1]
    sends = []

    def send(src, dst, s_sem, r_sem, **where):
        copy = pltpu.make_async_remote_copy(
            src_ref=src,
            dst_ref=dst,
            send_sem=s_sem,
            recv_sem=r_sem,
            device_id=where,
            device_id_type=MESH,
        )
        copy.start()
        sends.append(copy)
        return copy

    loads = [
        pltpu.make_async_copy(src, dst, w_sem.at[i])
        for i, (src, dst) in enumerate(
            ((wo_hbm, wo), (wg_hbm.at[0], wg), (wu_hbm.at[0], wu), (wd_hbm.at[0], wd))
        )
    ]
    for load in loads:
        load.start()

    barrier = pltpu.get_barrier_semaphore()
    for dz in range(n_attn):
        for dx in range(n_sect):
            for dc in range(n_pair):
                if dz + dx + dc:
                    pl.semaphore_signal(
                        barrier,
                        inc=1,
                        device_id={
                            "attn": lax.rem(z + dz, n_attn),
                            "sect": lax.rem(x + dx, n_sect),
                            "pair": lax.rem(c + dc, n_pair),
                        },
                        device_id_type=MESH,
                    )
    pl.semaphore_wait(barrier, n_attn * quarters - 1)

    def ahead(d):
        return lax.rem(z + d, n_attn)

    def behind(d):
        return lax.rem(z + (n_attn - d), n_attn)

    kv_slot = pl.ds(z * blocks, blocks)
    kv_copies = [
        send(
            kv_ref.at[kv_local],
            kvbuf.at[kv_slot],
            kv_s.at[d - 1],
            kv_r.at[d - 1],
            attn=ahead(d),
        )
        for d in range(1, n_attn)
    ]
    kvbuf[kv_slot] = kv_ref[kv_local]
    router_pad[...] = jnp.zeros_like(router_pad)
    router_pad[:, : router_ref.shape[1]] = router_ref[...]
    for copy in kv_copies:
        copy.wait_recv()

    listed = list_ref.shape[1]
    picked = [kvbuf[list_ref[0, j]] for j in range(listed)]
    cache = jnp.concatenate(picked, axis=0)
    keys = cache[:, :HEAD_DIM]
    values = cache[:, HEAD_DIM:]
    heads = jnp.concatenate(
        [q_ref[:, h * HEAD_DIM : (h + 1) * HEAD_DIM] for h in range(local_heads)], axis=0
    )
    scores = lax.dot_general(
        heads, keys, (((1,), (1,)), ((), ())), preferred_element_type=F32
    ) / math.sqrt(HEAD_DIM)
    place = lax.broadcasted_iota(jnp.int32, scores.shape, 1)
    scores = jnp.where(place < len_ref[0], scores, -jnp.inf)
    lifted = jnp.exp(scores - jnp.max(scores, axis=-1, keepdims=True))
    row_total = jnp.sum(lifted, axis=-1, keepdims=True)
    mixed = jnp.dot(lifted.astype(BF16), values, preferred_element_type=F32) / row_total
    for h in range(local_heads):
        att[0, :, h * HEAD_DIM : (h + 1) * HEAD_DIM] = mixed[
            h * group_rows : (h + 1) * group_rows
        ].astype(BF16)
    att_copies = [None] + [
        send(att.at[0], att.at[d], att_s.at[d - 1], att_r.at[d - 1], attn=ahead(d))
        for d in range(1, n_attn)
    ]

    def plane(step):
        return lax.div(step, n_pair), lax.rem(step, n_pair)

    loads[0].wait()
    rs_copies = []
    mix_copies = []

    def project(d):
        if d:
            att_copies[d].wait_recv()
        value = jnp.dot(att[d], wo[...], preferred_element_type=F32)
        value = value.reshape(part_f32.shape[1:])
        part_f32[d] = value
        part[d] = value.astype(BF16)
        copies = []
        for j in range(1, quarters):
            to = lax.rem(quarter + j, quarters)
            to_x, to_c = plane(to)
            copies.append(
                send(
                    part.at[d, to],
                    rs_in.at[d, j - 1],
                    rs_s.at[d, j - 1],
                    rs_r.at[d, j - 1],
                    sect=to_x,
                    pair=to_c,
                )
            )
        rs_copies.append(copies)

    def pass_on(d):
        for copy in rs_copies[d]:
            copy.wait_recv()
        total = part_f32[d, quarter]
        for j in range(quarters - 1):
            total = total + rs_in[d, j].astype(F32)
        if d == 0:
            mix_f32[z] = total
        else:
            sum_out[d - 1] = total.astype(BF16)
            mix_copies.append(
                send(
                    sum_out.at[d - 1],
                    mix_in.at[z],
                    mix_s.at[d - 1],
                    mix_r.at[d - 1],
                    attn=behind(d),
                )
            )

    for d in range(n_attn + 1):
        if d < n_attn:
            project(d)
        if d:
            pass_on(d - 1)
    for d in range(1, n_attn):
        mix_copies[d - 1].wait_recv()
        mix_f32[ahead(d)] = mix_in[ahead(d)].astype(F32)

    span = width // n_attn
    mixed_f32 = res_ref[...].astype(F32) + jnp.concatenate(
        [mix_f32[a] for a in range(n_attn)], axis=1
    )
    mixed_f32 = mixed_f32.astype(BF16).astype(F32)
    normed = (
        mixed_f32
        * lax.rsqrt(jnp.mean(mixed_f32 * mixed_f32, axis=-1, keepdims=True) + 1e-06)
        * gain_ref[...]
    ).astype(BF16)
    logits = jnp.dot(normed, router_pad[...], preferred_element_type=F32)
    lane = lax.broadcasted_iota(jnp.int32, logits.shape, 1)
    chosen = lane == ids_ref[:, 0:1]
    for k in range(1, ids_ref.shape[1]):
        chosen = jnp.logical_or(chosen, lane == ids_ref[:, k : k + 1])
    logits = jnp.where(chosen, logits, -jnp.inf)
    raised = jnp.exp(logits - jnp.max(logits, axis=-1, keepdims=True))
    route = raised / jnp.sum(raised, axis=-1, keepdims=True)
    rows[0, quarter, :, :width] = normed
    rows[0, quarter, :, width:] = route.astype(BF16)

    nz_copies = [None] + [
        send(
            rows.at[0, quarter],
            rows.at[d, quarter],
            nz_s.at[d - 1],
            nz_r.at[d - 1],
            attn=ahead(d),
        )
        for d in range(1, n_attn)
    ]
    nx_copies = [None] * n_attn
    nc_copies = [None] * n_attn
    for load in loads[1:]:
        load.wait()

    def to_cores(d, dx):
        from_q = lax.rem(x + (n_sect - dx), n_sect) * n_pair + c
        return [
            send(
                rows.at[d, from_q],
                rows.at[d, from_q],
                nc_s.at[d, dx, dc - 1],
                nc_r.at[d, dx, dc - 1],
                pair=lax.rem(c + dc, n_pair),
            )
            for dc in range(1, n_pair)
        ]

    def spread(d):
        if d:
            nz_copies[d].wait_recv()
        nx_copies[d] = [
            send(
                rows.at[d, quarter],
                rows.at[d, quarter],
                nx_s.at[d, dx - 1],
                nx_r.at[d, dx - 1],
                sect=lax.rem(x + dx, n_sect),
            )
            for dx in range(1, n_sect)
        ]
        nc_copies[d] = to_cores(d, 0)

    def spread_on(d):
        for dx in range(1, n_sect):
            nx_copies[d][dx - 1].wait_recv()
            nc_copies[d] += to_cores(d, dx)

    hid_copies = [None] * n_attn
    pair_copies = [None] * n_attn
    ret_copies = [None] * n_attn
    expert = z * n_pair + c

    def up(d):
        for copy in nc_copies[d]:
            copy.wait_recv()
        tokens = rows[d].reshape(quarters * own, rows.shape[-1])[:, :width]
        gate_val = jnp.dot(tokens, wg[...], preferred_element_type=F32)
        up_val = jnp.dot(tokens, wu[...], preferred_element_type=F32)
        hid[d, x] = (gate_val / (1.0 + jnp.exp(-gate_val)) * up_val).astype(BF16)
        hid_copies[d] = [
            send(
                hid.at[d, x],
                hid.at[d, x],
                hid_s.at[d, dx - 1],
                hid_r.at[d, dx - 1],
                sect=lax.rem(x + dx, n_sect),
            )
            for dx in range(1, n_sect)
        ]

    def down(d):
        for copy in hid_copies[d]:
            copy.wait_recv()
        hidden = jnp.concatenate([hid[d, i] for i in range(n_sect)], axis=1)
        value = jnp.dot(hidden, wd[...], preferred_element_type=F32)
        weights = rows[d].reshape(quarters * own, rows.shape[-1])[:, width:].astype(F32)
        lanes = lax.broadcasted_iota(jnp.int32, weights.shape, 1)
        weight = jnp.sum(jnp.where(lanes == expert, weights, 0.0), axis=-1, keepdims=True)
        value = (value * weight).reshape(n_sect, n_pair, own, value.shape[-1])
        for i in range(n_sect):
            for j in range(n_pair):
                prod_f32[d, j, i] = value[i, j]
                prod[d, j, i] = value[i, j].astype(BF16)
        pair_copies[d] = [
            send(
                prod.at[d, lax.rem(c + dc, n_pair)],
                pair_in.at[d, dc - 1],
                pair_s.at[d, dc - 1],
                pair_r.at[d, dc - 1],
                pair=lax.rem(c + dc, n_pair),
            )
            for dc in range(1, n_pair)
        ]

    def give_back(d):
        for copy in pair_copies[d]:
            copy.wait_recv()
        total = prod_f32[d, c]
        for j in range(n_pair - 1):
            total = total + pair_in[d, j].astype(F32)
        if d == 0:
            tot_f32[...] = total
        else:
            ret_out[d - 1] = total.astype(BF16)
            ret_copies[d] = send(
                ret_out.at[d - 1],
                ret_in.at[d - 1],
                ret_s.at[d - 1],
                ret_r.at[d - 1],
                attn=behind(d),
            )

    spread(0)
    for d in range(n_attn + 2):
        if d + 1 < n_attn:
            spread(d + 1)
        if d < n_attn:
            spread_on(d)
            up(d)
        if 1 <= d <= n_attn:
            down(d - 1)
        if d >= 2:
            give_back(d - 2)

    total = tot_f32[...]
    for d in range(1, n_attn):
        ret_copies[d].wait_recv()
        total = total + ret_in[d - 1].astype(F32)
    tot_f32[...] = total
    tot[...] = total.astype(BF16)
    fin_copies = [
        send(
            tot.at[lax.rem(x + dx, n_sect)],
            fin_in.at[x],
            fin_s.at[dx - 1],
            fin_r.at[dx - 1],
            sect=lax.rem(x + dx, n_sect),
        )
        for dx in range(1, n_sect)
    ]
    fin_f32[x] = tot_f32[x]
    for dx in range(1, n_sect):
        fin_copies[dx - 1].wait_recv()
        from_x = lax.rem(x + (n_sect - dx), n_sect)
        fin_f32[from_x] = fin_in[from_x].astype(F32)
    joined = jnp.concatenate([fin_f32[i] for i in range(n_sect)], axis=1)
    out_ref[...] = (mixed_f32 + joined).astype(BF16)
    for copy in sends:
        copy.wait_send()


def on_device(
    shape,
    queries,
    kv_pool,
    block_list,
    cache_len,
    out_weight,
    residual,
    norm_gain,
    router,
    expert_ids,
    w_gate,
    w_up,
    w_down,
):
    a, s, p = shape["attn"], shape["sect"], shape["pair"]
    q = s * p
    group_rows, head_cols = queries.shape
    own, width = residual.shape
    heads_rows, span = out_weight.shape
    hidden_part = w_gate.shape[2]
    hidden_all, out_cols = w_down.shape[1:]
    key_rows, key_cols = kv_pool.shape[2:]
    wide = width + LANES
    buffers = [
        ((heads_rows, span), BF16),
        ((width, hidden_part), BF16),
        ((width, hidden_part), BF16),
        ((hidden_all, out_cols), BF16),
        ((a * kv_pool.shape[1], key_rows, key_cols), BF16),
        ((a, group_rows, head_cols), BF16),
        ((a, q, own, span), F32),
        ((a, q, own, span), BF16),
        ((a, q - 1, own, span), BF16),
        ((a - 1, own, span), BF16),
        ((a, own, span), BF16),
        ((a, own, span), F32),
        ((width, LANES), BF16),
        ((a, q, own, wide), BF16),
        ((a, s, q * own, hidden_part), BF16),
        ((a, p, s, own, out_cols), F32),
        ((a, p, s, own, out_cols), BF16),
        ((a, p - 1, s, own, out_cols), BF16),
        ((a - 1, s, own, out_cols), BF16),
        ((a - 1, s, own, out_cols), BF16),
        ((s, own, out_cols), F32),
        ((s, own, out_cols), BF16),
        ((s, own, out_cols), BF16),
        ((s, own, out_cols), F32),
    ]
    held = sum(math.prod(dims) * jnp.dtype(kind).itemsize for dims, kind in buffers)
    fits = (
        2 * held <= VMEM_BYTES
        and span % LANES == 0
        and out_cols % LANES == 0
        and hidden_part % LANES == 0
        and w_gate.shape[0] == 1
        and router.shape[1] <= LANES
        and min(a, s, p) > 1
        and own % 16 == 0
        and group_rows == q * own
    )
    if not fits:
        return by_collectives(
            queries,
            kv_pool,
            block_list,
            cache_len,
            out_weight,
            residual,
            norm_gain,
            router,
            expert_ids,
            w_gate,
            w_up,
            w_down,
        )
    sems = [
        (4,),
        (a - 1,),
        (a - 1,),
        (a - 1,),
        (a - 1,),
        (a, q - 1),
        (a, q - 1),
        (a - 1,),
        (a - 1,),
        (a - 1,),
        (a - 1,),
        (a, s - 1),
        (a, s - 1),
        (a, s, p - 1),
        (a, s, p - 1),
        (a, s - 1),
        (a, s - 1),
        (a, p - 1),
        (a, p - 1),
        (a - 1,),
        (a - 1,),
        (s - 1,),
        (s - 1,),
    ]
    vmem = pl.BlockSpec(memory_space=pltpu.VMEM)
    smem = pl.BlockSpec(memory_space=pltpu.SMEM)
    hbm = pl.BlockSpec(memory_space=pl.ANY)
    return pl.pallas_call(
        functools.partial(layer_kernel, (a, s, p)),
        out_shape=jax.ShapeDtypeStruct(residual.shape, BF16),
        in_specs=[vmem, vmem, smem, smem, vmem, vmem, vmem, vmem, hbm, hbm, hbm, hbm],
        out_specs=vmem,
        scratch_shapes=[pltpu.VMEM(dims, kind) for dims, kind in buffers]
        + [pltpu.SemaphoreType.DMA(dims) for dims in sems],
        compiler_params=pltpu.CompilerParams(
            collective_id=0, has_side_effects=True, vmem_limit_bytes=VMEM_BYTES
        ),
    )(
        queries,
        kv_pool,
        block_list,
        cache_len,
        residual,
        norm_gain.reshape(1, -1),
        router,
        expert_ids,
        out_weight,
        w_gate,
        w_up,
        w_down,
    )


def solution(mesh):
    placed = (
        P(("group", "attn"), ("sect", "pair")),
        P("sect", ("group", "attn"), None, None),
        P(("group", "attn"), None),
        P(("group", "attn")),
        P(("sect", "pair"), "attn"),
        P(("group", "attn", "sect", "pair"), None),
        P(),
        P(),
        P(("group", "attn", "sect", "pair"), None),
        P(("attn", "pair"), None, "sect"),
        P(("attn", "pair"), None, "sect"),
        P(("attn", "pair"), None, "sect"),
    )
    return jax.shard_map(
        functools.partial(on_device, dict(mesh.shape)),
        mesh=mesh,
        in_specs=placed,
        out_specs=P(("group", "attn", "sect", "pair"), None),
        check_vma=False,
    )
```

```python
import functools
import math

import jax
import jax.numpy as jnp
from jax import lax
from jax.experimental import pallas as pl
from jax.experimental.pallas import tpu as pltpu
from jax.sharding import PartitionSpec as P

HEADS = 32
KV_HEADS = 4
HEAD_DIM = 128


def by_collectives(
    queries,
    kv_pool,
    block_list,
    cache_len,
    out_weight,
    residual,
    norm_gain,
    router,
    expert_ids,
    w_gate,
    w_up,
    w_down,
):
    head_dim = HEAD_DIM
    per_kv = HEADS // KV_HEADS
    group_rows, head_cols = queries.shape
    local_heads = head_cols // head_dim
    pool_all = lax.all_gather(kv_pool, "attn", axis=1, tiled=True)
    picked = jnp.take(pool_all, block_list[0], axis=1)
    kv_local = lax.axis_index("pair") * local_heads // per_kv
    chosen = lax.dynamic_index_in_dim(picked, kv_local, 0, keepdims=False)
    chosen = chosen.reshape(-1, 2 * head_dim)
    key_rows = chosen[:, :head_dim]
    values = chosen[:, head_dim:]
    query_heads = queries.reshape(group_rows, local_heads, head_dim)
    scores = jnp.einsum(
        "rhd,td->rht", query_heads, key_rows, preferred_element_type=jnp.float32
    ) / math.sqrt(head_dim)
    live_mask = jnp.arange(key_rows.shape[0]) < cache_len[0]
    scores = jnp.where(live_mask, scores, -jnp.inf)
    row_top = jnp.max(scores, axis=-1, keepdims=True)
    lifted = jnp.exp(scores - row_top)
    row_total = jnp.sum(lifted, axis=-1)
    soft_weights = lifted.astype(jnp.bfloat16)
    mixed_heads = (
        jnp.einsum("rht,td->rhd", soft_weights, values, preferred_element_type=jnp.float32)
        / row_total[..., None]
    )
    attended = mixed_heads.reshape(group_rows, head_cols).astype(jnp.bfloat16)
    partial_value = jnp.dot(
        attended,
        lax.all_gather(out_weight, "attn", axis=1, tiled=True),
        preferred_element_type=jnp.float32,
    )
    summed = lax.psum_scatter(partial_value, ("sect", "pair"), scatter_dimension=0, tiled=True)
    mixed_f32 = residual.astype(jnp.float32) + summed
    mixed_rows = mixed_f32.astype(jnp.bfloat16)
    mixed_f32 = mixed_rows.astype(jnp.float32)
    normed = (
        mixed_f32
        * lax.rsqrt(jnp.mean(mixed_f32 * mixed_f32, axis=-1, keepdims=True) + 1e-06)
        * norm_gain
    ).astype(jnp.bfloat16)
    logits = jnp.dot(normed, router, preferred_element_type=jnp.float32)
    chosen_logits = jnp.take_along_axis(logits, expert_ids, axis=1)
    route_weights = jax.nn.softmax(chosen_logits, axis=-1)
    row_count, top_count = expert_ids.shape
    expert_count = router.shape[1]
    model_width = residual.shape[1]
    capacity = max(2, row_count * top_count // expert_count * 2)
    flat_ids = expert_ids.reshape(-1)
    onehot = (flat_ids[:, None] == jnp.arange(expert_count, dtype=jnp.int32)[None, :]).astype(
        jnp.int32
    )
    earlier = jnp.cumsum(onehot, axis=0) - onehot
    slot_index = jnp.sum(earlier * onehot, axis=1)
    source = jnp.repeat(jnp.arange(row_count, dtype=jnp.int32), top_count)
    outgoing = (
        jnp.zeros((expert_count, capacity, model_width), jnp.bfloat16)
        .at[flat_ids, slot_index]
        .set(normed[source])
    )
    received = lax.all_to_all(outgoing, ("attn", "pair"), split_axis=0, concat_axis=0, tiled=True)
    sections = lax.axis_size("sect")
    every_section = lax.all_gather(received, "sect", axis=0, tiled=True)
    tokens_in = every_section.reshape(-1, model_width)
    gate_val = jnp.dot(tokens_in, w_gate[0], preferred_element_type=jnp.float32)
    up_val = jnp.dot(tokens_in, w_up[0], preferred_element_type=jnp.float32)
    part_hidden = (jax.nn.silu(gate_val) * up_val).astype(jnp.bfloat16)
    hidden = lax.all_gather(part_hidden, "sect", axis=1, tiled=True)
    out_slice = jnp.dot(hidden, w_down[0], preferred_element_type=jnp.float32).astype(jnp.bfloat16)
    out_slice = out_slice.reshape(sections, expert_count, capacity, model_width // sections)
    segmented = lax.all_to_all(out_slice, "sect", split_axis=0, concat_axis=3, tiled=True)
    returned = lax.all_to_all(
        segmented[0], ("attn", "pair"), split_axis=0, concat_axis=0, tiled=True
    )
    gathered = (
        returned[flat_ids, slot_index]
        .reshape(row_count, top_count, model_width)
        .astype(jnp.float32)
    )
    joined = jnp.sum(route_weights[:, :, None] * gathered, axis=1)
    return (mixed_f32 + joined).astype(jnp.bfloat16)


MESH = pl.DeviceIdType.MESH
LANES = 128
VMEM_BYTES = 60 * 1024 * 1024
BF16 = jnp.bfloat16
F32 = jnp.float32


def layer_kernel(
    sizes,
    q_hbm,
    kv_hbm,
    list_hbm,
    len_hbm,
    res_hbm,
    gain_hbm,
    router_hbm,
    ids_hbm,
    wo_hbm,
    wg_hbm,
    wu_hbm,
    wd_hbm,
    out_ref,
    q_ref,
    res_ref,
    gain_ref,
    router_ref,
    ids_ref,
    wo,
    wg,
    wu,
    wd,
    kvbuf,
    att,
    part_f32,
    part,
    rs_in,
    sum_out,
    mix_in,
    mix_f32,
    rows,
    hid,
    prod_f32,
    prod,
    pair_in,
    ret_out,
    ret_in,
    tot_f32,
    tot,
    fin_in,
    fin_f32,
    list_ref,
    len_ref,
    w_sem,
    kv_s,
    kv_r,
    att_s,
    att_r,
    rs_s,
    rs_r,
    mix_s,
    mix_r,
    nz_s,
    nz_r,
    nx_s,
    nx_r,
    nc_s,
    nc_r,
    hid_s,
    hid_r,
    pair_s,
    pair_r,
    ret_s,
    ret_r,
    fin_s,
    fin_r,
):
    n_attn, n_sect, n_pair = sizes
    quarters = n_sect * n_pair
    z = lax.axis_index("attn")
    x = lax.axis_index("sect")
    c = lax.axis_index("pair")
    quarter = x * n_pair + c
    own = res_ref.shape[0]
    width = res_ref.shape[1]
    group_rows, head_cols = q_ref.shape
    local_heads = head_cols // HEAD_DIM
    kv_local = c * local_heads // (HEADS // KV_HEADS)
    blocks = kv_hbm.shape[1]
    kv_slot = pl.ds(z * blocks, blocks)
    sends = []

    def send(src, dst, s_sem, r_sem, **where):
        copy = pltpu.make_async_remote_copy(
            src_ref=src,
            dst_ref=dst,
            send_sem=s_sem,
            recv_sem=r_sem,
            device_id=where,
            device_id_type=MESH,
        )
        copy.start()
        sends.append(copy)
        return copy

    loads = [
        pltpu.make_async_copy(src, dst, w_sem.at[i])
        for i, (src, dst) in enumerate(
            (
                (q_hbm, q_ref),
                (kv_hbm.at[kv_local], kvbuf.at[kv_slot]),
                (list_hbm, list_ref),
                (len_hbm, len_ref),
                (wo_hbm, wo),
                (res_hbm, res_ref),
                (gain_hbm, gain_ref),
                (router_hbm, router_ref),
                (ids_hbm, ids_ref),
                (wg_hbm.at[0], wg),
                (wu_hbm.at[0], wu),
                (wd_hbm.at[0], wd),
            )
        )
    ]
    for load in loads:
        load.start()

    barrier = pltpu.get_barrier_semaphore()
    for dz in range(n_attn):
        for dx in range(n_sect):
            for dc in range(n_pair):
                if dz + dx + dc:
                    pl.semaphore_signal(
                        barrier,
                        inc=1,
                        device_id={
                            "attn": lax.rem(z + dz, n_attn),
                            "sect": lax.rem(x + dx, n_sect),
                            "pair": lax.rem(c + dc, n_pair),
                        },
                        device_id_type=MESH,
                    )
    pl.semaphore_wait(barrier, n_attn * quarters - 1)

    def ahead(d):
        return lax.rem(z + d, n_attn)

    def behind(d):
        return lax.rem(z + (n_attn - d), n_attn)

    kv_copies = [
        send(
            kv_hbm.at[kv_local],
            kvbuf.at[kv_slot],
            kv_s.at[d - 1],
            kv_r.at[d - 1],
            attn=ahead(d),
        )
        for d in range(1, n_attn)
    ]
    for load in loads[:4]:
        load.wait()
    for copy in kv_copies:
        copy.wait_recv()

    listed = list_ref.shape[1]
    picked = [kvbuf[list_ref[0, j]] for j in range(listed)]
    cache = jnp.concatenate(picked, axis=0)
    keys = cache[:, :HEAD_DIM]
    values = cache[:, HEAD_DIM:]
    heads = jnp.concatenate(
        [q_ref[:, h * HEAD_DIM : (h + 1) * HEAD_DIM] for h in range(local_heads)], axis=0
    )
    scores = lax.dot_general(
        heads, keys, (((1,), (1,)), ((), ())), preferred_element_type=F32
    ) / math.sqrt(HEAD_DIM)
    place = lax.broadcasted_iota(jnp.int32, scores.shape, 1)
    scores = jnp.where(place < len_ref[0, 0], scores, -jnp.inf)
    lifted = jnp.exp(scores - jnp.max(scores, axis=-1, keepdims=True))
    row_total = jnp.sum(lifted, axis=-1, keepdims=True)
    mixed = jnp.dot(lifted.astype(BF16), values, preferred_element_type=F32) / row_total
    for h in range(local_heads):
        att[0, :, h * HEAD_DIM : (h + 1) * HEAD_DIM] = mixed[
            h * group_rows : (h + 1) * group_rows
        ].astype(BF16)
    att_copies = [None] + [
        send(att.at[0], att.at[d], att_s.at[d - 1], att_r.at[d - 1], attn=ahead(d))
        for d in range(1, n_attn)
    ]

    def plane(step):
        return lax.div(step, n_pair), lax.rem(step, n_pair)

    loads[4].wait()
    rs_copies = []
    mix_copies = []

    def project(d):
        if d:
            att_copies[d].wait_recv()
        value = jnp.dot(att[d], wo[...], preferred_element_type=F32)
        value = value.reshape(part_f32.shape[1:])
        part_f32[d] = value
        part[d] = value.astype(BF16)
        copies = []
        for j in range(1, quarters):
            to = lax.rem(quarter + j, quarters)
            to_x, to_c = plane(to)
            copies.append(
                send(
                    part.at[d, to],
                    rs_in.at[d, j - 1],
                    rs_s.at[d, j - 1],
                    rs_r.at[d, j - 1],
                    sect=to_x,
                    pair=to_c,
                )
            )
        rs_copies.append(copies)

    def pass_on(d):
        for copy in rs_copies[d]:
            copy.wait_recv()
        total = part_f32[d, quarter]
        for j in range(quarters - 1):
            total = total + rs_in[d, j].astype(F32)
        if d == 0:
            mix_f32[z] = total
        else:
            sum_out[d - 1] = total.astype(BF16)
            mix_copies.append(
                send(
                    sum_out.at[d - 1],
                    mix_in.at[z],
                    mix_s.at[d - 1],
                    mix_r.at[d - 1],
                    attn=behind(d),
                )
            )

    for d in range(n_attn + 1):
        if d < n_attn:
            project(d)
        if d:
            pass_on(d - 1)
    for d in range(1, n_attn):
        mix_copies[d - 1].wait_recv()
        mix_f32[ahead(d)] = mix_in[ahead(d)].astype(F32)

    for load in loads[5:9]:
        load.wait()

    span = width // n_attn
    mixed_f32 = res_ref[...].astype(F32) + jnp.concatenate(
        [mix_f32[a] for a in range(n_attn)], axis=1
    )
    mixed_f32 = mixed_f32.astype(BF16).astype(F32)
    normed = (
        mixed_f32
        * lax.rsqrt(jnp.mean(mixed_f32 * mixed_f32, axis=-1, keepdims=True) + 1e-06)
        * gain_ref[...]
    ).astype(BF16)
    logits = lax.dot_general(
        router_ref[...], normed, (((1,), (1,)), ((), ())), preferred_element_type=F32
    )
    lane = lax.broadcasted_iota(jnp.int32, logits.shape, 0)
    chosen = lane == ids_ref[0:1, :]
    for k in range(1, ids_ref.shape[0]):
        chosen = jnp.logical_or(chosen, lane == ids_ref[k : k + 1, :])
    logits = jnp.where(chosen, logits, -jnp.inf)
    raised = jnp.exp(logits - jnp.max(logits, axis=0, keepdims=True))
    route = raised / jnp.sum(raised, axis=0, keepdims=True)
    route = jnp.concatenate(
        [route, jnp.zeros((LANES - route.shape[0], own), F32)], axis=0
    )
    route = jnp.transpose(
        jnp.concatenate([route, jnp.zeros((LANES, LANES - own), F32)], axis=1)
    )[:own]
    rows[0, quarter, :, :width] = normed
    rows[0, quarter, :, width:] = route.astype(BF16)

    nz_copies = [None] + [
        send(
            rows.at[0, quarter],
            rows.at[d, quarter],
            nz_s.at[d - 1],
            nz_r.at[d - 1],
            attn=ahead(d),
        )
        for d in range(1, n_attn)
    ]
    nx_copies = [None] * n_attn
    nc_copies = [None] * n_attn
    for load in loads[9:]:
        load.wait()

    def to_cores(d, dx):
        from_q = lax.rem(x + (n_sect - dx), n_sect) * n_pair + c
        return [
            send(
                rows.at[d, from_q],
                rows.at[d, from_q],
                nc_s.at[d, dx, dc - 1],
                nc_r.at[d, dx, dc - 1],
                pair=lax.rem(c + dc, n_pair),
            )
            for dc in range(1, n_pair)
        ]

    def spread(d):
        if d:
            nz_copies[d].wait_recv()
        nx_copies[d] = [
            send(
                rows.at[d, quarter],
                rows.at[d, quarter],
                nx_s.at[d, dx - 1],
                nx_r.at[d, dx - 1],
                sect=lax.rem(x + dx, n_sect),
            )
            for dx in range(1, n_sect)
        ]
        nc_copies[d] = to_cores(d, 0)

    def spread_on(d):
        for dx in range(1, n_sect):
            nx_copies[d][dx - 1].wait_recv()
            nc_copies[d] += to_cores(d, dx)

    hid_copies = [None] * n_attn
    pair_copies = [None] * n_attn
    ret_copies = [None] * n_attn
    expert = z * n_pair + c

    def up(d):
        for copy in nc_copies[d]:
            copy.wait_recv()
        tokens = rows[d].reshape(quarters * own, rows.shape[-1])[:, :width]
        gate_val = jnp.dot(tokens, wg[...], preferred_element_type=F32)
        up_val = jnp.dot(tokens, wu[...], preferred_element_type=F32)
        hid[d, x] = (gate_val / (1.0 + jnp.exp(-gate_val)) * up_val).astype(BF16)
        hid_copies[d] = [
            send(
                hid.at[d, x],
                hid.at[d, x],
                hid_s.at[d, dx - 1],
                hid_r.at[d, dx - 1],
                sect=lax.rem(x + dx, n_sect),
            )
            for dx in range(1, n_sect)
        ]

    def down(d):
        for copy in hid_copies[d]:
            copy.wait_recv()
        hidden = jnp.concatenate([hid[d, i] for i in range(n_sect)], axis=1)
        value = jnp.dot(hidden, wd[...], preferred_element_type=F32)
        weights = rows[d].reshape(quarters * own, rows.shape[-1])[:, width:].astype(F32)
        lanes = lax.broadcasted_iota(jnp.int32, weights.shape, 1)
        weight = jnp.sum(jnp.where(lanes == expert, weights, 0.0), axis=-1, keepdims=True)
        value = (value * weight).reshape(n_sect, n_pair, own, value.shape[-1])
        for i in range(n_sect):
            for j in range(n_pair):
                prod_f32[d, j, i] = value[i, j]
                prod[d, j, i] = value[i, j].astype(BF16)
        pair_copies[d] = [
            send(
                prod.at[d, lax.rem(c + dc, n_pair)],
                pair_in.at[d, dc - 1],
                pair_s.at[d, dc - 1],
                pair_r.at[d, dc - 1],
                pair=lax.rem(c + dc, n_pair),
            )
            for dc in range(1, n_pair)
        ]

    def give_back(d):
        for copy in pair_copies[d]:
            copy.wait_recv()
        total = prod_f32[d, c]
        for j in range(n_pair - 1):
            total = total + pair_in[d, j].astype(F32)
        if d == 0:
            tot_f32[...] = total
        else:
            ret_out[d - 1] = total.astype(BF16)
            ret_copies[d] = send(
                ret_out.at[d - 1],
                ret_in.at[d - 1],
                ret_s.at[d - 1],
                ret_r.at[d - 1],
                attn=behind(d),
            )

    spread(0)
    spread_on(0)
    up(0)
    for d in range(1, n_attn):
        spread(d)
        if d == 1:
            down(0)
        else:
            spread_on(d - 1)
            up(d - 1)
        if d == 2:
            give_back(0)
    spread_on(n_attn - 1)
    up(n_attn - 1)
    for d in range(1, n_attn):
        down(d)
        if d > 1:
            give_back(d - 1)
    give_back(n_attn - 1)

    total = tot_f32[...]
    for d in range(1, n_attn):
        ret_copies[d].wait_recv()
        total = total + ret_in[d - 1].astype(F32)
    tot_f32[...] = total
    tot[...] = total.astype(BF16)
    fin_copies = [
        send(
            tot.at[lax.rem(x + dx, n_sect)],
            fin_in.at[x],
            fin_s.at[dx - 1],
            fin_r.at[dx - 1],
            sect=lax.rem(x + dx, n_sect),
        )
        for dx in range(1, n_sect)
    ]
    fin_f32[x] = tot_f32[x]
    for dx in range(1, n_sect):
        fin_copies[dx - 1].wait_recv()
        from_x = lax.rem(x + (n_sect - dx), n_sect)
        fin_f32[from_x] = fin_in[from_x].astype(F32)
    joined = jnp.concatenate([fin_f32[i] for i in range(n_sect)], axis=1)
    out_ref[...] = (mixed_f32 + joined).astype(BF16)
    for copy in sends:
        copy.wait_send()


def on_device(
    shape,
    queries,
    kv_pool,
    block_list,
    cache_len,
    out_weight,
    residual,
    norm_gain,
    router,
    expert_ids,
    w_gate,
    w_up,
    w_down,
):
    a, s, p = shape["attn"], shape["sect"], shape["pair"]
    q = s * p
    group_rows, head_cols = queries.shape
    own, width = residual.shape
    heads_rows, span = out_weight.shape
    hidden_part = w_gate.shape[2]
    hidden_all, out_cols = w_down.shape[1:]
    key_rows, key_cols = kv_pool.shape[2:]
    wide = width + LANES
    buffers = [
        ((group_rows, head_cols), BF16),
        ((own, width), BF16),
        ((1, width), F32),
        (router.shape[::-1], BF16),
        (expert_ids.shape[::-1], jnp.int32),
        ((heads_rows, span), BF16),
        ((width, hidden_part), BF16),
        ((width, hidden_part), BF16),
        ((hidden_all, out_cols), BF16),
        ((a * kv_pool.shape[1], key_rows, key_cols), BF16),
        ((a, group_rows, head_cols), BF16),
        ((a, q, own, span), F32),
        ((a, q, own, span), BF16),
        ((a, q - 1, own, span), BF16),
        ((a - 1, own, span), BF16),
        ((a, own, span), BF16),
        ((a, own, span), F32),
        ((a, q, own, wide), BF16),
        ((a, s, q * own, hidden_part), BF16),
        ((a, p, s, own, out_cols), F32),
        ((a, p, s, own, out_cols), BF16),
        ((a, p - 1, s, own, out_cols), BF16),
        ((a - 1, s, own, out_cols), BF16),
        ((a - 1, s, own, out_cols), BF16),
        ((s, own, out_cols), F32),
        ((s, own, out_cols), BF16),
        ((s, own, out_cols), BF16),
        ((s, own, out_cols), F32),
    ]
    held = sum(math.prod(dims) * jnp.dtype(kind).itemsize for dims, kind in buffers)
    fits = (
        2 * held <= VMEM_BYTES
        and span % LANES == 0
        and out_cols % LANES == 0
        and hidden_part % LANES == 0
        and w_gate.shape[0] == 1
        and router.shape[1] <= LANES
        and min(a, s, p) > 1
        and own % 16 == 0
        and own <= LANES
        and group_rows == q * own
    )
    if not fits:
        return by_collectives(
            queries,
            kv_pool,
            block_list,
            cache_len,
            out_weight,
            residual,
            norm_gain,
            router,
            expert_ids,
            w_gate,
            w_up,
            w_down,
        )
    sems = [
        (12,),
        (a - 1,),
        (a - 1,),
        (a - 1,),
        (a - 1,),
        (a, q - 1),
        (a, q - 1),
        (a - 1,),
        (a - 1,),
        (a - 1,),
        (a - 1,),
        (a, s - 1),
        (a, s - 1),
        (a, s, p - 1),
        (a, s, p - 1),
        (a, s - 1),
        (a, s - 1),
        (a, p - 1),
        (a, p - 1),
        (a - 1,),
        (a - 1,),
        (s - 1,),
        (s - 1,),
    ]
    vmem = pl.BlockSpec(memory_space=pltpu.VMEM)
    hbm = pl.BlockSpec(memory_space=pltpu.HBM)
    return pl.pallas_call(
        functools.partial(layer_kernel, (a, s, p)),
        out_shape=jax.ShapeDtypeStruct(residual.shape, BF16),
        in_specs=[hbm] * 12,
        out_specs=vmem,
        scratch_shapes=[pltpu.VMEM(dims, kind) for dims, kind in buffers]
        + [pltpu.SMEM(block_list.shape, jnp.int32), pltpu.SMEM((1, 1), jnp.int32)]
        + [pltpu.SemaphoreType.DMA(dims) for dims in sems],
        compiler_params=pltpu.CompilerParams(
            collective_id=0, has_side_effects=True, vmem_limit_bytes=VMEM_BYTES
        ),
    )(
        queries,
        kv_pool,
        block_list,
        cache_len.reshape(1, -1),
        residual,
        norm_gain.reshape(1, -1),
        router.T,
        expert_ids.T,
        out_weight,
        w_gate,
        w_up,
        w_down,
    )


def solution(mesh):
    placed = (
        P(("group", "attn"), ("sect", "pair")),
        P("sect", ("group", "attn"), None, None),
        P(("group", "attn"), None),
        P(("group", "attn")),
        P(("sect", "pair"), "attn"),
        P(("group", "attn", "sect", "pair"), None),
        P(),
        P(),
        P(("group", "attn", "sect", "pair"), None),
        P(("attn", "pair"), None, "sect"),
        P(("attn", "pair"), None, "sect"),
        P(("attn", "pair"), None, "sect"),
    )
    return jax.shard_map(
        functools.partial(on_device, dict(mesh.shape)),
        mesh=mesh,
        in_specs=placed,
        out_specs=P(("group", "attn", "sect", "pair"), None),
        check_vma=False,
    )
```

```python
import functools
import math

import jax
import jax.numpy as jnp
from jax import lax
from jax.experimental import pallas as pl
from jax.experimental.pallas import tpu as pltpu
from jax.sharding import PartitionSpec as P

HEADS = 32
KV_HEADS = 4
HEAD_DIM = 128


def by_collectives(
    queries,
    kv_pool,
    block_list,
    cache_len,
    out_weight,
    residual,
    norm_gain,
    router,
    expert_ids,
    w_gate,
    w_up,
    w_down,
):
    head_dim = HEAD_DIM
    per_kv = HEADS // KV_HEADS
    group_rows, head_cols = queries.shape
    local_heads = head_cols // head_dim
    pool_all = lax.all_gather(kv_pool, "attn", axis=1, tiled=True)
    picked = jnp.take(pool_all, block_list[0], axis=1)
    kv_local = lax.axis_index("pair") * local_heads // per_kv
    chosen = lax.dynamic_index_in_dim(picked, kv_local, 0, keepdims=False)
    chosen = chosen.reshape(-1, 2 * head_dim)
    key_rows = chosen[:, :head_dim]
    values = chosen[:, head_dim:]
    query_heads = queries.reshape(group_rows, local_heads, head_dim)
    scores = jnp.einsum(
        "rhd,td->rht", query_heads, key_rows, preferred_element_type=jnp.float32
    ) / math.sqrt(head_dim)
    live_mask = jnp.arange(key_rows.shape[0]) < cache_len[0]
    scores = jnp.where(live_mask, scores, -jnp.inf)
    row_top = jnp.max(scores, axis=-1, keepdims=True)
    lifted = jnp.exp(scores - row_top)
    row_total = jnp.sum(lifted, axis=-1)
    soft_weights = lifted.astype(jnp.bfloat16)
    mixed_heads = (
        jnp.einsum("rht,td->rhd", soft_weights, values, preferred_element_type=jnp.float32)
        / row_total[..., None]
    )
    attended = mixed_heads.reshape(group_rows, head_cols).astype(jnp.bfloat16)
    partial_value = jnp.dot(
        attended,
        lax.all_gather(out_weight, "attn", axis=1, tiled=True),
        preferred_element_type=jnp.float32,
    )
    summed = lax.psum_scatter(partial_value, ("sect", "pair"), scatter_dimension=0, tiled=True)
    mixed_f32 = residual.astype(jnp.float32) + summed
    mixed_rows = mixed_f32.astype(jnp.bfloat16)
    mixed_f32 = mixed_rows.astype(jnp.float32)
    normed = (
        mixed_f32
        * lax.rsqrt(jnp.mean(mixed_f32 * mixed_f32, axis=-1, keepdims=True) + 1e-06)
        * norm_gain
    ).astype(jnp.bfloat16)
    logits = jnp.dot(normed, router, preferred_element_type=jnp.float32)
    chosen_logits = jnp.take_along_axis(logits, expert_ids, axis=1)
    route_weights = jax.nn.softmax(chosen_logits, axis=-1)
    row_count, top_count = expert_ids.shape
    expert_count = router.shape[1]
    model_width = residual.shape[1]
    capacity = max(2, row_count * top_count // expert_count * 2)
    flat_ids = expert_ids.reshape(-1)
    onehot = (flat_ids[:, None] == jnp.arange(expert_count, dtype=jnp.int32)[None, :]).astype(
        jnp.int32
    )
    earlier = jnp.cumsum(onehot, axis=0) - onehot
    slot_index = jnp.sum(earlier * onehot, axis=1)
    source = jnp.repeat(jnp.arange(row_count, dtype=jnp.int32), top_count)
    outgoing = (
        jnp.zeros((expert_count, capacity, model_width), jnp.bfloat16)
        .at[flat_ids, slot_index]
        .set(normed[source])
    )
    received = lax.all_to_all(outgoing, ("attn", "pair"), split_axis=0, concat_axis=0, tiled=True)
    sections = lax.axis_size("sect")
    every_section = lax.all_gather(received, "sect", axis=0, tiled=True)
    tokens_in = every_section.reshape(-1, model_width)
    gate_val = jnp.dot(tokens_in, w_gate[0], preferred_element_type=jnp.float32)
    up_val = jnp.dot(tokens_in, w_up[0], preferred_element_type=jnp.float32)
    part_hidden = (jax.nn.silu(gate_val) * up_val).astype(jnp.bfloat16)
    hidden = lax.all_gather(part_hidden, "sect", axis=1, tiled=True)
    out_slice = jnp.dot(hidden, w_down[0], preferred_element_type=jnp.float32).astype(jnp.bfloat16)
    out_slice = out_slice.reshape(sections, expert_count, capacity, model_width // sections)
    segmented = lax.all_to_all(out_slice, "sect", split_axis=0, concat_axis=3, tiled=True)
    returned = lax.all_to_all(
        segmented[0], ("attn", "pair"), split_axis=0, concat_axis=0, tiled=True
    )
    gathered = (
        returned[flat_ids, slot_index]
        .reshape(row_count, top_count, model_width)
        .astype(jnp.float32)
    )
    joined = jnp.sum(route_weights[:, :, None] * gathered, axis=1)
    return (mixed_f32 + joined).astype(jnp.bfloat16)


MESH = pl.DeviceIdType.MESH
LANES = 128
VMEM_BYTES = 60 * 1024 * 1024
BF16 = jnp.bfloat16
F32 = jnp.float32


def layer_kernel(
    sizes,
    q_hbm,
    kv_hbm,
    list_hbm,
    len_hbm,
    res_hbm,
    gain_hbm,
    router_hbm,
    ids_hbm,
    wo_hbm,
    wg_hbm,
    wu_hbm,
    wd_hbm,
    out_ref,
    q_ref,
    res_ref,
    gain_ref,
    router_ref,
    ids_ref,
    wo,
    wg,
    wu,
    wd,
    kvbuf,
    att,
    part_f32,
    part,
    rs_in,
    sum_out,
    mix_in,
    mix_f32,
    rows,
    prod_f32,
    prod,
    pair_in,
    sect_f32,
    sect,
    sect_in,
    ret_out,
    ret_in,
    list_ref,
    len_ref,
    w_sem,
    kv_s,
    kv_r,
    att_s,
    att_r,
    rs_s,
    rs_r,
    mix_s,
    mix_r,
    nz_s,
    nz_r,
    nx_s,
    nx_r,
    nc_s,
    nc_r,
    wd_s,
    wd_r,
    pair_s,
    pair_r,
    sect_s,
    sect_r,
    ret_s,
    ret_r,
):
    n_attn, n_sect, n_pair = sizes
    quarters = n_sect * n_pair
    z = lax.axis_index("attn")
    x = lax.axis_index("sect")
    c = lax.axis_index("pair")
    quarter = x * n_pair + c
    own = res_ref.shape[0]
    width = res_ref.shape[1]
    group_rows, head_cols = q_ref.shape
    local_heads = head_cols // HEAD_DIM
    kv_local = c * local_heads // (HEADS // KV_HEADS)
    blocks = kv_hbm.shape[1]
    kv_slot = pl.ds(z * blocks, blocks)
    hidden_part = wg.shape[1]
    sends = []

    def send(src, dst, s_sem, r_sem, **where):
        copy = pltpu.make_async_remote_copy(
            src_ref=src,
            dst_ref=dst,
            send_sem=s_sem,
            recv_sem=r_sem,
            device_id=where,
            device_id_type=MESH,
        )
        copy.start()
        sends.append(copy)
        return copy

    loads = [
        pltpu.make_async_copy(src, dst, w_sem.at[i])
        for i, (src, dst) in enumerate(
            (
                (q_hbm, q_ref),
                (kv_hbm.at[kv_local], kvbuf.at[kv_slot]),
                (list_hbm, list_ref),
                (len_hbm, len_ref),
                (wo_hbm, wo),
                (res_hbm, res_ref),
                (gain_hbm, gain_ref),
                (router_hbm, router_ref),
                (ids_hbm, ids_ref),
                (wg_hbm.at[0], wg),
                (wu_hbm.at[0], wu),
                (wd_hbm.at[0, pl.ds(x * hidden_part, hidden_part)], wd.at[x]),
            )
        )
    ]
    for load in loads:
        load.start()

    barrier = pltpu.get_barrier_semaphore()
    for dz in range(n_attn):
        for dx in range(n_sect):
            for dc in range(n_pair):
                if dz + dx + dc:
                    pl.semaphore_signal(
                        barrier,
                        inc=1,
                        device_id={
                            "attn": lax.rem(z + dz, n_attn),
                            "sect": lax.rem(x + dx, n_sect),
                            "pair": lax.rem(c + dc, n_pair),
                        },
                        device_id_type=MESH,
                    )
    pl.semaphore_wait(barrier, n_attn * quarters - 1)

    def ahead(d):
        return lax.rem(z + d, n_attn)

    def behind(d):
        return lax.rem(z + (n_attn - d), n_attn)

    kv_copies = [
        send(
            kv_hbm.at[kv_local],
            kvbuf.at[kv_slot],
            kv_s.at[d - 1],
            kv_r.at[d - 1],
            attn=ahead(d),
        )
        for d in range(1, n_attn)
    ]
    wd_copies = []
    for dx in range(1, n_sect):
        to_x = lax.rem(x + dx, n_sect)
        wd_copies.append(
            send(
                wd_hbm.at[0, pl.ds(to_x * hidden_part, hidden_part)],
                wd.at[x],
                wd_s.at[dx - 1],
                wd_r.at[dx - 1],
                sect=to_x,
            )
        )
    for load in loads[:4]:
        load.wait()
    for copy in kv_copies:
        copy.wait_recv()

    listed = list_ref.shape[1]
    picked = [kvbuf[list_ref[0, j]] for j in range(listed)]
    cache = jnp.concatenate(picked, axis=0)
    keys = cache[:, :HEAD_DIM]
    values = cache[:, HEAD_DIM:]
    heads = jnp.concatenate(
        [q_ref[:, h * HEAD_DIM : (h + 1) * HEAD_DIM] for h in range(local_heads)], axis=0
    )
    scores = lax.dot_general(
        heads, keys, (((1,), (1,)), ((), ())), preferred_element_type=F32
    ) / math.sqrt(HEAD_DIM)
    place = lax.broadcasted_iota(jnp.int32, scores.shape, 1)
    scores = jnp.where(place < len_ref[0, 0], scores, -jnp.inf)
    lifted = jnp.exp(scores - jnp.max(scores, axis=-1, keepdims=True))
    row_total = jnp.sum(lifted, axis=-1, keepdims=True)
    mixed = jnp.dot(lifted.astype(BF16), values, preferred_element_type=F32) / row_total
    for h in range(local_heads):
        att[0, :, h * HEAD_DIM : (h + 1) * HEAD_DIM] = mixed[
            h * group_rows : (h + 1) * group_rows
        ].astype(BF16)
    att_copies = [None] + [
        send(att.at[0], att.at[d], att_s.at[d - 1], att_r.at[d - 1], attn=ahead(d))
        for d in range(1, n_attn)
    ]

    def plane(step):
        return lax.div(step, n_pair), lax.rem(step, n_pair)

    loads[4].wait()
    rs_copies = []
    mix_copies = []

    def project(d):
        if d:
            att_copies[d].wait_recv()
        value = jnp.dot(att[d], wo[...], preferred_element_type=F32)
        value = value.reshape(part_f32.shape[1:])
        part_f32[d] = value
        part[d] = value.astype(BF16)
        copies = []
        for j in range(1, quarters):
            to = lax.rem(quarter + j, quarters)
            to_x, to_c = plane(to)
            copies.append(
                send(
                    part.at[d, to],
                    rs_in.at[d, j - 1],
                    rs_s.at[d, j - 1],
                    rs_r.at[d, j - 1],
                    sect=to_x,
                    pair=to_c,
                )
            )
        rs_copies.append(copies)

    def pass_on(d):
        for copy in rs_copies[d]:
            copy.wait_recv()
        total = part_f32[d, quarter]
        for j in range(quarters - 1):
            total = total + rs_in[d, j].astype(F32)
        if d == 0:
            mix_f32[z] = total
        else:
            sum_out[d - 1] = total.astype(BF16)
            mix_copies.append(
                send(
                    sum_out.at[d - 1],
                    mix_in.at[z],
                    mix_s.at[d - 1],
                    mix_r.at[d - 1],
                    attn=behind(d),
                )
            )

    for d in range(n_attn + 1):
        if d < n_attn:
            project(d)
        if d:
            pass_on(d - 1)
    for d in range(1, n_attn):
        mix_copies[d - 1].wait_recv()
        mix_f32[ahead(d)] = mix_in[ahead(d)].astype(F32)

    for load in loads[5:9]:
        load.wait()

    span = width // n_attn
    mixed_f32 = res_ref[...].astype(F32) + jnp.concatenate(
        [mix_f32[a] for a in range(n_attn)], axis=1
    )
    mixed_f32 = mixed_f32.astype(BF16).astype(F32)
    normed = (
        mixed_f32
        * lax.rsqrt(jnp.mean(mixed_f32 * mixed_f32, axis=-1, keepdims=True) + 1e-06)
        * gain_ref[...]
    ).astype(BF16)
    logits = lax.dot_general(
        router_ref[...], normed, (((1,), (1,)), ((), ())), preferred_element_type=F32
    )
    lane = lax.broadcasted_iota(jnp.int32, logits.shape, 0)
    chosen = lane == ids_ref[0:1, :]
    for k in range(1, ids_ref.shape[0]):
        chosen = jnp.logical_or(chosen, lane == ids_ref[k : k + 1, :])
    logits = jnp.where(chosen, logits, -jnp.inf)
    raised = jnp.exp(logits - jnp.max(logits, axis=0, keepdims=True))
    route = raised / jnp.sum(raised, axis=0, keepdims=True)
    route = jnp.concatenate(
        [route, jnp.zeros((LANES - route.shape[0], own), F32)], axis=0
    )
    route = jnp.transpose(
        jnp.concatenate([route, jnp.zeros((LANES, LANES - own), F32)], axis=1)
    )[:own]
    rows[0, quarter, :, :width] = normed
    rows[0, quarter, :, width:] = route.astype(BF16)

    nz_copies = [None] + [
        send(
            rows.at[0, quarter],
            rows.at[d, quarter],
            nz_s.at[d - 1],
            nz_r.at[d - 1],
            attn=ahead(d),
        )
        for d in range(1, n_attn)
    ]
    nx_copies = [None] * n_attn
    nc_copies = [None] * n_attn
    for load in loads[9:]:
        load.wait()
    for copy in wd_copies:
        copy.wait_recv()

    def to_cores(d, dx):
        from_q = lax.rem(x + (n_sect - dx), n_sect) * n_pair + c
        return [
            send(
                rows.at[d, from_q],
                rows.at[d, from_q],
                nc_s.at[d, dx, dc - 1],
                nc_r.at[d, dx, dc - 1],
                pair=lax.rem(c + dc, n_pair),
            )
            for dc in range(1, n_pair)
        ]

    def spread(d):
        if d:
            nz_copies[d].wait_recv()
        nx_copies[d] = [
            send(
                rows.at[d, quarter],
                rows.at[d, quarter],
                nx_s.at[d, dx - 1],
                nx_r.at[d, dx - 1],
                sect=lax.rem(x + dx, n_sect),
            )
            for dx in range(1, n_sect)
        ]
        nc_copies[d] = to_cores(d, 0)

    def spread_on(d):
        for dx in range(1, n_sect):
            nx_copies[d][dx - 1].wait_recv()
            nc_copies[d] += to_cores(d, dx)

    sect_copies = [None] * n_attn
    pair_copies = [None] * n_attn
    ret_copies = [None] * n_attn
    expert = z * n_pair + c

    def up(d):
        for copy in nc_copies[d]:
            copy.wait_recv()
        tokens = rows[d].reshape(quarters * own, rows.shape[-1])[:, :width]
        gate_val = jnp.dot(tokens, wg[...], preferred_element_type=F32)
        up_val = jnp.dot(tokens, wu[...], preferred_element_type=F32)
        hidden = (gate_val / (1.0 + jnp.exp(-gate_val)) * up_val).astype(BF16)
        value = jnp.concatenate(
            [jnp.dot(hidden, wd[i], preferred_element_type=F32) for i in range(n_sect)],
            axis=1,
        )
        weights = rows[d].reshape(quarters * own, rows.shape[-1])[:, width:].astype(F32)
        lanes = lax.broadcasted_iota(jnp.int32, weights.shape, 1)
        weight = jnp.sum(jnp.where(lanes == expert, weights, 0.0), axis=-1, keepdims=True)
        value = (value * weight).reshape(n_sect, n_pair, own, value.shape[-1])
        for i in range(n_sect):
            for j in range(n_pair):
                prod_f32[d, j, i] = value[i, j]
                prod[d, j, i] = value[i, j].astype(BF16)
        pair_copies[d] = [
            send(
                prod.at[d, lax.rem(c + dc, n_pair)],
                pair_in.at[d, dc - 1],
                pair_s.at[d, dc - 1],
                pair_r.at[d, dc - 1],
                pair=lax.rem(c + dc, n_pair),
            )
            for dc in range(1, n_pair)
        ]

    def to_sect(d):
        for copy in pair_copies[d]:
            copy.wait_recv()
        total = prod_f32[d, c]
        for j in range(n_pair - 1):
            total = total + pair_in[d, j].astype(F32)
        sect_f32[d] = total
        sect[d] = total.astype(BF16)
        sect_copies[d] = [
            send(
                sect.at[d, lax.rem(x + dx, n_sect)],
                sect_in.at[d, dx - 1],
                sect_s.at[d, dx - 1],
                sect_r.at[d, dx - 1],
                sect=lax.rem(x + dx, n_sect),
            )
            for dx in range(1, n_sect)
        ]

    def give_back(d):
        for copy in sect_copies[d]:
            copy.wait_recv()
        total = sect_f32[d, x]
        for j in range(n_sect - 1):
            total = total + sect_in[d, j].astype(F32)
        if d == 0:
            return total
        ret_out[d - 1] = total.astype(BF16)
        ret_copies[d] = send(
            ret_out.at[d - 1],
            ret_in.at[d - 1],
            ret_s.at[d - 1],
            ret_r.at[d - 1],
            attn=behind(d),
        )

    spread(0)
    spread_on(0)
    up(0)
    turns = list(range(1, n_attn)) + [0]
    early = max(0, n_attn - 3)
    for d in range(1, n_attn):
        spread(d)
        if d >= 2:
            spread_on(d - 1)
            up(d - 1)
        if d >= 3:
            to_sect(d - 2)
    spread_on(n_attn - 1)
    up(n_attn - 1)
    for i in range(early - 1):
        give_back(turns[i])
    for i in range(early, n_attn):
        to_sect(turns[i])
        if i:
            give_back(turns[i - 1])
    joined = give_back(0)
    for d in range(1, n_attn):
        ret_copies[d].wait_recv()
        joined = joined + ret_in[d - 1].astype(F32)
    out_ref[...] = (mixed_f32 + joined).astype(BF16)
    for copy in sends:
        copy.wait_send()


def on_device(
    shape,
    queries,
    kv_pool,
    block_list,
    cache_len,
    out_weight,
    residual,
    norm_gain,
    router,
    expert_ids,
    w_gate,
    w_up,
    w_down,
):
    a, s, p = shape["attn"], shape["sect"], shape["pair"]
    q = s * p
    group_rows, head_cols = queries.shape
    own, width = residual.shape
    heads_rows, span = out_weight.shape
    hidden_part = w_gate.shape[2]
    out_cols = w_down.shape[2]
    key_rows, key_cols = kv_pool.shape[2:]
    wide = width + LANES
    buffers = [
        ((group_rows, head_cols), BF16),
        ((own, width), BF16),
        ((1, width), F32),
        (router.shape[::-1], BF16),
        (expert_ids.shape[::-1], jnp.int32),
        ((heads_rows, span), BF16),
        ((width, hidden_part), BF16),
        ((width, hidden_part), BF16),
        ((s, hidden_part, out_cols), BF16),
        ((a * kv_pool.shape[1], key_rows, key_cols), BF16),
        ((a, group_rows, head_cols), BF16),
        ((a, q, own, span), F32),
        ((a, q, own, span), BF16),
        ((a, q - 1, own, span), BF16),
        ((a - 1, own, span), BF16),
        ((a, own, span), BF16),
        ((a, own, span), F32),
        ((a, q, own, wide), BF16),
        ((a, p, s, own, width), F32),
        ((a, p, s, own, width), BF16),
        ((a, p - 1, s, own, width), BF16),
        ((a, s, own, width), F32),
        ((a, s, own, width), BF16),
        ((a, s - 1, own, width), BF16),
        ((a - 1, own, width), BF16),
        ((a - 1, own, width), BF16),
    ]
    held = sum(math.prod(dims) * jnp.dtype(kind).itemsize for dims, kind in buffers)
    fits = (
        2 * held <= VMEM_BYTES
        and span % LANES == 0
        and out_cols % LANES == 0
        and hidden_part % LANES == 0
        and w_gate.shape[0] == 1
        and router.shape[1] <= LANES
        and min(a, s, p) > 1
        and own % 16 == 0
        and own <= LANES
        and group_rows == q * own
        and hidden_part % 16 == 0
        and out_cols * s == width
    )
    if not fits:
        return by_collectives(
            queries,
            kv_pool,
            block_list,
            cache_len,
            out_weight,
            residual,
            norm_gain,
            router,
            expert_ids,
            w_gate,
            w_up,
            w_down,
        )
    sems = [
        (12,),
        (a - 1,),
        (a - 1,),
        (a - 1,),
        (a - 1,),
        (a, q - 1),
        (a, q - 1),
        (a - 1,),
        (a - 1,),
        (a - 1,),
        (a - 1,),
        (a, s - 1),
        (a, s - 1),
        (a, s, p - 1),
        (a, s, p - 1),
        (s - 1,),
        (s - 1,),
        (a, p - 1),
        (a, p - 1),
        (a, s - 1),
        (a, s - 1),
        (a - 1,),
        (a - 1,),
    ]
    vmem = pl.BlockSpec(memory_space=pltpu.VMEM)
    hbm = pl.BlockSpec(memory_space=pltpu.HBM)
    return pl.pallas_call(
        functools.partial(layer_kernel, (a, s, p)),
        out_shape=jax.ShapeDtypeStruct(residual.shape, BF16),
        in_specs=[hbm] * 12,
        out_specs=vmem,
        scratch_shapes=[pltpu.VMEM(dims, kind) for dims, kind in buffers]
        + [pltpu.SMEM(block_list.shape, jnp.int32), pltpu.SMEM((1, 1), jnp.int32)]
        + [pltpu.SemaphoreType.DMA(dims) for dims in sems],
        compiler_params=pltpu.CompilerParams(
            collective_id=0, has_side_effects=True, vmem_limit_bytes=VMEM_BYTES
        ),
    )(
        queries,
        kv_pool,
        block_list,
        cache_len.reshape(1, -1),
        residual,
        norm_gain.reshape(1, -1),
        router.T,
        expert_ids.T,
        out_weight,
        w_gate,
        w_up,
        w_down,
    )


def solution(mesh):
    placed = (
        P(("group", "attn"), ("sect", "pair")),
        P("sect", ("group", "attn"), None, None),
        P(("group", "attn"), None),
        P(("group", "attn")),
        P(("sect", "pair"), "attn"),
        P(("group", "attn", "sect", "pair"), None),
        P(),
        P(),
        P(("group", "attn", "sect", "pair"), None),
        P(("attn", "pair"), None, "sect"),
        P(("attn", "pair"), None, "sect"),
        P(("attn", "pair"), None, "sect"),
    )
    return jax.shard_map(
        functools.partial(on_device, dict(mesh.shape)),
        mesh=mesh,
        in_specs=placed,
        out_specs=P(("group", "attn", "sect", "pair"), None),
        check_vma=False,
    )
```

```python
import functools
import math

import jax
import jax.numpy as jnp
from jax import lax
from jax.experimental import pallas as pl
from jax.experimental.pallas import tpu as pltpu
from jax.sharding import PartitionSpec as P

HEADS = 32
KV_HEADS = 4
HEAD_DIM = 128


def by_collectives(
    queries,
    kv_pool,
    block_list,
    cache_len,
    out_weight,
    residual,
    norm_gain,
    router,
    expert_ids,
    w_gate,
    w_up,
    w_down,
):
    head_dim = HEAD_DIM
    per_kv = HEADS // KV_HEADS
    group_rows, head_cols = queries.shape
    local_heads = head_cols // head_dim
    pool_all = lax.all_gather(kv_pool, "attn", axis=1, tiled=True)
    picked = jnp.take(pool_all, block_list[0], axis=1)
    kv_local = lax.axis_index("pair") * local_heads // per_kv
    chosen = lax.dynamic_index_in_dim(picked, kv_local, 0, keepdims=False)
    chosen = chosen.reshape(-1, 2 * head_dim)
    key_rows = chosen[:, :head_dim]
    values = chosen[:, head_dim:]
    query_heads = queries.reshape(group_rows, local_heads, head_dim)
    scores = jnp.einsum(
        "rhd,td->rht", query_heads, key_rows, preferred_element_type=jnp.float32
    ) / math.sqrt(head_dim)
    live_mask = jnp.arange(key_rows.shape[0]) < cache_len[0]
    scores = jnp.where(live_mask, scores, -jnp.inf)
    row_top = jnp.max(scores, axis=-1, keepdims=True)
    lifted = jnp.exp(scores - row_top)
    row_total = jnp.sum(lifted, axis=-1)
    soft_weights = lifted.astype(jnp.bfloat16)
    mixed_heads = (
        jnp.einsum("rht,td->rhd", soft_weights, values, preferred_element_type=jnp.float32)
        / row_total[..., None]
    )
    attended = mixed_heads.reshape(group_rows, head_cols).astype(jnp.bfloat16)
    partial_value = jnp.dot(
        attended,
        lax.all_gather(out_weight, "attn", axis=1, tiled=True),
        preferred_element_type=jnp.float32,
    )
    summed = lax.psum_scatter(partial_value, ("sect", "pair"), scatter_dimension=0, tiled=True)
    mixed_f32 = residual.astype(jnp.float32) + summed
    mixed_rows = mixed_f32.astype(jnp.bfloat16)
    mixed_f32 = mixed_rows.astype(jnp.float32)
    normed = (
        mixed_f32
        * lax.rsqrt(jnp.mean(mixed_f32 * mixed_f32, axis=-1, keepdims=True) + 1e-06)
        * norm_gain
    ).astype(jnp.bfloat16)
    logits = jnp.dot(normed, router, preferred_element_type=jnp.float32)
    chosen_logits = jnp.take_along_axis(logits, expert_ids, axis=1)
    route_weights = jax.nn.softmax(chosen_logits, axis=-1)
    row_count, top_count = expert_ids.shape
    expert_count = router.shape[1]
    model_width = residual.shape[1]
    capacity = max(2, row_count * top_count // expert_count * 2)
    flat_ids = expert_ids.reshape(-1)
    onehot = (flat_ids[:, None] == jnp.arange(expert_count, dtype=jnp.int32)[None, :]).astype(
        jnp.int32
    )
    earlier = jnp.cumsum(onehot, axis=0) - onehot
    slot_index = jnp.sum(earlier * onehot, axis=1)
    source = jnp.repeat(jnp.arange(row_count, dtype=jnp.int32), top_count)
    outgoing = (
        jnp.zeros((expert_count, capacity, model_width), jnp.bfloat16)
        .at[flat_ids, slot_index]
        .set(normed[source])
    )
    received = lax.all_to_all(outgoing, ("attn", "pair"), split_axis=0, concat_axis=0, tiled=True)
    sections = lax.axis_size("sect")
    every_section = lax.all_gather(received, "sect", axis=0, tiled=True)
    tokens_in = every_section.reshape(-1, model_width)
    gate_val = jnp.dot(tokens_in, w_gate[0], preferred_element_type=jnp.float32)
    up_val = jnp.dot(tokens_in, w_up[0], preferred_element_type=jnp.float32)
    part_hidden = (jax.nn.silu(gate_val) * up_val).astype(jnp.bfloat16)
    hidden = lax.all_gather(part_hidden, "sect", axis=1, tiled=True)
    out_slice = jnp.dot(hidden, w_down[0], preferred_element_type=jnp.float32).astype(jnp.bfloat16)
    out_slice = out_slice.reshape(sections, expert_count, capacity, model_width // sections)
    segmented = lax.all_to_all(out_slice, "sect", split_axis=0, concat_axis=3, tiled=True)
    returned = lax.all_to_all(
        segmented[0], ("attn", "pair"), split_axis=0, concat_axis=0, tiled=True
    )
    gathered = (
        returned[flat_ids, slot_index]
        .reshape(row_count, top_count, model_width)
        .astype(jnp.float32)
    )
    joined = jnp.sum(route_weights[:, :, None] * gathered, axis=1)
    return (mixed_f32 + joined).astype(jnp.bfloat16)


MESH = pl.DeviceIdType.MESH
LANES = 128
VMEM_BYTES = 60 * 1024 * 1024
BF16 = jnp.bfloat16
F32 = jnp.float32


def layer_kernel(
    sizes,
    q_hbm,
    kv_hbm,
    list_hbm,
    len_hbm,
    res_hbm,
    gain_hbm,
    router_hbm,
    ids_hbm,
    wo_hbm,
    wg_hbm,
    wu_hbm,
    wd_hbm,
    out_ref,
    q_ref,
    res_ref,
    gain_ref,
    router_ref,
    ids_ref,
    wo,
    wg,
    wu,
    wd,
    kvbuf,
    att,
    part_f32,
    part,
    rs_in,
    sum_out,
    mix_in,
    mix_f32,
    rows,
    prod_f32,
    prod,
    pair_in,
    sect_f32,
    sect,
    sect_in,
    ret_out,
    ret_in,
    list_ref,
    len_ref,
    w_sem,
    kv_s,
    kv_r,
    att_s,
    att_r,
    rs_s,
    rs_r,
    mix_s,
    mix_r,
    nz_s,
    nz_r,
    nx_s,
    nx_r,
    nc_s,
    nc_r,
    wd_s,
    wd_r,
    pair_s,
    pair_r,
    sect_s,
    sect_r,
    ret_s,
    ret_r,
):
    n_attn, n_sect, n_pair = sizes
    quarters = n_sect * n_pair
    z = lax.axis_index("attn")
    x = lax.axis_index("sect")
    c = lax.axis_index("pair")
    quarter = x * n_pair + c
    own = res_ref.shape[0]
    width = res_ref.shape[1]
    group_rows, head_cols = q_ref.shape
    local_heads = head_cols // HEAD_DIM
    kv_local = c * local_heads // (HEADS // KV_HEADS)
    blocks = kv_hbm.shape[1]
    kv_slot = pl.ds(z * blocks, blocks)
    hidden_part = wg.shape[1]
    sends = []

    def send(src, dst, s_sem, r_sem, **where):
        copy = pltpu.make_async_remote_copy(
            src_ref=src,
            dst_ref=dst,
            send_sem=s_sem,
            recv_sem=r_sem,
            device_id=where,
            device_id_type=MESH,
        )
        copy.start()
        sends.append(copy)
        return copy

    loads = [
        pltpu.make_async_copy(src, dst, w_sem.at[i])
        for i, (src, dst) in enumerate(
            (
                (q_hbm, q_ref),
                (kv_hbm.at[kv_local], kvbuf.at[kv_slot]),
                (list_hbm, list_ref),
                (len_hbm, len_ref),
                (wo_hbm, wo),
                (res_hbm, res_ref),
                (gain_hbm, gain_ref),
                (router_hbm, router_ref),
                (ids_hbm, ids_ref),
                (wg_hbm.at[0], wg),
                (wu_hbm.at[0], wu),
                (wd_hbm.at[0, pl.ds(x * hidden_part, hidden_part)], wd.at[x]),
            )
        )
    ]
    for load in loads:
        load.start()

    barrier = pltpu.get_barrier_semaphore()
    for dz in range(n_attn):
        for dx in range(n_sect):
            for dc in range(n_pair):
                if dz + dx + dc:
                    pl.semaphore_signal(
                        barrier,
                        inc=1,
                        device_id={
                            "attn": lax.rem(z + dz, n_attn),
                            "sect": lax.rem(x + dx, n_sect),
                            "pair": lax.rem(c + dc, n_pair),
                        },
                        device_id_type=MESH,
                    )
    pl.semaphore_wait(barrier, n_attn * quarters - 1)

    def ahead(d):
        return lax.rem(z + d, n_attn)

    def behind(d):
        return lax.rem(z + (n_attn - d), n_attn)

    kv_copies = [
        send(
            kv_hbm.at[kv_local],
            kvbuf.at[kv_slot],
            kv_s.at[d - 1],
            kv_r.at[d - 1],
            attn=ahead(d),
        )
        for d in range(1, n_attn)
    ]
    wd_copies = []
    for dx in range(1, n_sect):
        to_x = lax.rem(x + dx, n_sect)
        wd_copies.append(
            send(
                wd_hbm.at[0, pl.ds(to_x * hidden_part, hidden_part)],
                wd.at[x],
                wd_s.at[dx - 1],
                wd_r.at[dx - 1],
                sect=to_x,
            )
        )
    for load in loads[:4]:
        load.wait()
    for copy in kv_copies:
        copy.wait_recv()

    listed = list_ref.shape[1]
    picked = [kvbuf[list_ref[0, j]] for j in range(listed)]
    cache = jnp.concatenate(picked, axis=0)
    keys = cache[:, :HEAD_DIM]
    values = cache[:, HEAD_DIM:]
    pieces, piece_cols = att.shape[1], att.shape[3]
    last = n_attn - 1

    def hop(src, piece, to, sem):
        return pltpu.make_async_remote_copy(
            src_ref=att.at[src, piece],
            dst_ref=att.at[src, piece],
            send_sem=sem,
            recv_sem=att_r.at[src, piece],
            device_id={"attn": to},
            device_id_type=MESH,
        )

    piece_heads = piece_cols // HEAD_DIM
    for piece in range(pieces):
        start = piece * piece_cols
        heads = jnp.concatenate(
            [
                q_ref[:, start + h * HEAD_DIM : start + (h + 1) * HEAD_DIM]
                for h in range(piece_heads)
            ],
            axis=0,
        )
        scores = lax.dot_general(
            heads, keys, (((1,), (1,)), ((), ())), preferred_element_type=F32
        ) / math.sqrt(HEAD_DIM)
        place = lax.broadcasted_iota(jnp.int32, scores.shape, 1)
        scores = jnp.where(place < len_ref[0, 0], scores, -jnp.inf)
        lifted = jnp.exp(scores - jnp.max(scores, axis=-1, keepdims=True))
        row_total = jnp.sum(lifted, axis=-1, keepdims=True)
        mixed = jnp.dot(lifted.astype(BF16), values, preferred_element_type=F32) / row_total
        for h in range(piece_heads):
            att[z, piece, :, h * HEAD_DIM : (h + 1) * HEAD_DIM] = mixed[
                h * group_rows : (h + 1) * group_rows
            ].astype(BF16)

        @pl.when(z < last)
        def _(piece=piece):
            hop(z, piece, z + 1, att_s.at[0, piece, 1]).start()

        @pl.when(z > 0)
        def _(piece=piece):
            hop(z, piece, z - 1, att_s.at[0, piece, 0]).start()

    longer = jnp.where(2 * z > last, -1, 1)
    shorter = jnp.minimum(z, last - z)

    def nearest(i):
        if i == 0:
            return z
        j = i - 1
        paired = j < 2 * shorter
        reach = jnp.where(paired, j // 2 + 1, j - shorter + 1)
        if j % 2:
            return z + jnp.where(paired, -longer, longer) * reach
        return z + longer * reach

    def goes_on(src):
        return jnp.where(src < z, last - z, z) > 0

    def onward(src):
        return jnp.where(src < z, z + 1, z - 1)

    def arrive(i):
        src = nearest(i)
        for piece in range(pieces):
            hop(src, piece, ahead(1), att_s.at[i, piece, 0]).wait_recv()

            @pl.when(goes_on(src))
            def _(piece=piece):
                hop(src, piece, onward(src), att_s.at[i, piece, 0]).start()

    def plane(step):
        return lax.div(step, n_pair), lax.rem(step, n_pair)

    loads[4].wait()
    rs_copies = []
    mix_copies = []

    def project(d):
        if d:
            arrive(d)
        src = nearest(d)
        value = jnp.dot(att[src, 0], wo[:piece_cols], preferred_element_type=F32)
        for piece in range(1, pieces):
            value += jnp.dot(
                att[src, piece],
                wo[piece * piece_cols : (piece + 1) * piece_cols],
                preferred_element_type=F32,
            )
        value = value.reshape(part_f32.shape[1:])
        part_f32[d] = value
        part[d] = value.astype(BF16)
        copies = []
        for j in range(1, quarters):
            to = lax.rem(quarter + j, quarters)
            to_x, to_c = plane(to)
            copies.append(
                send(
                    part.at[d, to],
                    rs_in.at[d, j - 1],
                    rs_s.at[d, j - 1],
                    rs_r.at[d, j - 1],
                    sect=to_x,
                    pair=to_c,
                )
            )
        rs_copies.append(copies)

    def pass_on(d):
        for copy in rs_copies[d]:
            copy.wait_recv()
        total = part_f32[d, quarter]
        for j in range(quarters - 1):
            total = total + rs_in[d, j].astype(F32)
        if d == 0:
            mix_f32[z] = total
        else:
            sum_out[d - 1] = total.astype(BF16)
            mix_copies.append(
                send(
                    sum_out.at[d - 1],
                    mix_in.at[z],
                    mix_s.at[d - 1],
                    mix_r.at[z],
                    attn=nearest(d),
                )
            )

    for d in range(n_attn + 1):
        if d < n_attn:
            project(d)
        if d:
            pass_on(d - 1)
    for d in range(1, n_attn):
        pltpu.make_async_remote_copy(
            src_ref=sum_out.at[d - 1],
            dst_ref=mix_in.at[ahead(d)],
            send_sem=mix_s.at[d - 1],
            recv_sem=mix_r.at[ahead(d)],
            device_id={"attn": ahead(d)},
            device_id_type=MESH,
        ).wait_recv()
        mix_f32[ahead(d)] = mix_in[ahead(d)].astype(F32)

    for load in loads[5:9]:
        load.wait()

    span = width // n_attn
    mixed_f32 = res_ref[...].astype(F32) + jnp.concatenate(
        [mix_f32[a] for a in range(n_attn)], axis=1
    )
    mixed_f32 = mixed_f32.astype(BF16).astype(F32)
    normed = (
        mixed_f32
        * lax.rsqrt(jnp.mean(mixed_f32 * mixed_f32, axis=-1, keepdims=True) + 1e-06)
        * gain_ref[...]
    ).astype(BF16)
    logits = lax.dot_general(
        router_ref[...], normed, (((1,), (1,)), ((), ())), preferred_element_type=F32
    )
    lane = lax.broadcasted_iota(jnp.int32, logits.shape, 0)
    chosen = lane == ids_ref[0:1, :]
    for k in range(1, ids_ref.shape[0]):
        chosen = jnp.logical_or(chosen, lane == ids_ref[k : k + 1, :])
    logits = jnp.where(chosen, logits, -jnp.inf)
    raised = jnp.exp(logits - jnp.max(logits, axis=0, keepdims=True))
    route = raised / jnp.sum(raised, axis=0, keepdims=True)
    route = jnp.concatenate(
        [route, jnp.zeros((LANES - route.shape[0], own), F32)], axis=0
    )
    route = jnp.transpose(
        jnp.concatenate([route, jnp.zeros((LANES, LANES - own), F32)], axis=1)
    )[:own]
    rows[0, quarter, :, :width] = normed
    rows[0, quarter, :, width:] = route.astype(BF16)

    nz_copies = [None] + [
        send(
            rows.at[0, quarter],
            rows.at[d, quarter],
            nz_s.at[d - 1],
            nz_r.at[d - 1],
            attn=ahead(d),
        )
        for d in range(1, n_attn)
    ]
    nx_copies = [None] * n_attn
    nc_copies = [None] * n_attn
    for load in loads[9:]:
        load.wait()
    for copy in wd_copies:
        copy.wait_recv()

    def to_cores(d, dx):
        from_q = lax.rem(x + (n_sect - dx), n_sect) * n_pair + c
        return [
            send(
                rows.at[d, from_q],
                rows.at[d, from_q],
                nc_s.at[d, dx, dc - 1],
                nc_r.at[d, dx, dc - 1],
                pair=lax.rem(c + dc, n_pair),
            )
            for dc in range(1, n_pair)
        ]

    def spread(d):
        if d:
            nz_copies[d].wait_recv()
        nx_copies[d] = [
            send(
                rows.at[d, quarter],
                rows.at[d, quarter],
                nx_s.at[d, dx - 1],
                nx_r.at[d, dx - 1],
                sect=lax.rem(x + dx, n_sect),
            )
            for dx in range(1, n_sect)
        ]
        nc_copies[d] = to_cores(d, 0)

    def spread_on(d):
        for dx in range(1, n_sect):
            nx_copies[d][dx - 1].wait_recv()
            nc_copies[d] += to_cores(d, dx)

    sect_copies = [None] * n_attn
    pair_copies = [None] * n_attn
    ret_copies = [None] * n_attn
    expert = z * n_pair + c

    def up(d):
        for copy in nc_copies[d]:
            copy.wait_recv()
        tokens = rows[d].reshape(quarters * own, rows.shape[-1])[:, :width]
        gate_val = jnp.dot(tokens, wg[...], preferred_element_type=F32)
        up_val = jnp.dot(tokens, wu[...], preferred_element_type=F32)
        hidden = (gate_val / (1.0 + jnp.exp(-gate_val)) * up_val).astype(BF16)
        value = jnp.concatenate(
            [jnp.dot(hidden, wd[i], preferred_element_type=F32) for i in range(n_sect)],
            axis=1,
        )
        weights = rows[d].reshape(quarters * own, rows.shape[-1])[:, width:].astype(F32)
        lanes = lax.broadcasted_iota(jnp.int32, weights.shape, 1)
        weight = jnp.sum(jnp.where(lanes == expert, weights, 0.0), axis=-1, keepdims=True)
        value = (value * weight).reshape(n_sect, n_pair, own, value.shape[-1])
        for i in range(n_sect):
            for j in range(n_pair):
                prod_f32[d, j, i] = value[i, j]
                prod[d, j, i] = value[i, j].astype(BF16)
        pair_copies[d] = [
            send(
                prod.at[d, lax.rem(c + dc, n_pair)],
                pair_in.at[d, dc - 1],
                pair_s.at[d, dc - 1],
                pair_r.at[d, dc - 1],
                pair=lax.rem(c + dc, n_pair),
            )
            for dc in range(1, n_pair)
        ]

    def to_sect(d):
        for copy in pair_copies[d]:
            copy.wait_recv()
        total = prod_f32[d, c]
        for j in range(n_pair - 1):
            total = total + pair_in[d, j].astype(F32)
        sect_f32[d] = total
        sect[d] = total.astype(BF16)
        sect_copies[d] = [
            send(
                sect.at[d, lax.rem(x + dx, n_sect)],
                sect_in.at[d, dx - 1],
                sect_s.at[d, dx - 1],
                sect_r.at[d, dx - 1],
                sect=lax.rem(x + dx, n_sect),
            )
            for dx in range(1, n_sect)
        ]

    def give_back(d):
        for copy in sect_copies[d]:
            copy.wait_recv()
        total = sect_f32[d, x]
        for j in range(n_sect - 1):
            total = total + sect_in[d, j].astype(F32)
        if d == 0:
            return total
        ret_out[d - 1] = total.astype(BF16)
        ret_copies[d] = send(
            ret_out.at[d - 1],
            ret_in.at[d - 1],
            ret_s.at[d - 1],
            ret_r.at[d - 1],
            attn=behind(d),
        )

    spread(0)
    spread_on(0)
    up(0)
    turns = list(range(1, n_attn)) + [0]
    early = max(0, n_attn - 3)
    for d in range(1, n_attn):
        spread(d)
        if d >= 2:
            spread_on(d - 1)
            up(d - 1)
        if d >= 3:
            to_sect(d - 2)
    spread_on(n_attn - 1)
    up(n_attn - 1)
    for i in range(early - 1):
        give_back(turns[i])
    for i in range(early, n_attn):
        to_sect(turns[i])
        if i:
            give_back(turns[i - 1])
    joined = give_back(0)
    for d in range(1, n_attn):
        ret_copies[d].wait_recv()
        joined = joined + ret_in[d - 1].astype(F32)
    out_ref[...] = (mixed_f32 + joined).astype(BF16)
    for copy in sends:
        copy.wait_send()
    for piece in range(pieces):

        @pl.when(z < last)
        def _(piece=piece):
            hop(z, piece, z + 1, att_s.at[0, piece, 1]).wait_send()

        @pl.when(z > 0)
        def _(piece=piece):
            hop(z, piece, z - 1, att_s.at[0, piece, 0]).wait_send()

        for i in range(1, n_attn):
            src = nearest(i)

            @pl.when(goes_on(src))
            def _(piece=piece, i=i, src=src):
                hop(src, piece, onward(src), att_s.at[i, piece, 0]).wait_send()


def on_device(
    shape,
    queries,
    kv_pool,
    block_list,
    cache_len,
    out_weight,
    residual,
    norm_gain,
    router,
    expert_ids,
    w_gate,
    w_up,
    w_down,
):
    a, s, p = shape["attn"], shape["sect"], shape["pair"]
    q = s * p
    group_rows, head_cols = queries.shape
    own, width = residual.shape
    heads_rows, span = out_weight.shape
    hidden_part = w_gate.shape[2]
    out_cols = w_down.shape[2]
    key_rows, key_cols = kv_pool.shape[2:]
    wide = width + LANES
    pieces = 2 - head_cols // HEAD_DIM % 2
    buffers = [
        ((group_rows, head_cols), BF16),
        ((own, width), BF16),
        ((1, width), F32),
        (router.shape[::-1], BF16),
        (expert_ids.shape[::-1], jnp.int32),
        ((heads_rows, span), BF16),
        ((width, hidden_part), BF16),
        ((width, hidden_part), BF16),
        ((s, hidden_part, out_cols), BF16),
        ((a * kv_pool.shape[1], key_rows, key_cols), BF16),
        ((a, pieces, group_rows, head_cols // pieces), BF16),
        ((a, q, own, span), F32),
        ((a, q, own, span), BF16),
        ((a, q - 1, own, span), BF16),
        ((a - 1, own, span), BF16),
        ((a, own, span), BF16),
        ((a, own, span), F32),
        ((a, q, own, wide), BF16),
        ((a, p, s, own, width), F32),
        ((a, p, s, own, width), BF16),
        ((a, p - 1, s, own, width), BF16),
        ((a, s, own, width), F32),
        ((a, s, own, width), BF16),
        ((a, s - 1, own, width), BF16),
        ((a - 1, own, width), BF16),
        ((a - 1, own, width), BF16),
    ]
    held = sum(math.prod(dims) * jnp.dtype(kind).itemsize for dims, kind in buffers)
    fits = (
        2 * held <= VMEM_BYTES
        and span % LANES == 0
        and out_cols % LANES == 0
        and hidden_part % LANES == 0
        and w_gate.shape[0] == 1
        and router.shape[1] <= LANES
        and min(a, s, p) > 1
        and own % 16 == 0
        and own <= LANES
        and group_rows == q * own
        and hidden_part % 16 == 0
        and out_cols * s == width
    )
    if not fits:
        return by_collectives(
            queries,
            kv_pool,
            block_list,
            cache_len,
            out_weight,
            residual,
            norm_gain,
            router,
            expert_ids,
            w_gate,
            w_up,
            w_down,
        )
    sems = [
        (12,),
        (a - 1,),
        (a - 1,),
        (a, pieces, 2),
        (a, pieces),
        (a, q - 1),
        (a, q - 1),
        (a - 1,),
        (a,),
        (a - 1,),
        (a - 1,),
        (a, s - 1),
        (a, s - 1),
        (a, s, p - 1),
        (a, s, p - 1),
        (s - 1,),
        (s - 1,),
        (a, p - 1),
        (a, p - 1),
        (a, s - 1),
        (a, s - 1),
        (a - 1,),
        (a - 1,),
    ]
    vmem = pl.BlockSpec(memory_space=pltpu.VMEM)
    hbm = pl.BlockSpec(memory_space=pltpu.HBM)
    return pl.pallas_call(
        functools.partial(layer_kernel, (a, s, p)),
        out_shape=jax.ShapeDtypeStruct(residual.shape, BF16),
        in_specs=[hbm] * 12,
        out_specs=vmem,
        scratch_shapes=[pltpu.VMEM(dims, kind) for dims, kind in buffers]
        + [pltpu.SMEM(block_list.shape, jnp.int32), pltpu.SMEM((1, 1), jnp.int32)]
        + [pltpu.SemaphoreType.DMA(dims) for dims in sems],
        compiler_params=pltpu.CompilerParams(
            collective_id=0, has_side_effects=True, vmem_limit_bytes=VMEM_BYTES
        ),
    )(
        queries,
        kv_pool,
        block_list,
        cache_len.reshape(1, -1),
        residual,
        norm_gain.reshape(1, -1),
        router.T,
        expert_ids.T,
        out_weight,
        w_gate,
        w_up,
        w_down,
    )


def solution(mesh):
    placed = (
        P(("group", "attn"), ("sect", "pair")),
        P("sect", ("group", "attn"), None, None),
        P(("group", "attn"), None),
        P(("group", "attn")),
        P(("sect", "pair"), "attn"),
        P(("group", "attn", "sect", "pair"), None),
        P(),
        P(),
        P(("group", "attn", "sect", "pair"), None),
        P(("attn", "pair"), None, "sect"),
        P(("attn", "pair"), None, "sect"),
        P(("attn", "pair"), None, "sect"),
    )
    return jax.shard_map(
        functools.partial(on_device, dict(mesh.shape)),
        mesh=mesh,
        in_specs=placed,
        out_specs=P(("group", "attn", "sect", "pair"), None),
        check_vma=False,
    )
```

```python
import functools
import math

import jax
import jax.numpy as jnp
from jax import lax
from jax.experimental import pallas as pl
from jax.experimental.pallas import tpu as pltpu
from jax.sharding import PartitionSpec as P

HEADS = 32
KV_HEADS = 4
HEAD_DIM = 128


def by_collectives(
    queries,
    kv_pool,
    block_list,
    cache_len,
    out_weight,
    residual,
    norm_gain,
    router,
    expert_ids,
    w_gate,
    w_up,
    w_down,
):
    head_dim = HEAD_DIM
    per_kv = HEADS // KV_HEADS
    group_rows, head_cols = queries.shape
    local_heads = head_cols // head_dim
    pool_all = lax.all_gather(kv_pool, "attn", axis=1, tiled=True)
    picked = jnp.take(pool_all, block_list[0], axis=1)
    kv_local = lax.axis_index("pair") * local_heads // per_kv
    chosen = lax.dynamic_index_in_dim(picked, kv_local, 0, keepdims=False)
    chosen = chosen.reshape(-1, 2 * head_dim)
    key_rows = chosen[:, :head_dim]
    values = chosen[:, head_dim:]
    query_heads = queries.reshape(group_rows, local_heads, head_dim)
    scores = jnp.einsum(
        "rhd,td->rht", query_heads, key_rows, preferred_element_type=jnp.float32
    ) / math.sqrt(head_dim)
    live_mask = jnp.arange(key_rows.shape[0]) < cache_len[0]
    scores = jnp.where(live_mask, scores, -jnp.inf)
    row_top = jnp.max(scores, axis=-1, keepdims=True)
    lifted = jnp.exp(scores - row_top)
    row_total = jnp.sum(lifted, axis=-1)
    soft_weights = lifted.astype(jnp.bfloat16)
    mixed_heads = (
        jnp.einsum("rht,td->rhd", soft_weights, values, preferred_element_type=jnp.float32)
        / row_total[..., None]
    )
    attended = mixed_heads.reshape(group_rows, head_cols).astype(jnp.bfloat16)
    partial_value = jnp.dot(
        attended,
        lax.all_gather(out_weight, "attn", axis=1, tiled=True),
        preferred_element_type=jnp.float32,
    )
    summed = lax.psum_scatter(partial_value, ("sect", "pair"), scatter_dimension=0, tiled=True)
    mixed_f32 = residual.astype(jnp.float32) + summed
    mixed_rows = mixed_f32.astype(jnp.bfloat16)
    mixed_f32 = mixed_rows.astype(jnp.float32)
    normed = (
        mixed_f32
        * lax.rsqrt(jnp.mean(mixed_f32 * mixed_f32, axis=-1, keepdims=True) + 1e-06)
        * norm_gain
    ).astype(jnp.bfloat16)
    logits = jnp.dot(normed, router, preferred_element_type=jnp.float32)
    chosen_logits = jnp.take_along_axis(logits, expert_ids, axis=1)
    route_weights = jax.nn.softmax(chosen_logits, axis=-1)
    row_count, top_count = expert_ids.shape
    expert_count = router.shape[1]
    model_width = residual.shape[1]
    capacity = max(2, row_count * top_count // expert_count * 2)
    flat_ids = expert_ids.reshape(-1)
    onehot = (flat_ids[:, None] == jnp.arange(expert_count, dtype=jnp.int32)[None, :]).astype(
        jnp.int32
    )
    earlier = jnp.cumsum(onehot, axis=0) - onehot
    slot_index = jnp.sum(earlier * onehot, axis=1)
    source = jnp.repeat(jnp.arange(row_count, dtype=jnp.int32), top_count)
    outgoing = (
        jnp.zeros((expert_count, capacity, model_width), jnp.bfloat16)
        .at[flat_ids, slot_index]
        .set(normed[source])
    )
    received = lax.all_to_all(outgoing, ("attn", "pair"), split_axis=0, concat_axis=0, tiled=True)
    sections = lax.axis_size("sect")
    every_section = lax.all_gather(received, "sect", axis=0, tiled=True)
    tokens_in = every_section.reshape(-1, model_width)
    gate_val = jnp.dot(tokens_in, w_gate[0], preferred_element_type=jnp.float32)
    up_val = jnp.dot(tokens_in, w_up[0], preferred_element_type=jnp.float32)
    part_hidden = (jax.nn.silu(gate_val) * up_val).astype(jnp.bfloat16)
    hidden = lax.all_gather(part_hidden, "sect", axis=1, tiled=True)
    out_slice = jnp.dot(hidden, w_down[0], preferred_element_type=jnp.float32).astype(jnp.bfloat16)
    out_slice = out_slice.reshape(sections, expert_count, capacity, model_width // sections)
    segmented = lax.all_to_all(out_slice, "sect", split_axis=0, concat_axis=3, tiled=True)
    returned = lax.all_to_all(
        segmented[0], ("attn", "pair"), split_axis=0, concat_axis=0, tiled=True
    )
    gathered = (
        returned[flat_ids, slot_index]
        .reshape(row_count, top_count, model_width)
        .astype(jnp.float32)
    )
    joined = jnp.sum(route_weights[:, :, None] * gathered, axis=1)
    return (mixed_f32 + joined).astype(jnp.bfloat16)


MESH = pl.DeviceIdType.MESH
LANES = 128
VMEM_BYTES = 60 * 1024 * 1024
BF16 = jnp.bfloat16
F32 = jnp.float32


def layer_kernel(
    sizes,
    q_hbm,
    kv_hbm,
    list_hbm,
    len_hbm,
    res_hbm,
    gain_hbm,
    router_hbm,
    ids_hbm,
    wo_hbm,
    wg_hbm,
    wu_hbm,
    wd_hbm,
    out_ref,
    q_all,
    res_ref,
    gain_ref,
    router_ref,
    ids_ref,
    wo,
    wg,
    wu,
    wd,
    kvbuf,
    bias,
    att,
    part_f32,
    part,
    rs_in,
    sum_out,
    mix_in,
    mix_f32,
    rows,
    prod_f32,
    prod,
    pair_in,
    sect_f32,
    sect,
    sect_in,
    ret_out,
    ret_in,
    list_ref,
    len_ref,
    w_sem,
    kv_s,
    kv_r,
    bias_s,
    bias_r,
    q_s,
    q_r,
    rs_s,
    rs_r,
    mix_s,
    mix_r,
    nz_s,
    nz_r,
    nx_s,
    nx_r,
    nc_s,
    nc_r,
    wd_s,
    wd_r,
    pair_s,
    pair_r,
    sect_s,
    sect_r,
    ret_s,
    ret_r,
):
    n_attn, n_sect, n_pair = sizes
    quarters = n_sect * n_pair
    z = lax.axis_index("attn")
    x = lax.axis_index("sect")
    c = lax.axis_index("pair")
    quarter = x * n_pair + c
    own = res_ref.shape[0]
    width = res_ref.shape[1]
    group_rows, head_cols = q_hbm.shape
    local_heads = head_cols // HEAD_DIM
    kv_local = c * local_heads // (HEADS // KV_HEADS)
    blocks = kv_hbm.shape[1]
    kv_slot = pl.ds(z * blocks, blocks)
    hidden_part = wg.shape[1]
    sends = []

    def send(src, dst, s_sem, r_sem, **where):
        copy = pltpu.make_async_remote_copy(
            src_ref=src,
            dst_ref=dst,
            send_sem=s_sem,
            recv_sem=r_sem,
            device_id=where,
            device_id_type=MESH,
        )
        copy.start()
        sends.append(copy)
        return copy

    loads = [
        pltpu.make_async_copy(src, dst, w_sem.at[i])
        for i, (src, dst) in enumerate(
            (
                (list_hbm, list_ref),
                (len_hbm, len_ref),
                (kv_hbm.at[kv_local], kvbuf.at[kv_slot]),
                (q_hbm, q_all.at[0]),
                (wo_hbm, wo),
                (res_hbm, res_ref),
                (gain_hbm, gain_ref),
                (router_hbm, router_ref),
                (ids_hbm, ids_ref),
                (wg_hbm.at[0], wg),
                (wu_hbm.at[0], wu),
                (wd_hbm.at[0, pl.ds(x * hidden_part, hidden_part)], wd.at[x]),
            )
        )
    ]
    for load in loads:
        load.start()

    barrier = pltpu.get_barrier_semaphore()
    for dz in range(n_attn):
        for dx in range(n_sect):
            for dc in range(n_pair):
                if dz + dx + dc:
                    pl.semaphore_signal(
                        barrier,
                        inc=1,
                        device_id={
                            "attn": lax.rem(z + dz, n_attn),
                            "sect": lax.rem(x + dx, n_sect),
                            "pair": lax.rem(c + dc, n_pair),
                        },
                        device_id_type=MESH,
                    )
    pl.semaphore_wait(barrier, n_attn * quarters - 1)

    def ahead(d):
        return lax.rem(z + d, n_attn)

    def behind(d):
        return lax.rem(z + (n_attn - d), n_attn)

    kv_copies = [
        send(
            kv_hbm.at[kv_local],
            kvbuf.at[kv_slot],
            kv_s.at[d - 1],
            kv_r.at[d - 1],
            attn=ahead(d),
        )
        for d in range(1, n_attn)
    ]
    q_copies = [None] + [
        send(q_hbm, q_all.at[d], q_s.at[d - 1], q_r.at[d - 1], attn=ahead(d))
        for d in range(1, n_attn)
    ]
    for load in loads[:2]:
        load.wait()
    block_keys = kvbuf.shape[1]
    place = lax.broadcasted_iota(jnp.int32, bias.shape[1:], 1)
    block, within = place // block_keys, place % block_keys
    live = within < 0
    for j in range(list_ref.shape[1]):
        used = jnp.logical_and(
            block == list_ref[0, j], within + j * block_keys < len_ref[0, 0]
        )
        live = jnp.logical_or(live, used)
    bias[0] = jnp.where(live, 0.0, -jnp.inf)
    bias_copies = [None] + [
        send(bias.at[0], bias.at[d], bias_s.at[d - 1], bias_r.at[d - 1], attn=ahead(d))
        for d in range(1, n_attn)
    ]

    wd_copies = []
    for dx in range(1, n_sect):
        to_x = lax.rem(x + dx, n_sect)
        wd_copies.append(
            send(
                wd_hbm.at[0, pl.ds(to_x * hidden_part, hidden_part)],
                wd.at[x],
                wd_s.at[dx - 1],
                wd_r.at[dx - 1],
                sect=to_x,
            )
        )
    for load in loads[2:4]:
        load.wait()
    for copy in kv_copies:
        copy.wait_recv()

    cache = kvbuf[...].reshape(-1, kvbuf.shape[2])
    keys = cache[:, :HEAD_DIM]
    values = cache[:, HEAD_DIM:]
    scale = 1.0 / math.sqrt(HEAD_DIM)
    stacked = local_heads // (2 - local_heads % 2)

    def attend(d):
        if d:
            q_copies[d].wait_recv()
            bias_copies[d].wait_recv()
        for first in range(0, local_heads, stacked):
            spans = [
                slice((first + h) * HEAD_DIM, (first + h + 1) * HEAD_DIM) for h in range(stacked)
            ]
            heads = jnp.concatenate([q_all[d, :, span] for span in spans], axis=0)
            scores = lax.dot_general(
                heads, keys, (((1,), (1,)), ((), ())), preferred_element_type=F32
            )
            scores = scores * scale + bias[d]
            lifted = jnp.exp(scores - jnp.max(scores, axis=-1, keepdims=True))
            row_total = jnp.sum(lifted, axis=-1, keepdims=True)
            mixed = jnp.dot(lifted.astype(BF16), values, preferred_element_type=F32)
            mixed = (mixed / row_total).astype(BF16)
            for h in range(stacked):
                att[d, :, spans[h]] = mixed[h * group_rows : (h + 1) * group_rows]

    def plane(step):
        return lax.div(step, n_pair), lax.rem(step, n_pair)

    loads[4].wait()
    rs_copies = []
    mix_copies = []

    def project(d):
        attend(d)
        value = jnp.dot(att[d], wo[...], preferred_element_type=F32)
        value = value.reshape(part_f32.shape[1:])
        part_f32[d] = value
        part[d] = value.astype(BF16)
        copies = []
        for j in range(1, quarters):
            to = lax.rem(quarter + j, quarters)
            to_x, to_c = plane(to)
            copies.append(
                send(
                    part.at[d, to],
                    rs_in.at[d, j - 1],
                    rs_s.at[d, j - 1],
                    rs_r.at[d, j - 1],
                    sect=to_x,
                    pair=to_c,
                )
            )
        rs_copies.append(copies)

    def pass_on(d):
        for copy in rs_copies[d]:
            copy.wait_recv()
        total = part_f32[d, quarter]
        for j in range(quarters - 1):
            total = total + rs_in[d, j].astype(F32)
        if d == 0:
            mix_f32[z] = total
        else:
            sum_out[d - 1] = total.astype(BF16)
            mix_copies.append(
                send(
                    sum_out.at[d - 1],
                    mix_in.at[z],
                    mix_s.at[d - 1],
                    mix_r.at[d - 1],
                    attn=behind(d),
                )
            )

    for d in range(n_attn + 1):
        if d < n_attn:
            project(d)
        if d:
            pass_on(d - 1)
    for d in range(1, n_attn):
        mix_copies[d - 1].wait_recv()
        mix_f32[ahead(d)] = mix_in[ahead(d)].astype(F32)

    for load in loads[5:9]:
        load.wait()

    span = width // n_attn
    mixed_f32 = res_ref[...].astype(F32) + jnp.concatenate(
        [mix_f32[a] for a in range(n_attn)], axis=1
    )
    mixed_f32 = mixed_f32.astype(BF16).astype(F32)
    normed = (
        mixed_f32
        * lax.rsqrt(jnp.mean(mixed_f32 * mixed_f32, axis=-1, keepdims=True) + 1e-06)
        * gain_ref[...]
    ).astype(BF16)
    logits = lax.dot_general(
        router_ref[...], normed, (((1,), (1,)), ((), ())), preferred_element_type=F32
    )
    lane = lax.broadcasted_iota(jnp.int32, logits.shape, 0)
    chosen = lane == ids_ref[0:1, :]
    for k in range(1, ids_ref.shape[0]):
        chosen = jnp.logical_or(chosen, lane == ids_ref[k : k + 1, :])
    logits = jnp.where(chosen, logits, -jnp.inf)
    raised = jnp.exp(logits - jnp.max(logits, axis=0, keepdims=True))
    route = raised / jnp.sum(raised, axis=0, keepdims=True)
    route = jnp.concatenate(
        [route, jnp.zeros((LANES - route.shape[0], own), F32)], axis=0
    )
    route = jnp.transpose(
        jnp.concatenate([route, jnp.zeros((LANES, LANES - own), F32)], axis=1)
    )[:own]
    rows[0, quarter, :, :width] = normed
    rows[0, quarter, :, width:] = route.astype(BF16)

    nz_copies = [None] + [
        send(
            rows.at[0, quarter],
            rows.at[d, quarter],
            nz_s.at[d - 1],
            nz_r.at[d - 1],
            attn=ahead(d),
        )
        for d in range(1, n_attn)
    ]
    nx_copies = [None] * n_attn
    nc_copies = [None] * n_attn
    for load in loads[9:]:
        load.wait()
    for copy in wd_copies:
        copy.wait_recv()

    def to_cores(d, dx):
        from_q = lax.rem(x + (n_sect - dx), n_sect) * n_pair + c
        return [
            send(
                rows.at[d, from_q],
                rows.at[d, from_q],
                nc_s.at[d, dx, dc - 1],
                nc_r.at[d, dx, dc - 1],
                pair=lax.rem(c + dc, n_pair),
            )
            for dc in range(1, n_pair)
        ]

    def spread(d):
        if d:
            nz_copies[d].wait_recv()
        nx_copies[d] = [
            send(
                rows.at[d, quarter],
                rows.at[d, quarter],
                nx_s.at[d, dx - 1],
                nx_r.at[d, dx - 1],
                sect=lax.rem(x + dx, n_sect),
            )
            for dx in range(1, n_sect)
        ]
        nc_copies[d] = to_cores(d, 0)

    def spread_on(d):
        for dx in range(1, n_sect):
            nx_copies[d][dx - 1].wait_recv()
            nc_copies[d] += to_cores(d, dx)

    sect_copies = [None] * n_attn
    pair_copies = [None] * n_attn
    ret_copies = [None] * n_attn
    expert = z * n_pair + c

    def up(d):
        for copy in nc_copies[d]:
            copy.wait_recv()
        tokens = rows[d].reshape(quarters * own, rows.shape[-1])[:, :width]
        gate_val = jnp.dot(tokens, wg[...], preferred_element_type=F32)
        up_val = jnp.dot(tokens, wu[...], preferred_element_type=F32)
        hidden = (gate_val / (1.0 + jnp.exp(-gate_val)) * up_val).astype(BF16)
        value = jnp.concatenate(
            [jnp.dot(hidden, wd[i], preferred_element_type=F32) for i in range(n_sect)],
            axis=1,
        )
        weights = rows[d].reshape(quarters * own, rows.shape[-1])[:, width:].astype(F32)
        lanes = lax.broadcasted_iota(jnp.int32, weights.shape, 1)
        weight = jnp.sum(jnp.where(lanes == expert, weights, 0.0), axis=-1, keepdims=True)
        value = (value * weight).reshape(n_sect, n_pair, own, value.shape[-1])
        for i in range(n_sect):
            for j in range(n_pair):
                prod_f32[d, j, i] = value[i, j]
                prod[d, j, i] = value[i, j].astype(BF16)
        pair_copies[d] = [
            send(
                prod.at[d, lax.rem(c + dc, n_pair)],
                pair_in.at[d, dc - 1],
                pair_s.at[d, dc - 1],
                pair_r.at[d, dc - 1],
                pair=lax.rem(c + dc, n_pair),
            )
            for dc in range(1, n_pair)
        ]

    def to_sect(d):
        for copy in pair_copies[d]:
            copy.wait_recv()
        total = prod_f32[d, c]
        for j in range(n_pair - 1):
            total = total + pair_in[d, j].astype(F32)
        sect_f32[d] = total
        sect[d] = total.astype(BF16)
        sect_copies[d] = [
            send(
                sect.at[d, lax.rem(x + dx, n_sect)],
                sect_in.at[d, dx - 1],
                sect_s.at[d, dx - 1],
                sect_r.at[d, dx - 1],
                sect=lax.rem(x + dx, n_sect),
            )
            for dx in range(1, n_sect)
        ]

    def give_back(d):
        for copy in sect_copies[d]:
            copy.wait_recv()
        total = sect_f32[d, x]
        for j in range(n_sect - 1):
            total = total + sect_in[d, j].astype(F32)
        if d == 0:
            return total
        ret_out[d - 1] = total.astype(BF16)
        ret_copies[d] = send(
            ret_out.at[d - 1],
            ret_in.at[d - 1],
            ret_s.at[d - 1],
            ret_r.at[d - 1],
            attn=behind(d),
        )

    spread(0)
    spread_on(0)
    up(0)
    turns = list(range(1, n_attn)) + [0]
    early = max(0, n_attn - 3)
    for d in range(1, n_attn):
        spread(d)
        if d >= 2:
            spread_on(d - 1)
            up(d - 1)
        if d >= 3:
            to_sect(d - 2)
    spread_on(n_attn - 1)
    up(n_attn - 1)
    for i in range(early - 1):
        give_back(turns[i])
    for i in range(early, n_attn):
        to_sect(turns[i])
        if i:
            give_back(turns[i - 1])
    joined = give_back(0)
    for d in range(1, n_attn):
        ret_copies[d].wait_recv()
        joined = joined + ret_in[d - 1].astype(F32)
    out_ref[...] = (mixed_f32 + joined).astype(BF16)
    for copy in sends:
        copy.wait_send()


def on_device(
    shape,
    queries,
    kv_pool,
    block_list,
    cache_len,
    out_weight,
    residual,
    norm_gain,
    router,
    expert_ids,
    w_gate,
    w_up,
    w_down,
):
    a, s, p = shape["attn"], shape["sect"], shape["pair"]
    q = s * p
    group_rows, head_cols = queries.shape
    own, width = residual.shape
    heads_rows, span = out_weight.shape
    hidden_part = w_gate.shape[2]
    out_cols = w_down.shape[2]
    key_rows, key_cols = kv_pool.shape[2:]
    wide = width + LANES
    buffers = [
        ((a, group_rows, head_cols), BF16),
        ((own, width), BF16),
        ((1, width), F32),
        (router.shape[::-1], BF16),
        (expert_ids.shape[::-1], jnp.int32),
        ((heads_rows, span), BF16),
        ((width, hidden_part), BF16),
        ((width, hidden_part), BF16),
        ((s, hidden_part, out_cols), BF16),
        ((a * kv_pool.shape[1], key_rows, key_cols), BF16),
        ((a, 1, a * kv_pool.shape[1] * key_rows), F32),
        ((a, group_rows, head_cols), BF16),
        ((a, q, own, span), F32),
        ((a, q, own, span), BF16),
        ((a, q - 1, own, span), BF16),
        ((a - 1, own, span), BF16),
        ((a, own, span), BF16),
        ((a, own, span), F32),
        ((a, q, own, wide), BF16),
        ((a, p, s, own, width), F32),
        ((a, p, s, own, width), BF16),
        ((a, p - 1, s, own, width), BF16),
        ((a, s, own, width), F32),
        ((a, s, own, width), BF16),
        ((a, s - 1, own, width), BF16),
        ((a - 1, own, width), BF16),
        ((a - 1, own, width), BF16),
    ]
    held = sum(math.prod(dims) * jnp.dtype(kind).itemsize for dims, kind in buffers)
    fits = (
        2 * held <= VMEM_BYTES
        and span % LANES == 0
        and out_cols % LANES == 0
        and hidden_part % LANES == 0
        and w_gate.shape[0] == 1
        and router.shape[1] <= LANES
        and min(a, s, p) > 1
        and own % 16 == 0
        and own <= LANES
        and group_rows == q * own
        and hidden_part % 16 == 0
        and out_cols * s == width
    )
    if not fits:
        return by_collectives(
            queries,
            kv_pool,
            block_list,
            cache_len,
            out_weight,
            residual,
            norm_gain,
            router,
            expert_ids,
            w_gate,
            w_up,
            w_down,
        )
    sems = [
        (12,),
        (a - 1,),
        (a - 1,),
        (a - 1,),
        (a - 1,),
        (a - 1,),
        (a - 1,),
        (a, q - 1),
        (a, q - 1),
        (a - 1,),
        (a - 1,),
        (a - 1,),
        (a - 1,),
        (a, s - 1),
        (a, s - 1),
        (a, s, p - 1),
        (a, s, p - 1),
        (s - 1,),
        (s - 1,),
        (a, p - 1),
        (a, p - 1),
        (a, s - 1),
        (a, s - 1),
        (a - 1,),
        (a - 1,),
    ]
    vmem = pl.BlockSpec(memory_space=pltpu.VMEM)
    hbm = pl.BlockSpec(memory_space=pltpu.HBM)
    return pl.pallas_call(
        functools.partial(layer_kernel, (a, s, p)),
        out_shape=jax.ShapeDtypeStruct(residual.shape, BF16),
        in_specs=[hbm] * 12,
        out_specs=vmem,
        scratch_shapes=[pltpu.VMEM(dims, kind) for dims, kind in buffers]
        + [pltpu.SMEM(block_list.shape, jnp.int32), pltpu.SMEM((1, 1), jnp.int32)]
        + [pltpu.SemaphoreType.DMA(dims) for dims in sems],
        compiler_params=pltpu.CompilerParams(
            collective_id=0, has_side_effects=True, vmem_limit_bytes=VMEM_BYTES
        ),
    )(
        queries,
        kv_pool,
        block_list,
        cache_len.reshape(1, -1),
        residual,
        norm_gain.reshape(1, -1),
        router.T,
        expert_ids.T,
        out_weight,
        w_gate,
        w_up,
        w_down,
    )


def solution(mesh):
    placed = (
        P(("group", "attn"), ("sect", "pair")),
        P("sect", ("group", "attn"), None, None),
        P(("group", "attn"), None),
        P(("group", "attn")),
        P(("sect", "pair"), "attn"),
        P(("group", "attn", "sect", "pair"), None),
        P(),
        P(),
        P(("group", "attn", "sect", "pair"), None),
        P(("attn", "pair"), None, "sect"),
        P(("attn", "pair"), None, "sect"),
        P(("attn", "pair"), None, "sect"),
    )
    return jax.shard_map(
        functools.partial(on_device, dict(mesh.shape)),
        mesh=mesh,
        in_specs=placed,
        out_specs=P(("group", "attn", "sect", "pair"), None),
        check_vma=False,
    )
```

```python
import functools
import math

import jax
import jax.numpy as jnp
from jax import lax
from jax.experimental import pallas as pl
from jax.experimental.pallas import tpu as pltpu
from jax.sharding import PartitionSpec as P

HEADS = 32
KV_HEADS = 4
HEAD_DIM = 128


def by_collectives(
    queries,
    kv_pool,
    block_list,
    cache_len,
    out_weight,
    residual,
    norm_gain,
    router,
    expert_ids,
    w_gate,
    w_up,
    w_down,
):
    head_dim = HEAD_DIM
    per_kv = HEADS // KV_HEADS
    group_rows, head_cols = queries.shape
    local_heads = head_cols // head_dim
    pool_all = lax.all_gather(kv_pool, "attn", axis=1, tiled=True)
    picked = jnp.take(pool_all, block_list[0], axis=1)
    kv_local = lax.axis_index("pair") * local_heads // per_kv
    chosen = lax.dynamic_index_in_dim(picked, kv_local, 0, keepdims=False)
    chosen = chosen.reshape(-1, 2 * head_dim)
    key_rows = chosen[:, :head_dim]
    values = chosen[:, head_dim:]
    query_heads = queries.reshape(group_rows, local_heads, head_dim)
    scores = jnp.einsum(
        "rhd,td->rht", query_heads, key_rows, preferred_element_type=jnp.float32
    ) / math.sqrt(head_dim)
    live_mask = jnp.arange(key_rows.shape[0]) < cache_len[0]
    scores = jnp.where(live_mask, scores, -jnp.inf)
    row_top = jnp.max(scores, axis=-1, keepdims=True)
    lifted = jnp.exp(scores - row_top)
    row_total = jnp.sum(lifted, axis=-1)
    soft_weights = lifted.astype(jnp.bfloat16)
    mixed_heads = (
        jnp.einsum("rht,td->rhd", soft_weights, values, preferred_element_type=jnp.float32)
        / row_total[..., None]
    )
    attended = mixed_heads.reshape(group_rows, head_cols).astype(jnp.bfloat16)
    partial_value = jnp.dot(
        attended,
        lax.all_gather(out_weight, "attn", axis=1, tiled=True),
        preferred_element_type=jnp.float32,
    )
    summed = lax.psum_scatter(partial_value, ("sect", "pair"), scatter_dimension=0, tiled=True)
    mixed_f32 = residual.astype(jnp.float32) + summed
    mixed_rows = mixed_f32.astype(jnp.bfloat16)
    mixed_f32 = mixed_rows.astype(jnp.float32)
    normed = (
        mixed_f32
        * lax.rsqrt(jnp.mean(mixed_f32 * mixed_f32, axis=-1, keepdims=True) + 1e-06)
        * norm_gain
    ).astype(jnp.bfloat16)
    logits = jnp.dot(normed, router, preferred_element_type=jnp.float32)
    chosen_logits = jnp.take_along_axis(logits, expert_ids, axis=1)
    route_weights = jax.nn.softmax(chosen_logits, axis=-1)
    row_count, top_count = expert_ids.shape
    expert_count = router.shape[1]
    model_width = residual.shape[1]
    capacity = max(2, row_count * top_count // expert_count * 2)
    flat_ids = expert_ids.reshape(-1)
    onehot = (flat_ids[:, None] == jnp.arange(expert_count, dtype=jnp.int32)[None, :]).astype(
        jnp.int32
    )
    earlier = jnp.cumsum(onehot, axis=0) - onehot
    slot_index = jnp.sum(earlier * onehot, axis=1)
    source = jnp.repeat(jnp.arange(row_count, dtype=jnp.int32), top_count)
    outgoing = (
        jnp.zeros((expert_count, capacity, model_width), jnp.bfloat16)
        .at[flat_ids, slot_index]
        .set(normed[source])
    )
    received = lax.all_to_all(outgoing, ("attn", "pair"), split_axis=0, concat_axis=0, tiled=True)
    sections = lax.axis_size("sect")
    every_section = lax.all_gather(received, "sect", axis=0, tiled=True)
    tokens_in = every_section.reshape(-1, model_width)
    gate_val = jnp.dot(tokens_in, w_gate[0], preferred_element_type=jnp.float32)
    up_val = jnp.dot(tokens_in, w_up[0], preferred_element_type=jnp.float32)
    part_hidden = (jax.nn.silu(gate_val) * up_val).astype(jnp.bfloat16)
    hidden = lax.all_gather(part_hidden, "sect", axis=1, tiled=True)
    out_slice = jnp.dot(hidden, w_down[0], preferred_element_type=jnp.float32).astype(jnp.bfloat16)
    out_slice = out_slice.reshape(sections, expert_count, capacity, model_width // sections)
    segmented = lax.all_to_all(out_slice, "sect", split_axis=0, concat_axis=3, tiled=True)
    returned = lax.all_to_all(
        segmented[0], ("attn", "pair"), split_axis=0, concat_axis=0, tiled=True
    )
    gathered = (
        returned[flat_ids, slot_index]
        .reshape(row_count, top_count, model_width)
        .astype(jnp.float32)
    )
    joined = jnp.sum(route_weights[:, :, None] * gathered, axis=1)
    return (mixed_f32 + joined).astype(jnp.bfloat16)


MESH = pl.DeviceIdType.MESH
LANES = 128
VMEM_BYTES = 60 * 1024 * 1024
BF16 = jnp.bfloat16
F32 = jnp.float32


def layer_kernel(
    sizes,
    q_hbm,
    kv_hbm,
    list_hbm,
    len_hbm,
    res_hbm,
    gain_hbm,
    router_hbm,
    ids_hbm,
    wo_hbm,
    wg_hbm,
    wu_hbm,
    wd_hbm,
    out_ref,
    q_ref,
    res_ref,
    gain_ref,
    router_ref,
    ids_ref,
    wo,
    wg,
    wu,
    wd,
    kvbuf,
    att,
    part,
    mix_own,
    mix_in,
    mix_f32,
    rows,
    prod_f32,
    prod,
    pair_in,
    sect_f32,
    sect,
    sect_in,
    ret_out,
    ret_in,
    list_ref,
    len_ref,
    w_sem,
    kv_s,
    kv_r,
    att_s,
    att_r,
    mix_s,
    mix_r,
    nz_s,
    nz_r,
    nx_s,
    nx_r,
    nc_s,
    nc_r,
    wd_s,
    wd_r,
    pair_s,
    pair_r,
    sect_s,
    sect_r,
    ret_s,
    ret_r,
):
    n_attn, n_sect, n_pair = sizes
    quarters = n_sect * n_pair
    z = lax.axis_index("attn")
    x = lax.axis_index("sect")
    c = lax.axis_index("pair")
    quarter = x * n_pair + c
    own = res_ref.shape[0]
    width = res_ref.shape[1]
    group_rows, head_cols = q_ref.shape
    local_heads = head_cols // HEAD_DIM
    kv_local = c * local_heads // (HEADS // KV_HEADS)
    blocks = kv_hbm.shape[1]
    kv_slot = pl.ds(z * blocks, blocks)
    hidden_part = wg.shape[1]
    sends = []

    def send(src, dst, s_sem, r_sem, **where):
        copy = pltpu.make_async_remote_copy(
            src_ref=src,
            dst_ref=dst,
            send_sem=s_sem,
            recv_sem=r_sem,
            device_id=where,
            device_id_type=MESH,
        )
        copy.start()
        sends.append(copy)
        return copy

    loads = [
        pltpu.make_async_copy(src, dst, w_sem.at[i])
        for i, (src, dst) in enumerate(
            (
                (q_hbm, q_ref),
                (kv_hbm.at[kv_local], kvbuf.at[kv_slot]),
                (list_hbm, list_ref),
                (len_hbm, len_ref),
                (wo_hbm, wo),
                (res_hbm, res_ref),
                (gain_hbm, gain_ref),
                (router_hbm, router_ref),
                (ids_hbm, ids_ref),
                (wg_hbm.at[0], wg),
                (wu_hbm.at[0], wu),
                (wd_hbm.at[0, pl.ds(x * hidden_part, hidden_part)], wd.at[x]),
            )
        )
    ]
    for load in loads:
        load.start()

    barrier = pltpu.get_barrier_semaphore()
    for dz in range(n_attn):
        for dx in range(n_sect):
            for dc in range(n_pair):
                if dz + dx + dc:
                    pl.semaphore_signal(
                        barrier,
                        inc=1,
                        device_id={
                            "attn": lax.rem(z + dz, n_attn),
                            "sect": lax.rem(x + dx, n_sect),
                            "pair": lax.rem(c + dc, n_pair),
                        },
                        device_id_type=MESH,
                    )
    pl.semaphore_wait(barrier, n_attn * quarters - 1)

    def ahead(d):
        return lax.rem(z + d, n_attn)

    def behind(d):
        return lax.rem(z + (n_attn - d), n_attn)

    kv_copies = [
        send(
            kv_hbm.at[kv_local],
            kvbuf.at[kv_slot],
            kv_s.at[d - 1],
            kv_r.at[d - 1],
            attn=ahead(d),
        )
        for d in range(1, n_attn)
    ]
    wd_copies = []
    for dx in range(1, n_sect):
        to_x = lax.rem(x + dx, n_sect)
        wd_copies.append(
            send(
                wd_hbm.at[0, pl.ds(to_x * hidden_part, hidden_part)],
                wd.at[x],
                wd_s.at[dx - 1],
                wd_r.at[dx - 1],
                sect=to_x,
            )
        )
    for load in loads[:4]:
        load.wait()
    for copy in kv_copies:
        copy.wait_recv()

    listed = list_ref.shape[1]
    picked = [kvbuf[list_ref[0, j]] for j in range(listed)]
    cache = jnp.concatenate(picked, axis=0)
    keys = cache[:, :HEAD_DIM]
    values = cache[:, HEAD_DIM:]
    heads = jnp.concatenate(
        [q_ref[:, h * HEAD_DIM : (h + 1) * HEAD_DIM] for h in range(local_heads)], axis=0
    )
    scores = lax.dot_general(
        heads, keys, (((1,), (1,)), ((), ())), preferred_element_type=F32
    ) * (1.0 / math.sqrt(HEAD_DIM))
    place = lax.broadcasted_iota(jnp.int32, scores.shape, 1)
    scores = jnp.where(place < len_ref[0, 0], scores, -jnp.inf)
    lifted = jnp.exp(scores - jnp.max(scores, axis=-1, keepdims=True))
    row_total = jnp.sum(lifted, axis=-1, keepdims=True)
    mixed = jnp.dot(lifted.astype(BF16), values, preferred_element_type=F32) / row_total
    for h in range(local_heads):
        att[0, :, h * HEAD_DIM : (h + 1) * HEAD_DIM] = mixed[
            h * group_rows : (h + 1) * group_rows
        ].astype(BF16)
    att_copies = [None] + [
        send(att.at[0], att.at[d], att_s.at[d - 1], att_r.at[d - 1], attn=ahead(d))
        for d in range(1, n_attn)
    ]

    def plane(step):
        return lax.div(step, n_pair), lax.rem(step, n_pair)

    loads[4].wait()
    for d in range(n_attn):
        if d:
            att_copies[d].wait_recv()
        value = jnp.dot(att[d], wo[...], preferred_element_type=F32)
        value = value.reshape(part.shape[1:])
        part[d] = value.astype(BF16)
        if d == 0:
            mix_own[...] = value
        for j in range(quarters):
            if d + j == 0:
                continue
            to = lax.rem(quarter + j, quarters)
            to_x, to_c = plane(to)
            send(
                part.at[d, to],
                mix_in.at[z, j],
                mix_s.at[d, j],
                mix_r.at[z, j],
                attn=behind(d),
                sect=to_x,
                pair=to_c,
            )
    for d in range(n_attn):
        src = ahead(d)
        total = None
        for j in range(quarters):
            if d + j == 0:
                total = mix_own[quarter]
                continue
            pltpu.make_async_remote_copy(
                src_ref=part.at[d, j],
                dst_ref=mix_in.at[src, j],
                send_sem=mix_s.at[d, j],
                recv_sem=mix_r.at[src, j],
                device_id={"attn": ahead(1)},
                device_id_type=MESH,
            ).wait_recv()
            got = mix_in[src, j].astype(F32)
            total = got if total is None else total + got
        mix_f32[src] = total
    for load in loads[5:9]:
        load.wait()

    span = width // n_attn
    mixed_f32 = res_ref[...].astype(F32) + jnp.concatenate(
        [mix_f32[a] for a in range(n_attn)], axis=1
    )
    mixed_f32 = mixed_f32.astype(BF16).astype(F32)
    normed = (
        mixed_f32
        * lax.rsqrt(jnp.mean(mixed_f32 * mixed_f32, axis=-1, keepdims=True) + 1e-06)
        * gain_ref[...]
    ).astype(BF16)
    logits = lax.dot_general(
        router_ref[...], normed, (((1,), (1,)), ((), ())), preferred_element_type=F32
    )
    lane = lax.broadcasted_iota(jnp.int32, logits.shape, 0)
    chosen = lane == ids_ref[0:1, :]
    for k in range(1, ids_ref.shape[0]):
        chosen = jnp.logical_or(chosen, lane == ids_ref[k : k + 1, :])
    logits = jnp.where(chosen, logits, -jnp.inf)
    raised = jnp.exp(logits - jnp.max(logits, axis=0, keepdims=True))
    route = raised / jnp.sum(raised, axis=0, keepdims=True)
    route = jnp.concatenate(
        [route, jnp.zeros((LANES - route.shape[0], own), F32)], axis=0
    )
    route = jnp.transpose(
        jnp.concatenate([route, jnp.zeros((LANES, LANES - own), F32)], axis=1)
    )[:own]
    rows[0, quarter, :, :width] = normed
    rows[0, quarter, :, width:] = route.astype(BF16)

    nz_copies = [None] + [
        send(
            rows.at[0, quarter],
            rows.at[d, quarter],
            nz_s.at[d - 1],
            nz_r.at[d - 1],
            attn=ahead(d),
        )
        for d in range(1, n_attn)
    ]
    nx_copies = [None] * n_attn
    nc_copies = [None] * n_attn
    for load in loads[9:]:
        load.wait()
    for copy in wd_copies:
        copy.wait_recv()

    def to_cores(d, dx):
        from_q = lax.rem(x + (n_sect - dx), n_sect) * n_pair + c
        return [
            send(
                rows.at[d, from_q],
                rows.at[d, from_q],
                nc_s.at[d, dx, dc - 1],
                nc_r.at[d, dx, dc - 1],
                pair=lax.rem(c + dc, n_pair),
            )
            for dc in range(1, n_pair)
        ]

    def spread(d):
        if d:
            nz_copies[d].wait_recv()
        nx_copies[d] = [
            send(
                rows.at[d, quarter],
                rows.at[d, quarter],
                nx_s.at[d, dx - 1],
                nx_r.at[d, dx - 1],
                sect=lax.rem(x + dx, n_sect),
            )
            for dx in range(1, n_sect)
        ]
        nc_copies[d] = to_cores(d, 0)

    def spread_on(d):
        for dx in range(1, n_sect):
            nx_copies[d][dx - 1].wait_recv()
            nc_copies[d] += to_cores(d, dx)

    sect_copies = [None] * n_attn
    pair_copies = [None] * n_attn
    ret_copies = [None] * n_attn
    expert = z * n_pair + c

    def up(d):
        for copy in nc_copies[d]:
            copy.wait_recv()
        tokens = rows[d].reshape(quarters * own, rows.shape[-1])[:, :width]
        gate_val = jnp.dot(tokens, wg[...], preferred_element_type=F32)
        up_val = jnp.dot(tokens, wu[...], preferred_element_type=F32)
        hidden = (gate_val / (1.0 + jnp.exp(-gate_val)) * up_val).astype(BF16)
        value = jnp.concatenate(
            [jnp.dot(hidden, wd[i], preferred_element_type=F32) for i in range(n_sect)],
            axis=1,
        )
        weights = rows[d].reshape(quarters * own, rows.shape[-1])[:, width:].astype(F32)
        lanes = lax.broadcasted_iota(jnp.int32, weights.shape, 1)
        weight = jnp.sum(jnp.where(lanes == expert, weights, 0.0), axis=-1, keepdims=True)
        value = (value * weight).reshape(n_sect, n_pair, own, value.shape[-1])
        for i in range(n_sect):
            for j in range(n_pair):
                prod_f32[d, j, i] = value[i, j]
                prod[d, j, i] = value[i, j].astype(BF16)
        pair_copies[d] = [
            send(
                prod.at[d, lax.rem(c + dc, n_pair)],
                pair_in.at[d, dc - 1],
                pair_s.at[d, dc - 1],
                pair_r.at[d, dc - 1],
                pair=lax.rem(c + dc, n_pair),
            )
            for dc in range(1, n_pair)
        ]

    def to_sect(d):
        for copy in pair_copies[d]:
            copy.wait_recv()
        total = prod_f32[d, c]
        for j in range(n_pair - 1):
            total = total + pair_in[d, j].astype(F32)
        sect_f32[d] = total
        sect[d] = total.astype(BF16)
        sect_copies[d] = [
            send(
                sect.at[d, lax.rem(x + dx, n_sect)],
                sect_in.at[d, dx - 1],
                sect_s.at[d, dx - 1],
                sect_r.at[d, dx - 1],
                sect=lax.rem(x + dx, n_sect),
            )
            for dx in range(1, n_sect)
        ]

    def give_back(d):
        for copy in sect_copies[d]:
            copy.wait_recv()
        total = sect_f32[d, x]
        for j in range(n_sect - 1):
            total = total + sect_in[d, j].astype(F32)
        if d == 0:
            return total
        ret_out[d - 1] = total.astype(BF16)
        ret_copies[d] = send(
            ret_out.at[d - 1],
            ret_in.at[d - 1],
            ret_s.at[d - 1],
            ret_r.at[d - 1],
            attn=behind(d),
        )

    spread(0)
    spread_on(0)
    up(0)
    turns = list(range(1, n_attn)) + [0]
    early = max(0, n_attn - 3)
    for d in range(1, n_attn):
        spread(d)
        if d >= 2:
            spread_on(d - 1)
            up(d - 1)
        if d >= 3:
            to_sect(d - 2)
    spread_on(n_attn - 1)
    up(n_attn - 1)
    for i in range(early - 1):
        give_back(turns[i])
    for i in range(early, n_attn):
        to_sect(turns[i])
        if i:
            give_back(turns[i - 1])
    joined = give_back(0)
    for d in range(1, n_attn):
        ret_copies[d].wait_recv()
        joined = joined + ret_in[d - 1].astype(F32)
    out_ref[...] = (mixed_f32 + joined).astype(BF16)
    for copy in sends:
        copy.wait_send()


def on_device(
    shape,
    queries,
    kv_pool,
    block_list,
    cache_len,
    out_weight,
    residual,
    norm_gain,
    router,
    expert_ids,
    w_gate,
    w_up,
    w_down,
):
    a, s, p = shape["attn"], shape["sect"], shape["pair"]
    q = s * p
    group_rows, head_cols = queries.shape
    own, width = residual.shape
    heads_rows, span = out_weight.shape
    hidden_part = w_gate.shape[2]
    out_cols = w_down.shape[2]
    key_rows, key_cols = kv_pool.shape[2:]
    wide = width + LANES
    buffers = [
        ((group_rows, head_cols), BF16),
        ((own, width), BF16),
        ((1, width), F32),
        (router.shape[::-1], BF16),
        (expert_ids.shape[::-1], jnp.int32),
        ((heads_rows, span), BF16),
        ((width, hidden_part), BF16),
        ((width, hidden_part), BF16),
        ((s, hidden_part, out_cols), BF16),
        ((a * kv_pool.shape[1], key_rows, key_cols), BF16),
        ((a, group_rows, head_cols), BF16),
        ((a, q, own, span), BF16),
        ((q, own, span), F32),
        ((a, q, own, span), BF16),
        ((a, own, span), F32),
        ((a, q, own, wide), BF16),
        ((a, p, s, own, width), F32),
        ((a, p, s, own, width), BF16),
        ((a, p - 1, s, own, width), BF16),
        ((a, s, own, width), F32),
        ((a, s, own, width), BF16),
        ((a, s - 1, own, width), BF16),
        ((a - 1, own, width), BF16),
        ((a - 1, own, width), BF16),
    ]
    held = sum(math.prod(dims) * jnp.dtype(kind).itemsize for dims, kind in buffers)
    fits = (
        2 * held <= VMEM_BYTES
        and span % LANES == 0
        and out_cols % LANES == 0
        and hidden_part % LANES == 0
        and w_gate.shape[0] == 1
        and router.shape[1] <= LANES
        and min(a, s, p) > 1
        and own % 16 == 0
        and own <= LANES
        and group_rows == q * own
        and hidden_part % 16 == 0
        and out_cols * s == width
    )
    if not fits:
        return by_collectives(
            queries,
            kv_pool,
            block_list,
            cache_len,
            out_weight,
            residual,
            norm_gain,
            router,
            expert_ids,
            w_gate,
            w_up,
            w_down,
        )
    sems = [
        (12,),
        (a - 1,),
        (a - 1,),
        (a - 1,),
        (a - 1,),
        (a, q),
        (a, q),
        (a - 1,),
        (a - 1,),
        (a, s - 1),
        (a, s - 1),
        (a, s, p - 1),
        (a, s, p - 1),
        (s - 1,),
        (s - 1,),
        (a, p - 1),
        (a, p - 1),
        (a, s - 1),
        (a, s - 1),
        (a - 1,),
        (a - 1,),
    ]
    vmem = pl.BlockSpec(memory_space=pltpu.VMEM)
    hbm = pl.BlockSpec(memory_space=pltpu.HBM)
    return pl.pallas_call(
        functools.partial(layer_kernel, (a, s, p)),
        out_shape=jax.ShapeDtypeStruct(residual.shape, BF16),
        in_specs=[hbm] * 12,
        out_specs=vmem,
        scratch_shapes=[pltpu.VMEM(dims, kind) for dims, kind in buffers]
        + [pltpu.SMEM(block_list.shape, jnp.int32), pltpu.SMEM((1, 1), jnp.int32)]
        + [pltpu.SemaphoreType.DMA(dims) for dims in sems],
        compiler_params=pltpu.CompilerParams(
            collective_id=0, has_side_effects=True, vmem_limit_bytes=VMEM_BYTES
        ),
    )(
        queries,
        kv_pool,
        block_list,
        cache_len.reshape(1, -1),
        residual,
        norm_gain.reshape(1, -1),
        router.T,
        expert_ids.T,
        out_weight,
        w_gate,
        w_up,
        w_down,
    )


def solution(mesh):
    placed = (
        P(("group", "attn"), ("sect", "pair")),
        P("sect", ("group", "attn"), None, None),
        P(("group", "attn"), None),
        P(("group", "attn")),
        P(("sect", "pair"), "attn"),
        P(("group", "attn", "sect", "pair"), None),
        P(),
        P(),
        P(("group", "attn", "sect", "pair"), None),
        P(("attn", "pair"), None, "sect"),
        P(("attn", "pair"), None, "sect"),
        P(("attn", "pair"), None, "sect"),
    )
    return jax.shard_map(
        functools.partial(on_device, dict(mesh.shape)),
        mesh=mesh,
        in_specs=placed,
        out_specs=P(("group", "attn", "sect", "pair"), None),
        check_vma=False,
    )
```

```python
import functools
import math

import jax
import jax.numpy as jnp
from jax import lax
from jax.experimental import pallas as pl
from jax.experimental.pallas import tpu as pltpu
from jax.sharding import PartitionSpec as P

HEADS = 32
KV_HEADS = 4
HEAD_DIM = 128


def by_collectives(
    queries,
    kv_pool,
    block_list,
    cache_len,
    out_weight,
    residual,
    norm_gain,
    router,
    expert_ids,
    w_gate,
    w_up,
    w_down,
):
    head_dim = HEAD_DIM
    per_kv = HEADS // KV_HEADS
    group_rows, head_cols = queries.shape
    local_heads = head_cols // head_dim
    pool_all = lax.all_gather(kv_pool, "attn", axis=1, tiled=True)
    picked = jnp.take(pool_all, block_list[0], axis=1)
    kv_local = lax.axis_index("pair") * local_heads // per_kv
    chosen = lax.dynamic_index_in_dim(picked, kv_local, 0, keepdims=False)
    chosen = chosen.reshape(-1, 2 * head_dim)
    key_rows = chosen[:, :head_dim]
    values = chosen[:, head_dim:]
    query_heads = queries.reshape(group_rows, local_heads, head_dim)
    scores = jnp.einsum(
        "rhd,td->rht", query_heads, key_rows, preferred_element_type=jnp.float32
    ) / math.sqrt(head_dim)
    live_mask = jnp.arange(key_rows.shape[0]) < cache_len[0]
    scores = jnp.where(live_mask, scores, -jnp.inf)
    row_top = jnp.max(scores, axis=-1, keepdims=True)
    lifted = jnp.exp(scores - row_top)
    row_total = jnp.sum(lifted, axis=-1)
    soft_weights = lifted.astype(jnp.bfloat16)
    mixed_heads = (
        jnp.einsum("rht,td->rhd", soft_weights, values, preferred_element_type=jnp.float32)
        / row_total[..., None]
    )
    attended = mixed_heads.reshape(group_rows, head_cols).astype(jnp.bfloat16)
    partial_value = jnp.dot(
        attended,
        lax.all_gather(out_weight, "attn", axis=1, tiled=True),
        preferred_element_type=jnp.float32,
    )
    summed = lax.psum_scatter(partial_value, ("sect", "pair"), scatter_dimension=0, tiled=True)
    mixed_f32 = residual.astype(jnp.float32) + summed
    mixed_rows = mixed_f32.astype(jnp.bfloat16)
    mixed_f32 = mixed_rows.astype(jnp.float32)
    normed = (
        mixed_f32
        * lax.rsqrt(jnp.mean(mixed_f32 * mixed_f32, axis=-1, keepdims=True) + 1e-06)
        * norm_gain
    ).astype(jnp.bfloat16)
    logits = jnp.dot(normed, router, preferred_element_type=jnp.float32)
    chosen_logits = jnp.take_along_axis(logits, expert_ids, axis=1)
    route_weights = jax.nn.softmax(chosen_logits, axis=-1)
    row_count, top_count = expert_ids.shape
    expert_count = router.shape[1]
    model_width = residual.shape[1]
    capacity = max(2, row_count * top_count // expert_count * 2)
    flat_ids = expert_ids.reshape(-1)
    onehot = (flat_ids[:, None] == jnp.arange(expert_count, dtype=jnp.int32)[None, :]).astype(
        jnp.int32
    )
    earlier = jnp.cumsum(onehot, axis=0) - onehot
    slot_index = jnp.sum(earlier * onehot, axis=1)
    source = jnp.repeat(jnp.arange(row_count, dtype=jnp.int32), top_count)
    outgoing = (
        jnp.zeros((expert_count, capacity, model_width), jnp.bfloat16)
        .at[flat_ids, slot_index]
        .set(normed[source])
    )
    received = lax.all_to_all(outgoing, ("attn", "pair"), split_axis=0, concat_axis=0, tiled=True)
    sections = lax.axis_size("sect")
    every_section = lax.all_gather(received, "sect", axis=0, tiled=True)
    tokens_in = every_section.reshape(-1, model_width)
    gate_val = jnp.dot(tokens_in, w_gate[0], preferred_element_type=jnp.float32)
    up_val = jnp.dot(tokens_in, w_up[0], preferred_element_type=jnp.float32)
    part_hidden = (jax.nn.silu(gate_val) * up_val).astype(jnp.bfloat16)
    hidden = lax.all_gather(part_hidden, "sect", axis=1, tiled=True)
    out_slice = jnp.dot(hidden, w_down[0], preferred_element_type=jnp.float32).astype(jnp.bfloat16)
    out_slice = out_slice.reshape(sections, expert_count, capacity, model_width // sections)
    segmented = lax.all_to_all(out_slice, "sect", split_axis=0, concat_axis=3, tiled=True)
    returned = lax.all_to_all(
        segmented[0], ("attn", "pair"), split_axis=0, concat_axis=0, tiled=True
    )
    gathered = (
        returned[flat_ids, slot_index]
        .reshape(row_count, top_count, model_width)
        .astype(jnp.float32)
    )
    joined = jnp.sum(route_weights[:, :, None] * gathered, axis=1)
    return (mixed_f32 + joined).astype(jnp.bfloat16)


MESH = pl.DeviceIdType.MESH
LANES = 128
VMEM_BYTES = 60 * 1024 * 1024
BF16 = jnp.bfloat16
F32 = jnp.float32


def layer_kernel(
    sizes,
    q_hbm,
    kv_hbm,
    list_hbm,
    len_hbm,
    res_hbm,
    gain_hbm,
    router_hbm,
    ids_hbm,
    wo_hbm,
    wg_hbm,
    wu_hbm,
    wd_hbm,
    out_ref,
    q_ref,
    res_ref,
    gain_ref,
    router_ref,
    ids_ref,
    wo,
    wg,
    wu,
    wd,
    kvbuf,
    att,
    part_f32,
    part,
    rs_in,
    sum_out,
    mix_in,
    mix_f32,
    rows,
    prod_f32,
    prod,
    pair_in,
    sect_f32,
    sect,
    sect_in,
    ret_out,
    ret_in,
    list_ref,
    len_ref,
    w_sem,
    kv_s,
    kv_r,
    att_s,
    att_r,
    rs_s,
    rs_r,
    mix_s,
    mix_r,
    nz_s,
    nz_r,
    nx_s,
    nx_r,
    nc_s,
    nc_r,
    wd_s,
    wd_r,
    pair_s,
    pair_r,
    sect_s,
    sect_r,
    ret_s,
    ret_r,
):
    n_attn, n_sect, n_pair = sizes
    quarters = n_sect * n_pair
    z = lax.axis_index("attn")
    x = lax.axis_index("sect")
    c = lax.axis_index("pair")
    quarter = x * n_pair + c
    own = res_ref.shape[0]
    width = res_ref.shape[1]
    group_rows, head_cols = q_ref.shape
    local_heads = head_cols // HEAD_DIM
    kv_local = c * local_heads // (HEADS // KV_HEADS)
    blocks = kv_hbm.shape[1]
    kv_slot = pl.ds(z * blocks, blocks)
    hidden_part = wg.shape[1]
    sends = []

    def send(src, dst, s_sem, r_sem, **where):
        copy = pltpu.make_async_remote_copy(
            src_ref=src,
            dst_ref=dst,
            send_sem=s_sem,
            recv_sem=r_sem,
            device_id=where,
            device_id_type=MESH,
        )
        copy.start()
        sends.append(copy)
        return copy

    loads = [
        pltpu.make_async_copy(src, dst, w_sem.at[i])
        for i, (src, dst) in enumerate(
            (
                (q_hbm, q_ref),
                (kv_hbm.at[kv_local], kvbuf.at[kv_slot]),
                (list_hbm, list_ref),
                (len_hbm, len_ref),
                (wo_hbm, wo),
                (res_hbm, res_ref),
                (gain_hbm, gain_ref),
                (router_hbm, router_ref),
                (ids_hbm, ids_ref),
                (wg_hbm.at[0], wg),
                (wu_hbm.at[0], wu),
                (wd_hbm.at[0, pl.ds(x * hidden_part, hidden_part)], wd.at[x]),
            )
        )
    ]
    for load in loads:
        load.start()

    barrier = pltpu.get_barrier_semaphore()
    for dz in range(n_attn):
        for dx in range(n_sect):
            for dc in range(n_pair):
                if dz + dx + dc:
                    pl.semaphore_signal(
                        barrier,
                        inc=1,
                        device_id={
                            "attn": lax.rem(z + dz, n_attn),
                            "sect": lax.rem(x + dx, n_sect),
                            "pair": lax.rem(c + dc, n_pair),
                        },
                        device_id_type=MESH,
                    )
    pl.semaphore_wait(barrier, n_attn * quarters - 1)

    def ahead(d):
        return lax.rem(z + d, n_attn)

    def behind(d):
        return lax.rem(z + (n_attn - d), n_attn)

    kv_copies = [
        send(
            kv_hbm.at[kv_local],
            kvbuf.at[kv_slot],
            kv_s.at[d - 1],
            kv_r.at[d - 1],
            attn=ahead(d),
        )
        for d in range(1, n_attn)
    ]
    wd_copies = []
    for dx in range(1, n_sect):
        to_x = lax.rem(x + dx, n_sect)
        wd_copies.append(
            send(
                wd_hbm.at[0, pl.ds(to_x * hidden_part, hidden_part)],
                wd.at[x],
                wd_s.at[dx - 1],
                wd_r.at[dx - 1],
                sect=to_x,
            )
        )
    for load in loads[:4]:
        load.wait()
    for copy in kv_copies:
        copy.wait_recv()

    listed = list_ref.shape[1]
    picked = [kvbuf[list_ref[0, j]] for j in range(listed)]
    cache = jnp.concatenate(picked, axis=0)
    keys = cache[:, :HEAD_DIM]
    values = cache[:, HEAD_DIM:]
    pieces, piece_cols = att.shape[1], att.shape[3]
    piece_heads = piece_cols // HEAD_DIM
    att_copies = [[] for _ in range(n_attn)]
    for piece in range(pieces):
        start = piece * piece_cols
        heads = jnp.concatenate(
            [
                q_ref[:, start + h * HEAD_DIM : start + (h + 1) * HEAD_DIM]
                for h in range(piece_heads)
            ],
            axis=0,
        )
        scores = lax.dot_general(
            heads, keys, (((1,), (1,)), ((), ())), preferred_element_type=F32
        ) * (1.0 / math.sqrt(HEAD_DIM))
        place = lax.broadcasted_iota(jnp.int32, scores.shape, 1)
        scores = jnp.where(place < len_ref[0, 0], scores, -jnp.inf)
        lifted = jnp.exp(scores - jnp.max(scores, axis=-1, keepdims=True))
        row_total = jnp.sum(lifted, axis=-1, keepdims=True)
        mixed = jnp.dot(lifted.astype(BF16), values, preferred_element_type=F32) / row_total
        for h in range(piece_heads):
            att[0, piece, :, h * HEAD_DIM : (h + 1) * HEAD_DIM] = mixed[
                h * group_rows : (h + 1) * group_rows
            ].astype(BF16)
        for d in range(1, n_attn):
            att_copies[d].append(
                send(
                    att.at[0, piece],
                    att.at[d, piece],
                    att_s.at[d - 1, piece],
                    att_r.at[d - 1, piece],
                    attn=ahead(d),
                )
            )

    def plane(step):
        return lax.div(step, n_pair), lax.rem(step, n_pair)

    loads[4].wait()
    rs_copies = []
    mix_copies = []

    def project(d):
        for copy in att_copies[d]:
            copy.wait_recv()
        value = jnp.dot(att[d, 0], wo[:piece_cols], preferred_element_type=F32)
        for piece in range(1, pieces):
            value += jnp.dot(
                att[d, piece],
                wo[piece * piece_cols : (piece + 1) * piece_cols],
                preferred_element_type=F32,
            )
        value = value.reshape(part_f32.shape[1:])
        part_f32[d] = value
        part[d] = value.astype(BF16)
        copies = []
        for j in range(1, quarters):
            to = lax.rem(quarter + j, quarters)
            to_x, to_c = plane(to)
            copies.append(
                send(
                    part.at[d, to],
                    rs_in.at[d, j - 1],
                    rs_s.at[d, j - 1],
                    rs_r.at[d, j - 1],
                    sect=to_x,
                    pair=to_c,
                )
            )
        rs_copies.append(copies)

    def pass_on(d):
        for copy in rs_copies[d]:
            copy.wait_recv()
        total = part_f32[d, quarter]
        for j in range(quarters - 1):
            total = total + rs_in[d, j].astype(F32)
        if d == 0:
            mix_f32[z] = total
        else:
            sum_out[d - 1] = total.astype(BF16)
            mix_copies.append(
                send(
                    sum_out.at[d - 1],
                    mix_in.at[z],
                    mix_s.at[d - 1],
                    mix_r.at[d - 1],
                    attn=behind(d),
                )
            )

    for d in range(n_attn + 1):
        if d < n_attn:
            project(d)
        if d:
            pass_on(d - 1)
    for d in range(1, n_attn):
        mix_copies[d - 1].wait_recv()
        mix_f32[ahead(d)] = mix_in[ahead(d)].astype(F32)

    for load in loads[5:9]:
        load.wait()

    span = width // n_attn
    mixed_f32 = res_ref[...].astype(F32) + jnp.concatenate(
        [mix_f32[a] for a in range(n_attn)], axis=1
    )
    mixed_f32 = mixed_f32.astype(BF16).astype(F32)
    normed = (
        mixed_f32
        * lax.rsqrt(jnp.mean(mixed_f32 * mixed_f32, axis=-1, keepdims=True) + 1e-06)
        * gain_ref[...]
    ).astype(BF16)
    logits = lax.dot_general(
        router_ref[...], normed, (((1,), (1,)), ((), ())), preferred_element_type=F32
    )
    lane = lax.broadcasted_iota(jnp.int32, logits.shape, 0)
    chosen = lane == ids_ref[0:1, :]
    for k in range(1, ids_ref.shape[0]):
        chosen = jnp.logical_or(chosen, lane == ids_ref[k : k + 1, :])
    logits = jnp.where(chosen, logits, -jnp.inf)
    raised = jnp.exp(logits - jnp.max(logits, axis=0, keepdims=True))
    route = raised / jnp.sum(raised, axis=0, keepdims=True)
    route = jnp.concatenate(
        [route, jnp.zeros((LANES - route.shape[0], own), F32)], axis=0
    )
    route = jnp.transpose(
        jnp.concatenate([route, jnp.zeros((LANES, LANES - own), F32)], axis=1)
    )[:own]
    rows[0, quarter, :, :width] = normed
    rows[0, quarter, :, width:] = route.astype(BF16)

    nz_copies = [None] + [
        send(
            rows.at[0, quarter],
            rows.at[d, quarter],
            nz_s.at[d - 1],
            nz_r.at[d - 1],
            attn=ahead(d),
        )
        for d in range(1, n_attn)
    ]
    nx_copies = [None] * n_attn
    nc_copies = [None] * n_attn
    for load in loads[9:]:
        load.wait()
    for copy in wd_copies:
        copy.wait_recv()

    def to_cores(d, dx):
        from_q = lax.rem(x + (n_sect - dx), n_sect) * n_pair + c
        return [
            send(
                rows.at[d, from_q],
                rows.at[d, from_q],
                nc_s.at[d, dx, dc - 1],
                nc_r.at[d, dx, dc - 1],
                pair=lax.rem(c + dc, n_pair),
            )
            for dc in range(1, n_pair)
        ]

    def spread(d):
        if d:
            nz_copies[d].wait_recv()
        nx_copies[d] = [
            send(
                rows.at[d, quarter],
                rows.at[d, quarter],
                nx_s.at[d, dx - 1],
                nx_r.at[d, dx - 1],
                sect=lax.rem(x + dx, n_sect),
            )
            for dx in range(1, n_sect)
        ]
        nc_copies[d] = to_cores(d, 0)

    def spread_on(d):
        for dx in range(1, n_sect):
            nx_copies[d][dx - 1].wait_recv()
            nc_copies[d] += to_cores(d, dx)

    sect_copies = [None] * n_attn
    pair_copies = [None] * n_attn
    ret_copies = [None] * n_attn
    expert = z * n_pair + c

    def up(d):
        for copy in nc_copies[d]:
            copy.wait_recv()
        tokens = rows[d].reshape(quarters * own, rows.shape[-1])[:, :width]
        gate_val = jnp.dot(tokens, wg[...], preferred_element_type=F32)
        up_val = jnp.dot(tokens, wu[...], preferred_element_type=F32)
        hidden = (gate_val / (1.0 + jnp.exp(-gate_val)) * up_val).astype(BF16)
        value = jnp.concatenate(
            [jnp.dot(hidden, wd[i], preferred_element_type=F32) for i in range(n_sect)],
            axis=1,
        )
        weights = rows[d].reshape(quarters * own, rows.shape[-1])[:, width:].astype(F32)
        lanes = lax.broadcasted_iota(jnp.int32, weights.shape, 1)
        weight = jnp.sum(jnp.where(lanes == expert, weights, 0.0), axis=-1, keepdims=True)
        value = (value * weight).reshape(n_sect, n_pair, own, value.shape[-1])
        for i in range(n_sect):
            for j in range(n_pair):
                prod_f32[d, j, i] = value[i, j]
                prod[d, j, i] = value[i, j].astype(BF16)
        pair_copies[d] = [
            send(
                prod.at[d, lax.rem(c + dc, n_pair)],
                pair_in.at[d, dc - 1],
                pair_s.at[d, dc - 1],
                pair_r.at[d, dc - 1],
                pair=lax.rem(c + dc, n_pair),
            )
            for dc in range(1, n_pair)
        ]

    def to_sect(d):
        for copy in pair_copies[d]:
            copy.wait_recv()
        total = prod_f32[d, c]
        for j in range(n_pair - 1):
            total = total + pair_in[d, j].astype(F32)
        sect_f32[d] = total
        sect[d] = total.astype(BF16)
        sect_copies[d] = [
            send(
                sect.at[d, lax.rem(x + dx, n_sect)],
                sect_in.at[d, dx - 1],
                sect_s.at[d, dx - 1],
                sect_r.at[d, dx - 1],
                sect=lax.rem(x + dx, n_sect),
            )
            for dx in range(1, n_sect)
        ]

    def give_back(d):
        for copy in sect_copies[d]:
            copy.wait_recv()
        total = sect_f32[d, x]
        for j in range(n_sect - 1):
            total = total + sect_in[d, j].astype(F32)
        if d == 0:
            return total
        ret_out[d - 1] = total.astype(BF16)
        ret_copies[d] = send(
            ret_out.at[d - 1],
            ret_in.at[d - 1],
            ret_s.at[d - 1],
            ret_r.at[d - 1],
            attn=behind(d),
        )

    spread(0)
    spread_on(0)
    up(0)
    early = max(0, n_attn - 3)
    for d in range(1, n_attn):
        spread(d)
        if d == 1:
            to_sect(0)
        else:
            spread_on(d - 1)
            up(d - 1)
        if d >= 3:
            to_sect(d - 2)
    spread_on(n_attn - 1)
    up(n_attn - 1)
    for d in range(1, early):
        give_back(d)
    for d in range(early + 1, n_attn):
        to_sect(d)
        if d > 1:
            give_back(d - 1)
    give_back(n_attn - 1)
    joined = give_back(0)
    for d in range(1, n_attn):
        ret_copies[d].wait_recv()
        joined = joined + ret_in[d - 1].astype(F32)
    out_ref[...] = (mixed_f32 + joined).astype(BF16)
    for copy in sends:
        copy.wait_send()


def on_device(
    shape,
    queries,
    kv_pool,
    block_list,
    cache_len,
    out_weight,
    residual,
    norm_gain,
    router,
    expert_ids,
    w_gate,
    w_up,
    w_down,
):
    a, s, p = shape["attn"], shape["sect"], shape["pair"]
    q = s * p
    group_rows, head_cols = queries.shape
    own, width = residual.shape
    heads_rows, span = out_weight.shape
    hidden_part = w_gate.shape[2]
    out_cols = w_down.shape[2]
    key_rows, key_cols = kv_pool.shape[2:]
    wide = width + LANES
    pieces = 2 - head_cols // HEAD_DIM % 2
    buffers = [
        ((group_rows, head_cols), BF16),
        ((own, width), BF16),
        ((1, width), F32),
        (router.shape[::-1], BF16),
        (expert_ids.shape[::-1], jnp.int32),
        ((heads_rows, span), BF16),
        ((width, hidden_part), BF16),
        ((width, hidden_part), BF16),
        ((s, hidden_part, out_cols), BF16),
        ((a * kv_pool.shape[1], key_rows, key_cols), BF16),
        ((a, pieces, group_rows, head_cols // pieces), BF16),
        ((a, q, own, span), F32),
        ((a, q, own, span), BF16),
        ((a, q - 1, own, span), BF16),
        ((a - 1, own, span), BF16),
        ((a, own, span), BF16),
        ((a, own, span), F32),
        ((a, q, own, wide), BF16),
        ((a, p, s, own, width), F32),
        ((a, p, s, own, width), BF16),
        ((a, p - 1, s, own, width), BF16),
        ((a, s, own, width), F32),
        ((a, s, own, width), BF16),
        ((a, s - 1, own, width), BF16),
        ((a - 1, own, width), BF16),
        ((a - 1, own, width), BF16),
    ]
    held = sum(math.prod(dims) * jnp.dtype(kind).itemsize for dims, kind in buffers)
    fits = (
        2 * held <= VMEM_BYTES
        and span % LANES == 0
        and out_cols % LANES == 0
        and hidden_part % LANES == 0
        and w_gate.shape[0] == 1
        and router.shape[1] <= LANES
        and min(a, s, p) > 1
        and own % 16 == 0
        and own <= LANES
        and group_rows == q * own
        and hidden_part % 16 == 0
        and out_cols * s == width
    )
    if not fits:
        return by_collectives(
            queries,
            kv_pool,
            block_list,
            cache_len,
            out_weight,
            residual,
            norm_gain,
            router,
            expert_ids,
            w_gate,
            w_up,
            w_down,
        )
    sems = [
        (12,),
        (a - 1,),
        (a - 1,),
        (a - 1, pieces),
        (a - 1, pieces),
        (a, q - 1),
        (a, q - 1),
        (a - 1,),
        (a - 1,),
        (a - 1,),
        (a - 1,),
        (a, s - 1),
        (a, s - 1),
        (a, s, p - 1),
        (a, s, p - 1),
        (s - 1,),
        (s - 1,),
        (a, p - 1),
        (a, p - 1),
        (a, s - 1),
        (a, s - 1),
        (a - 1,),
        (a - 1,),
    ]
    vmem = pl.BlockSpec(memory_space=pltpu.VMEM)
    hbm = pl.BlockSpec(memory_space=pltpu.HBM)
    return pl.pallas_call(
        functools.partial(layer_kernel, (a, s, p)),
        out_shape=jax.ShapeDtypeStruct(residual.shape, BF16),
        in_specs=[hbm] * 12,
        out_specs=vmem,
        scratch_shapes=[pltpu.VMEM(dims, kind) for dims, kind in buffers]
        + [pltpu.SMEM(block_list.shape, jnp.int32), pltpu.SMEM((1, 1), jnp.int32)]
        + [pltpu.SemaphoreType.DMA(dims) for dims in sems],
        compiler_params=pltpu.CompilerParams(
            collective_id=0, has_side_effects=True, vmem_limit_bytes=VMEM_BYTES
        ),
    )(
        queries,
        kv_pool,
        block_list,
        cache_len.reshape(1, -1),
        residual,
        norm_gain.reshape(1, -1),
        router.T,
        expert_ids.T,
        out_weight,
        w_gate,
        w_up,
        w_down,
    )


def solution(mesh):
    placed = (
        P(("group", "attn"), ("sect", "pair")),
        P("sect", ("group", "attn"), None, None),
        P(("group", "attn"), None),
        P(("group", "attn")),
        P(("sect", "pair"), "attn"),
        P(("group", "attn", "sect", "pair"), None),
        P(),
        P(),
        P(("group", "attn", "sect", "pair"), None),
        P(("attn", "pair"), None, "sect"),
        P(("attn", "pair"), None, "sect"),
        P(("attn", "pair"), None, "sect"),
    )
    return jax.shard_map(
        functools.partial(on_device, dict(mesh.shape)),
        mesh=mesh,
        in_specs=placed,
        out_specs=P(("group", "attn", "sect", "pair"), None),
        check_vma=False,
    )
```

```python
import functools
import math

import jax
import jax.numpy as jnp
from jax import lax
from jax.experimental import pallas as pl
from jax.experimental.pallas import tpu as pltpu
from jax.sharding import PartitionSpec as P

HEADS = 32
KV_HEADS = 4
HEAD_DIM = 128


def by_collectives(
    queries,
    kv_pool,
    block_list,
    cache_len,
    out_weight,
    residual,
    norm_gain,
    router,
    expert_ids,
    w_gate,
    w_up,
    w_down,
):
    head_dim = HEAD_DIM
    per_kv = HEADS // KV_HEADS
    group_rows, head_cols = queries.shape
    local_heads = head_cols // head_dim
    pool_all = lax.all_gather(kv_pool, "attn", axis=1, tiled=True)
    picked = jnp.take(pool_all, block_list[0], axis=1)
    kv_local = lax.axis_index("pair") * local_heads // per_kv
    chosen = lax.dynamic_index_in_dim(picked, kv_local, 0, keepdims=False)
    chosen = chosen.reshape(-1, 2 * head_dim)
    key_rows = chosen[:, :head_dim]
    values = chosen[:, head_dim:]
    query_heads = queries.reshape(group_rows, local_heads, head_dim)
    scores = jnp.einsum(
        "rhd,td->rht", query_heads, key_rows, preferred_element_type=jnp.float32
    ) / math.sqrt(head_dim)
    live_mask = jnp.arange(key_rows.shape[0]) < cache_len[0]
    scores = jnp.where(live_mask, scores, -jnp.inf)
    row_top = jnp.max(scores, axis=-1, keepdims=True)
    lifted = jnp.exp(scores - row_top)
    row_total = jnp.sum(lifted, axis=-1)
    soft_weights = lifted.astype(jnp.bfloat16)
    mixed_heads = (
        jnp.einsum("rht,td->rhd", soft_weights, values, preferred_element_type=jnp.float32)
        / row_total[..., None]
    )
    attended = mixed_heads.reshape(group_rows, head_cols).astype(jnp.bfloat16)
    partial_value = jnp.dot(
        attended,
        lax.all_gather(out_weight, "attn", axis=1, tiled=True),
        preferred_element_type=jnp.float32,
    )
    summed = lax.psum_scatter(partial_value, ("sect", "pair"), scatter_dimension=0, tiled=True)
    mixed_f32 = residual.astype(jnp.float32) + summed
    mixed_rows = mixed_f32.astype(jnp.bfloat16)
    mixed_f32 = mixed_rows.astype(jnp.float32)
    normed = (
        mixed_f32
        * lax.rsqrt(jnp.mean(mixed_f32 * mixed_f32, axis=-1, keepdims=True) + 1e-06)
        * norm_gain
    ).astype(jnp.bfloat16)
    logits = jnp.dot(normed, router, preferred_element_type=jnp.float32)
    chosen_logits = jnp.take_along_axis(logits, expert_ids, axis=1)
    route_weights = jax.nn.softmax(chosen_logits, axis=-1)
    row_count, top_count = expert_ids.shape
    expert_count = router.shape[1]
    model_width = residual.shape[1]
    capacity = max(2, row_count * top_count // expert_count * 2)
    flat_ids = expert_ids.reshape(-1)
    onehot = (flat_ids[:, None] == jnp.arange(expert_count, dtype=jnp.int32)[None, :]).astype(
        jnp.int32
    )
    earlier = jnp.cumsum(onehot, axis=0) - onehot
    slot_index = jnp.sum(earlier * onehot, axis=1)
    source = jnp.repeat(jnp.arange(row_count, dtype=jnp.int32), top_count)
    outgoing = (
        jnp.zeros((expert_count, capacity, model_width), jnp.bfloat16)
        .at[flat_ids, slot_index]
        .set(normed[source])
    )
    received = lax.all_to_all(outgoing, ("attn", "pair"), split_axis=0, concat_axis=0, tiled=True)
    sections = lax.axis_size("sect")
    every_section = lax.all_gather(received, "sect", axis=0, tiled=True)
    tokens_in = every_section.reshape(-1, model_width)
    gate_val = jnp.dot(tokens_in, w_gate[0], preferred_element_type=jnp.float32)
    up_val = jnp.dot(tokens_in, w_up[0], preferred_element_type=jnp.float32)
    part_hidden = (jax.nn.silu(gate_val) * up_val).astype(jnp.bfloat16)
    hidden = lax.all_gather(part_hidden, "sect", axis=1, tiled=True)
    out_slice = jnp.dot(hidden, w_down[0], preferred_element_type=jnp.float32).astype(jnp.bfloat16)
    out_slice = out_slice.reshape(sections, expert_count, capacity, model_width // sections)
    segmented = lax.all_to_all(out_slice, "sect", split_axis=0, concat_axis=3, tiled=True)
    returned = lax.all_to_all(
        segmented[0], ("attn", "pair"), split_axis=0, concat_axis=0, tiled=True
    )
    gathered = (
        returned[flat_ids, slot_index]
        .reshape(row_count, top_count, model_width)
        .astype(jnp.float32)
    )
    joined = jnp.sum(route_weights[:, :, None] * gathered, axis=1)
    return (mixed_f32 + joined).astype(jnp.bfloat16)


MESH = pl.DeviceIdType.MESH
LANES = 128
VMEM_BYTES = 60 * 1024 * 1024
BF16 = jnp.bfloat16
F32 = jnp.float32


def layer_kernel(
    sizes,
    q_hbm,
    kv_hbm,
    list_hbm,
    len_hbm,
    res_hbm,
    gain_hbm,
    router_hbm,
    ids_hbm,
    wo_hbm,
    wg_hbm,
    wu_hbm,
    wd_hbm,
    out_ref,
    q_ref,
    res_ref,
    gain_ref,
    router_ref,
    ids_ref,
    wo,
    wg,
    wu,
    wd,
    kvbuf,
    att,
    part_f32,
    part,
    rs_in,
    sum_out,
    mix_in,
    mix_f32,
    rows,
    prod_f32,
    prod,
    pair_in,
    sect_f32,
    sect,
    sect_in,
    ret_out,
    ret_in,
    list_ref,
    len_ref,
    w_sem,
    kv_s,
    kv_r,
    att_s,
    att_r,
    rs_s,
    rs_r,
    mix_s,
    mix_r,
    nz_s,
    nz_r,
    nx_s,
    nx_r,
    nc_s,
    nc_r,
    wd_s,
    wd_r,
    pair_s,
    pair_r,
    sect_s,
    sect_r,
    ret_s,
    ret_r,
):
    n_attn, n_sect, n_pair = sizes
    quarters = n_sect * n_pair
    z = lax.axis_index("attn")
    x = lax.axis_index("sect")
    c = lax.axis_index("pair")
    quarter = x * n_pair + c
    own = res_ref.shape[0]
    width = res_ref.shape[1]
    group_rows, head_cols = q_ref.shape
    local_heads = head_cols // HEAD_DIM
    kv_local = c * local_heads // (HEADS // KV_HEADS)
    blocks = kv_hbm.shape[1]
    kv_slot = pl.ds(z * blocks, blocks)
    hidden_part = wg.shape[1]
    sends = []

    def send(src, dst, s_sem, r_sem, **where):
        copy = pltpu.make_async_remote_copy(
            src_ref=src,
            dst_ref=dst,
            send_sem=s_sem,
            recv_sem=r_sem,
            device_id=where,
            device_id_type=MESH,
        )
        copy.start()
        sends.append(copy)
        return copy

    loads = [
        pltpu.make_async_copy(src, dst, w_sem.at[i])
        for i, (src, dst) in enumerate(
            (
                (q_hbm, q_ref),
                (kv_hbm.at[kv_local], kvbuf.at[kv_slot]),
                (list_hbm, list_ref),
                (len_hbm, len_ref),
                (wo_hbm, wo),
                (res_hbm, res_ref),
                (gain_hbm, gain_ref),
                (router_hbm, router_ref),
                (ids_hbm, ids_ref),
                (wg_hbm.at[0], wg),
                (wu_hbm.at[0], wu),
                (wd_hbm.at[0, pl.ds(x * hidden_part, hidden_part)], wd.at[x]),
            )
        )
    ]
    for load in loads:
        load.start()

    barrier = pltpu.get_barrier_semaphore()
    for dz in range(n_attn):
        for dx in range(n_sect):
            for dc in range(n_pair):
                if (dz == 0) != (dx + dc == 0):
                    pl.semaphore_signal(
                        barrier,
                        inc=1,
                        device_id={
                            "attn": lax.rem(z + dz, n_attn),
                            "sect": lax.rem(x + dx, n_sect),
                            "pair": lax.rem(c + dc, n_pair),
                        },
                        device_id_type=MESH,
                    )
    pl.semaphore_wait(barrier, n_attn + quarters - 2)

    def ahead(d):
        return lax.rem(z + d, n_attn)

    def behind(d):
        return lax.rem(z + (n_attn - d), n_attn)

    kv_copies = [
        send(
            kv_hbm.at[kv_local],
            kvbuf.at[kv_slot],
            kv_s.at[d - 1],
            kv_r.at[d - 1],
            attn=ahead(d),
        )
        for d in range(1, n_attn)
    ]
    wd_copies = []
    for dx in range(1, n_sect):
        to_x = lax.rem(x + dx, n_sect)
        wd_copies.append(
            send(
                wd_hbm.at[0, pl.ds(to_x * hidden_part, hidden_part)],
                wd.at[x],
                wd_s.at[dx - 1],
                wd_r.at[dx - 1],
                sect=to_x,
            )
        )
    for load in loads[:4]:
        load.wait()
    for copy in kv_copies:
        copy.wait_recv()

    listed = list_ref.shape[1]
    picked = [kvbuf[list_ref[0, j]] for j in range(listed)]
    cache = jnp.concatenate(picked, axis=0)
    keys = cache[:, :HEAD_DIM]
    values = cache[:, HEAD_DIM:]
    heads = jnp.concatenate(
        [q_ref[:, h * HEAD_DIM : (h + 1) * HEAD_DIM] for h in range(local_heads)], axis=0
    )
    scores = lax.dot_general(
        heads, keys, (((1,), (1,)), ((), ())), preferred_element_type=F32
    ) * (1.0 / math.sqrt(HEAD_DIM))
    place = lax.broadcasted_iota(jnp.int32, scores.shape, 1)
    scores = jnp.where(place < len_ref[0, 0], scores, -jnp.inf)
    lifted = jnp.exp(scores - jnp.max(scores, axis=-1, keepdims=True))
    row_total = jnp.sum(lifted, axis=-1, keepdims=True)
    mixed = jnp.dot(lifted.astype(BF16), values, preferred_element_type=F32) / row_total
    for h in range(local_heads):
        att[0, :, h * HEAD_DIM : (h + 1) * HEAD_DIM] = mixed[
            h * group_rows : (h + 1) * group_rows
        ].astype(BF16)
    att_copies = [None] + [
        send(att.at[0], att.at[d], att_s.at[d - 1], att_r.at[d - 1], attn=ahead(d))
        for d in range(1, n_attn)
    ]

    def plane(step):
        return lax.div(step, n_pair), lax.rem(step, n_pair)

    loads[4].wait()
    rs_copies = []
    mix_copies = []

    def project(d):
        if d:
            att_copies[d].wait_recv()
        value = jnp.dot(att[d], wo[...], preferred_element_type=F32)
        value = value.reshape(part_f32.shape[1:])
        part_f32[d] = value
        part[d] = value.astype(BF16)
        copies = []
        for j in range(1, quarters):
            to = lax.rem(quarter + j, quarters)
            to_x, to_c = plane(to)
            copies.append(
                send(
                    part.at[d, to],
                    rs_in.at[d, j - 1],
                    rs_s.at[d, j - 1],
                    rs_r.at[d, j - 1],
                    sect=to_x,
                    pair=to_c,
                )
            )
        rs_copies.append(copies)

    def pass_on(d):
        for copy in rs_copies[d]:
            copy.wait_recv()
        total = part_f32[d, quarter]
        for j in range(quarters - 1):
            total = total + rs_in[d, j].astype(F32)
        if d == 0:
            mix_f32[z] = total
        else:
            sum_out[d - 1] = total.astype(BF16)
            mix_copies.append(
                send(
                    sum_out.at[d - 1],
                    mix_in.at[z],
                    mix_s.at[d - 1],
                    mix_r.at[d - 1],
                    attn=behind(d),
                )
            )

    for d in range(n_attn + 1):
        if d < n_attn:
            project(d)
        if d:
            pass_on(d - 1)
    for d in range(1, n_attn):
        mix_copies[d - 1].wait_recv()
        mix_f32[ahead(d)] = mix_in[ahead(d)].astype(F32)

    for load in loads[5:9]:
        load.wait()

    span = width // n_attn
    mixed_f32 = res_ref[...].astype(F32) + jnp.concatenate(
        [mix_f32[a] for a in range(n_attn)], axis=1
    )
    mixed_f32 = mixed_f32.astype(BF16).astype(F32)
    normed = (
        mixed_f32
        * lax.rsqrt(jnp.mean(mixed_f32 * mixed_f32, axis=-1, keepdims=True) + 1e-06)
        * gain_ref[...]
    ).astype(BF16)
    logits = lax.dot_general(
        router_ref[...], normed, (((1,), (1,)), ((), ())), preferred_element_type=F32
    )
    lane = lax.broadcasted_iota(jnp.int32, logits.shape, 0)
    chosen = lane == ids_ref[0:1, :]
    for k in range(1, ids_ref.shape[0]):
        chosen = jnp.logical_or(chosen, lane == ids_ref[k : k + 1, :])
    logits = jnp.where(chosen, logits, -jnp.inf)
    raised = jnp.exp(logits - jnp.max(logits, axis=0, keepdims=True))
    route = raised / jnp.sum(raised, axis=0, keepdims=True)
    route = jnp.concatenate(
        [route, jnp.zeros((LANES - route.shape[0], own), F32)], axis=0
    )
    route = jnp.transpose(
        jnp.concatenate([route, jnp.zeros((LANES, LANES - own), F32)], axis=1)
    )[:own]
    rows[0, quarter, :, :width] = normed
    rows[0, quarter, :, width:] = route.astype(BF16)

    nz_copies = [None] + [
        send(
            rows.at[0, quarter],
            rows.at[d, quarter],
            nz_s.at[d - 1],
            nz_r.at[d - 1],
            attn=ahead(d),
        )
        for d in range(1, n_attn)
    ]
    nx_copies = [None] * n_attn
    nc_copies = [None] * n_attn
    for load in loads[9:]:
        load.wait()
    for copy in wd_copies:
        copy.wait_recv()

    def to_cores(d, dx):
        from_q = lax.rem(x + (n_sect - dx), n_sect) * n_pair + c
        return [
            send(
                rows.at[d, from_q],
                rows.at[d, from_q],
                nc_s.at[d, dx, dc - 1],
                nc_r.at[d, dx, dc - 1],
                pair=lax.rem(c + dc, n_pair),
            )
            for dc in range(1, n_pair)
        ]

    def spread(d):
        if d:
            nz_copies[d].wait_recv()
        nx_copies[d] = [
            send(
                rows.at[d, quarter],
                rows.at[d, quarter],
                nx_s.at[d, dx - 1],
                nx_r.at[d, dx - 1],
                sect=lax.rem(x + dx, n_sect),
            )
            for dx in range(1, n_sect)
        ]
        nc_copies[d] = to_cores(d, 0)

    def spread_on(d):
        for dx in range(1, n_sect):
            nx_copies[d][dx - 1].wait_recv()
            nc_copies[d] += to_cores(d, dx)

    sect_copies = [None] * n_attn
    pair_copies = [None] * n_attn
    ret_copies = [None] * n_attn
    expert = z * n_pair + c

    def up(d):
        for copy in nc_copies[d]:
            copy.wait_recv()
        tokens = rows[d].reshape(quarters * own, rows.shape[-1])[:, :width]
        gate_val = jnp.dot(tokens, wg[...], preferred_element_type=F32)
        up_val = jnp.dot(tokens, wu[...], preferred_element_type=F32)
        hidden = (gate_val / (1.0 + jnp.exp(-gate_val)) * up_val).astype(BF16)
        value = jnp.concatenate(
            [jnp.dot(hidden, wd[i], preferred_element_type=F32) for i in range(n_sect)],
            axis=1,
        )
        weights = rows[d].reshape(quarters * own, rows.shape[-1])[:, width:].astype(F32)
        lanes = lax.broadcasted_iota(jnp.int32, weights.shape, 1)
        weight = jnp.sum(jnp.where(lanes == expert, weights, 0.0), axis=-1, keepdims=True)
        value = (value * weight).reshape(n_sect, n_pair, own, value.shape[-1])
        for i in range(n_sect):
            for j in range(n_pair):
                prod_f32[d, j, i] = value[i, j]
                prod[d, j, i] = value[i, j].astype(BF16)
        pair_copies[d] = [
            send(
                prod.at[d, lax.rem(c + dc, n_pair)],
                pair_in.at[d, dc - 1],
                pair_s.at[d, dc - 1],
                pair_r.at[d, dc - 1],
                pair=lax.rem(c + dc, n_pair),
            )
            for dc in range(1, n_pair)
        ]

    def to_sect(d):
        for copy in pair_copies[d]:
            copy.wait_recv()
        total = prod_f32[d, c]
        for j in range(n_pair - 1):
            total = total + pair_in[d, j].astype(F32)
        sect_f32[d] = total
        sect[d] = total.astype(BF16)
        sect_copies[d] = [
            send(
                sect.at[d, lax.rem(x + dx, n_sect)],
                sect_in.at[d, dx - 1],
                sect_s.at[d, dx - 1],
                sect_r.at[d, dx - 1],
                sect=lax.rem(x + dx, n_sect),
            )
            for dx in range(1, n_sect)
        ]

    def give_back(d):
        for copy in sect_copies[d]:
            copy.wait_recv()
        total = sect_f32[d, x]
        for j in range(n_sect - 1):
            total = total + sect_in[d, j].astype(F32)
        if d == 0:
            return total
        ret_out[d - 1] = total.astype(BF16)
        ret_copies[d] = send(
            ret_out.at[d - 1],
            ret_in.at[d - 1],
            ret_s.at[d - 1],
            ret_r.at[d - 1],
            attn=behind(d),
        )

    spread(0)
    spread_on(0)
    up(0)
    turns = list(range(1, n_attn)) + [0]
    early = max(0, n_attn - 3)
    for d in range(1, n_attn):
        spread(d)
        if d >= 2:
            spread_on(d - 1)
            up(d - 1)
        if d >= 3:
            to_sect(d - 2)
    spread_on(n_attn - 1)
    up(n_attn - 1)
    for i in range(early - 1):
        give_back(turns[i])
    for i in range(early, n_attn):
        to_sect(turns[i])
        if i:
            give_back(turns[i - 1])
    joined = give_back(0)
    for d in range(1, n_attn):
        ret_copies[d].wait_recv()
        joined = joined + ret_in[d - 1].astype(F32)
    out_ref[...] = (mixed_f32 + joined).astype(BF16)
    for copy in sends:
        copy.wait_send()


def on_device(
    shape,
    queries,
    kv_pool,
    block_list,
    cache_len,
    out_weight,
    residual,
    norm_gain,
    router,
    expert_ids,
    w_gate,
    w_up,
    w_down,
):
    a, s, p = shape["attn"], shape["sect"], shape["pair"]
    q = s * p
    group_rows, head_cols = queries.shape
    own, width = residual.shape
    heads_rows, span = out_weight.shape
    hidden_part = w_gate.shape[2]
    out_cols = w_down.shape[2]
    key_rows, key_cols = kv_pool.shape[2:]
    wide = width + LANES
    buffers = [
        ((group_rows, head_cols), BF16),
        ((own, width), BF16),
        ((1, width), F32),
        (router.shape[::-1], BF16),
        (expert_ids.shape[::-1], jnp.int32),
        ((heads_rows, span), BF16),
        ((width, hidden_part), BF16),
        ((width, hidden_part), BF16),
        ((s, hidden_part, out_cols), BF16),
        ((a * kv_pool.shape[1], key_rows, key_cols), BF16),
        ((a, group_rows, head_cols), BF16),
        ((a, q, own, span), F32),
        ((a, q, own, span), BF16),
        ((a, q - 1, own, span), BF16),
        ((a - 1, own, span), BF16),
        ((a, own, span), BF16),
        ((a, own, span), F32),
        ((a, q, own, wide), BF16),
        ((a, p, s, own, width), F32),
        ((a, p, s, own, width), BF16),
        ((a, p - 1, s, own, width), BF16),
        ((a, s, own, width), F32),
        ((a, s, own, width), BF16),
        ((a, s - 1, own, width), BF16),
        ((a - 1, own, width), BF16),
        ((a - 1, own, width), BF16),
    ]
    held = sum(math.prod(dims) * jnp.dtype(kind).itemsize for dims, kind in buffers)
    fits = (
        2 * held <= VMEM_BYTES
        and span % LANES == 0
        and out_cols % LANES == 0
        and hidden_part % LANES == 0
        and w_gate.shape[0] == 1
        and router.shape[1] <= LANES
        and min(a, s, p) > 1
        and own % 16 == 0
        and own <= LANES
        and group_rows == q * own
        and hidden_part % 16 == 0
        and out_cols * s == width
    )
    if not fits:
        return by_collectives(
            queries,
            kv_pool,
            block_list,
            cache_len,
            out_weight,
            residual,
            norm_gain,
            router,
            expert_ids,
            w_gate,
            w_up,
            w_down,
        )
    sems = [
        (12,),
        (a - 1,),
        (a - 1,),
        (a - 1,),
        (a - 1,),
        (a, q - 1),
        (a, q - 1),
        (a - 1,),
        (a - 1,),
        (a - 1,),
        (a - 1,),
        (a, s - 1),
        (a, s - 1),
        (a, s, p - 1),
        (a, s, p - 1),
        (s - 1,),
        (s - 1,),
        (a, p - 1),
        (a, p - 1),
        (a, s - 1),
        (a, s - 1),
        (a - 1,),
        (a - 1,),
    ]
    vmem = pl.BlockSpec(memory_space=pltpu.VMEM)
    hbm = pl.BlockSpec(memory_space=pltpu.HBM)
    return pl.pallas_call(
        functools.partial(layer_kernel, (a, s, p)),
        out_shape=jax.ShapeDtypeStruct(residual.shape, BF16),
        in_specs=[hbm] * 12,
        out_specs=vmem,
        scratch_shapes=[pltpu.VMEM(dims, kind) for dims, kind in buffers]
        + [pltpu.SMEM(block_list.shape, jnp.int32), pltpu.SMEM((1, 1), jnp.int32)]
        + [pltpu.SemaphoreType.DMA(dims) for dims in sems],
        compiler_params=pltpu.CompilerParams(
            collective_id=0, has_side_effects=True, vmem_limit_bytes=VMEM_BYTES
        ),
    )(
        queries,
        kv_pool,
        block_list,
        cache_len.reshape(1, -1),
        residual,
        norm_gain.reshape(1, -1),
        router.T,
        expert_ids.T,
        out_weight,
        w_gate,
        w_up,
        w_down,
    )


def solution(mesh):
    placed = (
        P(("group", "attn"), ("sect", "pair")),
        P("sect", ("group", "attn"), None, None),
        P(("group", "attn"), None),
        P(("group", "attn")),
        P(("sect", "pair"), "attn"),
        P(("group", "attn", "sect", "pair"), None),
        P(),
        P(),
        P(("group", "attn", "sect", "pair"), None),
        P(("attn", "pair"), None, "sect"),
        P(("attn", "pair"), None, "sect"),
        P(("attn", "pair"), None, "sect"),
    )
    return jax.shard_map(
        functools.partial(on_device, dict(mesh.shape)),
        mesh=mesh,
        in_specs=placed,
        out_specs=P(("group", "attn", "sect", "pair"), None),
        check_vma=False,
    )
```

```python
import functools
import math

import jax
import jax.numpy as jnp
from jax import lax
from jax.experimental import pallas as pl
from jax.experimental.pallas import tpu as pltpu
from jax.sharding import PartitionSpec as P

HEADS = 32
KV_HEADS = 4
HEAD_DIM = 128


def by_collectives(
    queries,
    kv_pool,
    block_list,
    cache_len,
    out_weight,
    residual,
    norm_gain,
    router,
    expert_ids,
    w_gate,
    w_up,
    w_down,
):
    head_dim = HEAD_DIM
    per_kv = HEADS // KV_HEADS
    group_rows, head_cols = queries.shape
    local_heads = head_cols // head_dim
    pool_all = lax.all_gather(kv_pool, "attn", axis=1, tiled=True)
    picked = jnp.take(pool_all, block_list[0], axis=1)
    kv_local = lax.axis_index("pair") * local_heads // per_kv
    chosen = lax.dynamic_index_in_dim(picked, kv_local, 0, keepdims=False)
    chosen = chosen.reshape(-1, 2 * head_dim)
    key_rows = chosen[:, :head_dim]
    values = chosen[:, head_dim:]
    query_heads = queries.reshape(group_rows, local_heads, head_dim)
    scores = jnp.einsum(
        "rhd,td->rht", query_heads, key_rows, preferred_element_type=jnp.float32
    ) / math.sqrt(head_dim)
    live_mask = jnp.arange(key_rows.shape[0]) < cache_len[0]
    scores = jnp.where(live_mask, scores, -jnp.inf)
    row_top = jnp.max(scores, axis=-1, keepdims=True)
    lifted = jnp.exp(scores - row_top)
    row_total = jnp.sum(lifted, axis=-1)
    soft_weights = lifted.astype(jnp.bfloat16)
    mixed_heads = (
        jnp.einsum("rht,td->rhd", soft_weights, values, preferred_element_type=jnp.float32)
        / row_total[..., None]
    )
    attended = mixed_heads.reshape(group_rows, head_cols).astype(jnp.bfloat16)
    partial_value = jnp.dot(
        attended,
        lax.all_gather(out_weight, "attn", axis=1, tiled=True),
        preferred_element_type=jnp.float32,
    )
    summed = lax.psum_scatter(partial_value, ("sect", "pair"), scatter_dimension=0, tiled=True)
    mixed_f32 = residual.astype(jnp.float32) + summed
    mixed_rows = mixed_f32.astype(jnp.bfloat16)
    mixed_f32 = mixed_rows.astype(jnp.float32)
    normed = (
        mixed_f32
        * lax.rsqrt(jnp.mean(mixed_f32 * mixed_f32, axis=-1, keepdims=True) + 1e-06)
        * norm_gain
    ).astype(jnp.bfloat16)
    logits = jnp.dot(normed, router, preferred_element_type=jnp.float32)
    chosen_logits = jnp.take_along_axis(logits, expert_ids, axis=1)
    route_weights = jax.nn.softmax(chosen_logits, axis=-1)
    row_count, top_count = expert_ids.shape
    expert_count = router.shape[1]
    model_width = residual.shape[1]
    capacity = max(2, row_count * top_count // expert_count * 2)
    flat_ids = expert_ids.reshape(-1)
    onehot = (flat_ids[:, None] == jnp.arange(expert_count, dtype=jnp.int32)[None, :]).astype(
        jnp.int32
    )
    earlier = jnp.cumsum(onehot, axis=0) - onehot
    slot_index = jnp.sum(earlier * onehot, axis=1)
    source = jnp.repeat(jnp.arange(row_count, dtype=jnp.int32), top_count)
    outgoing = (
        jnp.zeros((expert_count, capacity, model_width), jnp.bfloat16)
        .at[flat_ids, slot_index]
        .set(normed[source])
    )
    received = lax.all_to_all(outgoing, ("attn", "pair"), split_axis=0, concat_axis=0, tiled=True)
    sections = lax.axis_size("sect")
    every_section = lax.all_gather(received, "sect", axis=0, tiled=True)
    tokens_in = every_section.reshape(-1, model_width)
    gate_val = jnp.dot(tokens_in, w_gate[0], preferred_element_type=jnp.float32)
    up_val = jnp.dot(tokens_in, w_up[0], preferred_element_type=jnp.float32)
    part_hidden = (jax.nn.silu(gate_val) * up_val).astype(jnp.bfloat16)
    hidden = lax.all_gather(part_hidden, "sect", axis=1, tiled=True)
    out_slice = jnp.dot(hidden, w_down[0], preferred_element_type=jnp.float32).astype(jnp.bfloat16)
    out_slice = out_slice.reshape(sections, expert_count, capacity, model_width // sections)
    segmented = lax.all_to_all(out_slice, "sect", split_axis=0, concat_axis=3, tiled=True)
    returned = lax.all_to_all(
        segmented[0], ("attn", "pair"), split_axis=0, concat_axis=0, tiled=True
    )
    gathered = (
        returned[flat_ids, slot_index]
        .reshape(row_count, top_count, model_width)
        .astype(jnp.float32)
    )
    joined = jnp.sum(route_weights[:, :, None] * gathered, axis=1)
    return (mixed_f32 + joined).astype(jnp.bfloat16)


MESH = pl.DeviceIdType.MESH
LANES = 128
VMEM_BYTES = 60 * 1024 * 1024
BF16 = jnp.bfloat16
F32 = jnp.float32


def layer_kernel(
    sizes,
    q_hbm,
    kv_hbm,
    list_hbm,
    len_hbm,
    res_hbm,
    gain_hbm,
    router_hbm,
    ids_hbm,
    wo_hbm,
    wg_hbm,
    wu_hbm,
    wd_hbm,
    out_ref,
    q_ref,
    res_ref,
    gain_ref,
    router_ref,
    ids_ref,
    wo,
    wg,
    wu,
    wd,
    kvbuf,
    att,
    part_f32,
    part,
    rs_in,
    sum_out,
    mix_in,
    mix_f32,
    rows,
    prod_f32,
    prod,
    pair_in,
    sect_f32,
    sect,
    sect_in,
    ret_out,
    ret_in,
    list_ref,
    len_ref,
    w_sem,
    kv_s,
    kv_r,
    att_s,
    att_r,
    rs_s,
    rs_r,
    mix_s,
    mix_r,
    nz_s,
    nz_r,
    nx_s,
    nx_r,
    nc_s,
    nc_r,
    wd_s,
    wd_r,
    pair_s,
    pair_r,
    sect_s,
    sect_r,
    ret_s,
    ret_r,
):
    n_attn, n_sect, n_pair = sizes
    quarters = n_sect * n_pair
    z = lax.axis_index("attn")
    x = lax.axis_index("sect")
    c = lax.axis_index("pair")
    quarter = x * n_pair + c
    own = res_ref.shape[0]
    width = res_ref.shape[1]
    group_rows, head_cols = q_ref.shape
    local_heads = head_cols // HEAD_DIM
    kv_local = c * local_heads // (HEADS // KV_HEADS)
    blocks = kv_hbm.shape[1]
    kv_slot = pl.ds(z * blocks, blocks)
    hidden_part = wg.shape[1]
    sends = []

    def send(src, dst, s_sem, r_sem, **where):
        copy = pltpu.make_async_remote_copy(
            src_ref=src,
            dst_ref=dst,
            send_sem=s_sem,
            recv_sem=r_sem,
            device_id=where,
            device_id_type=MESH,
        )
        copy.start()
        sends.append(copy)
        return copy

    loads = [
        pltpu.make_async_copy(src, dst, w_sem.at[i])
        for i, (src, dst) in enumerate(
            (
                (q_hbm, q_ref),
                (kv_hbm.at[kv_local], kvbuf.at[kv_slot]),
                (list_hbm, list_ref),
                (len_hbm, len_ref),
                (wo_hbm, wo),
                (res_hbm, res_ref),
                (gain_hbm, gain_ref),
                (router_hbm, router_ref),
                (ids_hbm, ids_ref),
                (wg_hbm.at[0], wg),
                (wu_hbm.at[0], wu),
                (wd_hbm.at[0, pl.ds(x * hidden_part, hidden_part)], wd.at[x]),
            )
        )
    ]
    for load in loads:
        load.start()

    barrier = pltpu.get_barrier_semaphore()
    for dz in range(n_attn):
        for dx in range(n_sect):
            for dc in range(n_pair):
                if (dz == 0) != (dx + dc == 0):
                    pl.semaphore_signal(
                        barrier,
                        inc=1,
                        device_id={
                            "attn": lax.rem(z + dz, n_attn),
                            "sect": lax.rem(x + dx, n_sect),
                            "pair": lax.rem(c + dc, n_pair),
                        },
                        device_id_type=MESH,
                    )
    pl.semaphore_wait(barrier, n_attn + quarters - 2)

    def ahead(d):
        return lax.rem(z + d, n_attn)

    def behind(d):
        return lax.rem(z + (n_attn - d), n_attn)

    kv_copies = [
        send(
            kv_hbm.at[kv_local],
            kvbuf.at[kv_slot],
            kv_s.at[d - 1],
            kv_r.at[d - 1],
            attn=ahead(d),
        )
        for d in range(1, n_attn)
    ]
    wd_copies = []
    for dx in range(1, n_sect):
        to_x = lax.rem(x + dx, n_sect)
        wd_copies.append(
            send(
                wd_hbm.at[0, pl.ds(to_x * hidden_part, hidden_part)],
                wd.at[x],
                wd_s.at[dx - 1],
                wd_r.at[dx - 1],
                sect=to_x,
            )
        )
    for load in loads[:4]:
        load.wait()
    for copy in kv_copies:
        copy.wait_recv()

    listed = list_ref.shape[1]
    picked = [kvbuf[list_ref[0, j]] for j in range(listed)]
    cache = jnp.concatenate(picked, axis=0)
    keys = cache[:, :HEAD_DIM]
    values = cache[:, HEAD_DIM:]
    heads = jnp.concatenate(
        [q_ref[:, h * HEAD_DIM : (h + 1) * HEAD_DIM] for h in range(local_heads)], axis=0
    )
    scores = lax.dot_general(
        heads, keys, (((1,), (1,)), ((), ())), preferred_element_type=F32
    ) * (1.0 / math.sqrt(HEAD_DIM))
    place = lax.broadcasted_iota(jnp.int32, scores.shape, 1)
    scores = jnp.where(place < len_ref[0, 0], scores, -jnp.inf)
    lifted = jnp.exp(scores - jnp.max(scores, axis=-1, keepdims=True))
    row_total = jnp.sum(lifted, axis=-1, keepdims=True)
    mixed = jnp.dot(lifted.astype(BF16), values, preferred_element_type=F32) / row_total
    for h in range(local_heads):
        att[0, :, h * HEAD_DIM : (h + 1) * HEAD_DIM] = mixed[
            h * group_rows : (h + 1) * group_rows
        ].astype(BF16)
    att_copies = [None] + [
        send(att.at[0], att.at[d], att_s.at[d - 1], att_r.at[d - 1], attn=ahead(d))
        for d in range(1, n_attn)
    ]

    def plane(step):
        return lax.div(step, n_pair), lax.rem(step, n_pair)

    loads[4].wait()
    rs_copies = []
    mix_copies = []

    def project(d):
        if d:
            att_copies[d].wait_recv()
        value = jnp.dot(att[d], wo[...], preferred_element_type=F32)
        value = value.reshape(part_f32.shape[1:])
        part_f32[d] = value
        part[d] = value.astype(BF16)
        copies = []
        for j in range(1, quarters):
            to = lax.rem(quarter + j, quarters)
            to_x, to_c = plane(to)
            copies.append(
                send(
                    part.at[d, to],
                    rs_in.at[d, j - 1],
                    rs_s.at[d, j - 1],
                    rs_r.at[d, j - 1],
                    sect=to_x,
                    pair=to_c,
                )
            )
        rs_copies.append(copies)

    def pass_on(d):
        for copy in rs_copies[d]:
            copy.wait_recv()
        total = part_f32[d, quarter]
        for j in range(quarters - 1):
            total = total + rs_in[d, j].astype(F32)
        if d == 0:
            mix_f32[z] = total
        else:
            sum_out[d - 1] = total.astype(BF16)
            mix_copies.append(
                send(
                    sum_out.at[d - 1],
                    mix_in.at[z],
                    mix_s.at[d - 1],
                    mix_r.at[d - 1],
                    attn=behind(d),
                )
            )

    for d in range(n_attn + 1):
        if d < n_attn:
            project(d)
        if d:
            pass_on(d - 1)
    for d in range(1, n_attn):
        mix_copies[d - 1].wait_recv()
        mix_f32[ahead(d)] = mix_in[ahead(d)].astype(F32)

    for load in loads[5:9]:
        load.wait()

    span = width // n_attn
    mixed_f32 = res_ref[...].astype(F32) + jnp.concatenate(
        [mix_f32[a] for a in range(n_attn)], axis=1
    )
    mixed_f32 = mixed_f32.astype(BF16).astype(F32)
    normed = (
        mixed_f32
        * lax.rsqrt(jnp.mean(mixed_f32 * mixed_f32, axis=-1, keepdims=True) + 1e-06)
        * gain_ref[...]
    ).astype(BF16)
    logits = lax.dot_general(
        router_ref[...], normed, (((1,), (1,)), ((), ())), preferred_element_type=F32
    )
    lane = lax.broadcasted_iota(jnp.int32, logits.shape, 0)
    chosen = lane == ids_ref[0:1, :]
    for k in range(1, ids_ref.shape[0]):
        chosen = jnp.logical_or(chosen, lane == ids_ref[k : k + 1, :])
    logits = jnp.where(chosen, logits, -jnp.inf)
    raised = jnp.exp(logits - jnp.max(logits, axis=0, keepdims=True))
    route = raised / jnp.sum(raised, axis=0, keepdims=True)
    route = jnp.concatenate(
        [route, jnp.zeros((LANES - route.shape[0], own), F32)], axis=0
    )
    route = jnp.transpose(
        jnp.concatenate([route, jnp.zeros((LANES, LANES - own), F32)], axis=1)
    )[:own]
    rows[0, c, x, :, :width] = normed
    rows[0, c, x, :, width:] = route.astype(BF16)

    nz_copies = [None] + [
        send(
            rows.at[0, c, x],
            rows.at[d, c, x],
            nz_s.at[d - 1],
            nz_r.at[d - 1],
            attn=ahead(d),
        )
        for d in range(1, n_attn)
    ]
    nx_copies = [None] * n_attn
    nc_copies = [None] * n_attn
    for load in loads[9:]:
        load.wait()
    for copy in wd_copies:
        copy.wait_recv()

    def spread(d):
        if d:
            nz_copies[d].wait_recv()
        nx_copies[d] = [
            send(
                rows.at[d, c, x],
                rows.at[d, c, x],
                nx_s.at[d, dx - 1],
                nx_r.at[d, dx - 1],
                sect=lax.rem(x + dx, n_sect),
            )
            for dx in range(1, n_sect)
        ]

    def spread_on(d):
        for copy in nx_copies[d]:
            copy.wait_recv()
        nc_copies[d] = [
            send(
                rows.at[d, c],
                rows.at[d, c],
                nc_s.at[d, dc - 1],
                nc_r.at[d, dc - 1],
                pair=lax.rem(c + dc, n_pair),
            )
            for dc in range(1, n_pair)
        ]

    sect_copies = [None] * n_attn
    pair_copies = [None] * n_attn
    ret_copies = [None] * n_attn
    expert = z * n_pair + c

    def up(d):
        for copy in nc_copies[d]:
            copy.wait_recv()
        tokens = rows[d].reshape(quarters * own, rows.shape[-1])[:, :width]
        gate_val = jnp.dot(tokens, wg[...], preferred_element_type=F32)
        up_val = jnp.dot(tokens, wu[...], preferred_element_type=F32)
        hidden = (gate_val / (1.0 + jnp.exp(-gate_val)) * up_val).astype(BF16)
        value = jnp.concatenate(
            [jnp.dot(hidden, wd[i], preferred_element_type=F32) for i in range(n_sect)],
            axis=1,
        )
        weights = rows[d].reshape(quarters * own, rows.shape[-1])[:, width:].astype(F32)
        lanes = lax.broadcasted_iota(jnp.int32, weights.shape, 1)
        weight = jnp.sum(jnp.where(lanes == expert, weights, 0.0), axis=-1, keepdims=True)
        value = (value * weight).reshape(n_pair, n_sect, own, value.shape[-1])
        prod_f32[d] = value
        prod[d] = value.astype(BF16)
        pair_copies[d] = [
            send(
                prod.at[d, lax.rem(c + dc, n_pair)],
                pair_in.at[d, dc - 1],
                pair_s.at[d, dc - 1],
                pair_r.at[d, dc - 1],
                pair=lax.rem(c + dc, n_pair),
            )
            for dc in range(1, n_pair)
        ]

    def to_sect(d):
        for copy in pair_copies[d]:
            copy.wait_recv()
        total = prod_f32[d, c]
        for j in range(n_pair - 1):
            total = total + pair_in[d, j].astype(F32)
        sect_f32[d] = total
        sect[d] = total.astype(BF16)
        sect_copies[d] = [
            send(
                sect.at[d, lax.rem(x + dx, n_sect)],
                sect_in.at[d, dx - 1],
                sect_s.at[d, dx - 1],
                sect_r.at[d, dx - 1],
                sect=lax.rem(x + dx, n_sect),
            )
            for dx in range(1, n_sect)
        ]

    def give_back(d):
        for copy in sect_copies[d]:
            copy.wait_recv()
        total = sect_f32[d, x]
        for j in range(n_sect - 1):
            total = total + sect_in[d, j].astype(F32)
        if d == 0:
            return total
        ret_out[d - 1] = total.astype(BF16)
        ret_copies[d] = send(
            ret_out.at[d - 1],
            ret_in.at[d - 1],
            ret_s.at[d - 1],
            ret_r.at[d - 1],
            attn=behind(d),
        )

    spread(0)
    spread_on(0)
    up(0)
    turns = list(range(1, n_attn)) + [0]
    early = max(0, n_attn - 3)
    for d in range(1, n_attn):
        spread(d)
        if d >= 2:
            spread_on(d - 1)
            up(d - 1)
        if d >= 3:
            to_sect(d - 2)
    spread_on(n_attn - 1)
    up(n_attn - 1)
    for i in range(early - 1):
        give_back(turns[i])
    for i in range(early, n_attn):
        to_sect(turns[i])
        if i:
            give_back(turns[i - 1])
    joined = give_back(0)
    for d in range(1, n_attn):
        ret_copies[d].wait_recv()
        joined = joined + ret_in[d - 1].astype(F32)
    out_ref[...] = (mixed_f32 + joined).astype(BF16)
    for copy in sends:
        copy.wait_send()


def on_device(
    shape,
    queries,
    kv_pool,
    block_list,
    cache_len,
    out_weight,
    residual,
    norm_gain,
    router,
    expert_ids,
    w_gate,
    w_up,
    w_down,
):
    a, s, p = shape["attn"], shape["sect"], shape["pair"]
    q = s * p
    group_rows, head_cols = queries.shape
    own, width = residual.shape
    heads_rows, span = out_weight.shape
    hidden_part = w_gate.shape[2]
    out_cols = w_down.shape[2]
    key_rows, key_cols = kv_pool.shape[2:]
    wide = width + LANES
    buffers = [
        ((group_rows, head_cols), BF16),
        ((own, width), BF16),
        ((1, width), F32),
        (router.shape[::-1], BF16),
        (expert_ids.shape[::-1], jnp.int32),
        ((heads_rows, span), BF16),
        ((width, hidden_part), BF16),
        ((width, hidden_part), BF16),
        ((s, hidden_part, out_cols), BF16),
        ((a * kv_pool.shape[1], key_rows, key_cols), BF16),
        ((a, group_rows, head_cols), BF16),
        ((a, q, own, span), F32),
        ((a, q, own, span), BF16),
        ((a, q - 1, own, span), BF16),
        ((a - 1, own, span), BF16),
        ((a, own, span), BF16),
        ((a, own, span), F32),
        ((a, p, s, own, wide), BF16),
        ((a, p, s, own, width), F32),
        ((a, p, s, own, width), BF16),
        ((a, p - 1, s, own, width), BF16),
        ((a, s, own, width), F32),
        ((a, s, own, width), BF16),
        ((a, s - 1, own, width), BF16),
        ((a - 1, own, width), BF16),
        ((a - 1, own, width), BF16),
    ]
    held = sum(math.prod(dims) * jnp.dtype(kind).itemsize for dims, kind in buffers)
    fits = (
        2 * held <= VMEM_BYTES
        and span % LANES == 0
        and out_cols % LANES == 0
        and hidden_part % LANES == 0
        and w_gate.shape[0] == 1
        and router.shape[1] <= LANES
        and min(a, s, p) > 1
        and own % 16 == 0
        and own <= LANES
        and group_rows == q * own
        and hidden_part % 16 == 0
        and out_cols * s == width
    )
    if not fits:
        return by_collectives(
            queries,
            kv_pool,
            block_list,
            cache_len,
            out_weight,
            residual,
            norm_gain,
            router,
            expert_ids,
            w_gate,
            w_up,
            w_down,
        )
    sems = [
        (12,),
        (a - 1,),
        (a - 1,),
        (a - 1,),
        (a - 1,),
        (a, q - 1),
        (a, q - 1),
        (a - 1,),
        (a - 1,),
        (a - 1,),
        (a - 1,),
        (a, s - 1),
        (a, s - 1),
        (a, p - 1),
        (a, p - 1),
        (s - 1,),
        (s - 1,),
        (a, p - 1),
        (a, p - 1),
        (a, s - 1),
        (a, s - 1),
        (a - 1,),
        (a - 1,),
    ]
    vmem = pl.BlockSpec(memory_space=pltpu.VMEM)
    hbm = pl.BlockSpec(memory_space=pltpu.HBM)
    return pl.pallas_call(
        functools.partial(layer_kernel, (a, s, p)),
        out_shape=jax.ShapeDtypeStruct(residual.shape, BF16),
        in_specs=[hbm] * 12,
        out_specs=vmem,
        scratch_shapes=[pltpu.VMEM(dims, kind) for dims, kind in buffers]
        + [pltpu.SMEM(block_list.shape, jnp.int32), pltpu.SMEM((1, 1), jnp.int32)]
        + [pltpu.SemaphoreType.DMA(dims) for dims in sems],
        compiler_params=pltpu.CompilerParams(
            collective_id=0, has_side_effects=True, vmem_limit_bytes=VMEM_BYTES
        ),
    )(
        queries,
        kv_pool,
        block_list,
        cache_len.reshape(1, -1),
        residual,
        norm_gain.reshape(1, -1),
        router.T,
        expert_ids.T,
        out_weight,
        w_gate,
        w_up,
        w_down,
    )


def solution(mesh):
    placed = (
        P(("group", "attn"), ("sect", "pair")),
        P("sect", ("group", "attn"), None, None),
        P(("group", "attn"), None),
        P(("group", "attn")),
        P(("sect", "pair"), "attn"),
        P(("group", "attn", "sect", "pair"), None),
        P(),
        P(),
        P(("group", "attn", "sect", "pair"), None),
        P(("attn", "pair"), None, "sect"),
        P(("attn", "pair"), None, "sect"),
        P(("attn", "pair"), None, "sect"),
    )
    return jax.shard_map(
        functools.partial(on_device, dict(mesh.shape)),
        mesh=mesh,
        in_specs=placed,
        out_specs=P(("group", "attn", "sect", "pair"), None),
        check_vma=False,
    )
```
